32 devices in a mesh: gx: 8 (over y, x, core), gy: 4 (over z).
Axes of the slice: x: 2, y: 2, z: 4, core: 2. Of those that a mesh axis runs over, the one named last changes fastest.
Arguments:
- wave_fields: float32 [9, 32, 32, 1024], P(None, None, 'gy', 'gx'), may hold values from -6 to 6
- lame_lambda: float32 [32, 32, 1024], P(None, 'gy', 'gx'), may hold values from 0.5 to 1
- shear_modulus: float32 [32, 32, 1024], P(None, 'gy', 'gx'), may hold values from 0.3 to 0.7
- buoyancy: float32 [32, 32, 1024], P(None, 'gy', 'gx'), may hold values from 0.5 to 1
- ocean_state: float32 [3, 32, 1024], P(None, 'gy', 'gx'), may hold values from -6 to 6
- water_depth: float32 [32, 1024], P('gy', 'gx'), may hold values from 0.5 to 2
- seafloor_index: int32 [32, 1024], P('gy', 'gx'), may hold values from 0 to 15
- wet_mask: int32 [32, 1024], P('gy', 'gx'), may hold values 0 or 1
Outputs:
- wave_out: float32 [9, 32, 32, 1024], P(None, None, 'gy', 'gx')
- ocean_out: float32 [3, 32, 1024], P(None, 'gy', 'gx')
The draws below stay inside these ranges and needn't reach their ends.
All inputs are finite; a program needn't handle non-finite values. No bound on the sum of `wet_mask` on one device may be relied on, other than what follows from the above.
Results may differ from the reference program's by a relative error of at most 0.0001.
Values sent between devices are 32-bit elements; how exact they have to be, the bound alone decides.
No kernel may reach another device: no remote copies, remote signals or barrier semaphores. Data moves between devices by JAX's collectives and lax.ppermute only.
A program may use at most 64 MiB of HBM per device.

```python
import math
import jax
import jax.numpy as jnp

CZ = 32
STEPS = 2
NX = 1024
NY = 32


def with_ends(array, own_key, least, top_value):
    dims = array.shape
    place = [jax.random.randint(jax.random.fold_in(own_key, axis), (), 0, dims[axis]) for axis in range(len(dims))]
    array = array.at[tuple(place)].set(least)
    longest = dims.index(max(dims))
    place[longest] = (place[longest] + 1) % dims[longest]
    return array.at[tuple(place)].set(top_value)


def block_scale(stream_key, dims, shards, smallest, top_value):
    gain, own = 1.0, jax.random.fold_in(stream_key, 6)
    for axis_at, shards_of in shards:
        draws = jnp.exp(jax.random.uniform(jax.random.fold_in(own, axis_at), (shards_of,), jnp.float32, smallest / len(shards), top_value / len(shards)))
        gain = gain * jnp.repeat(draws, dims[axis_at] // shards_of).reshape([-1 if axis == axis_at else 1 for axis in range(len(dims))])
    return gain


def scatter_about(own_key, shape, scale, most, shards=(), kind=jnp.bfloat16):
    array = scale * jax.random.normal(own_key, shape, jnp.float32)
    if shards:
        array = array * block_scale(own_key, shape, shards, -0.22, 0.18)
    return jnp.clip(array, -most, most).astype(kind)


def setup_inputs(seed: int = 0) -> dict:
    streams_of = jax.random.split(jax.random.key(seed), 9)
    wave_fields = scatter_about(streams_of[0], (9, CZ, NY, NX), 1.0, 6.0, ((2, 4), (3, 8)), jnp.float32)
    lame_lambda = jnp.clip(0.5 + 0.5 * jax.random.uniform(streams_of[1], (CZ, NY, NX), jnp.float32) ** block_scale(streams_of[1], (CZ, NY, NX), ((1, 4), (2, 8)), -0.2, 0.2), 0.5, 1.0)
    shear_modulus = jnp.clip(0.3 + 0.39999998 * jax.random.uniform(streams_of[2], (CZ, NY, NX), jnp.float32) ** block_scale(streams_of[2], (CZ, NY, NX), ((1, 4), (2, 8)), -0.2, 0.2), 0.3, 0.7)
    buoyancy = jnp.clip(0.5 + 0.5 * jax.random.uniform(streams_of[3], (CZ, NY, NX), jnp.float32) ** block_scale(streams_of[3], (CZ, NY, NX), ((1, 4), (2, 8)), -0.2, 0.2), 0.5, 1.0)
    ocean_state = scatter_about(streams_of[4], (3, NY, NX), 1.0, 6.0, ((1, 4), (2, 8)), jnp.float32)
    water_depth = jnp.clip(jnp.exp(math.log(2.0) - 1.3862944 * jax.random.uniform(streams_of[5], (NY, NX), jnp.float32) ** block_scale(streams_of[5], (NY, NX), ((0, 4), (1, 8)), -0.2, 0.2)), 0.5, 2.0)
    seafloor_index = with_ends(jax.random.randint(streams_of[6], (NY, NX), 0, CZ // 2), jax.random.fold_in(streams_of[6], 1), 0, (CZ // 2) - 1).astype(jnp.int32)
    wet_mask = with_ends((jax.random.randint(streams_of[7], (NY, NX), 0, 4) < 3).astype(jnp.int32), jax.random.fold_in(streams_of[7], 1), 0, 1)
    return dict(wave_fields=wave_fields, lame_lambda=lame_lambda, shear_modulus=shear_modulus, buoyancy=buoyancy, ocean_state=ocean_state, water_depth=water_depth, seafloor_index=seafloor_index, wet_mask=wet_mask)


coef_near = 9.0 / 8.0
coef_far = -1.0 / 24.0
courant = 0.3
ocean_rate = 0.3
uplift = 0.5
loading = 0.5
viscous = 0.1


def differ(padded, direction, margins, forward):
    extent = padded.shape

    def sample(offset):
        selector = []
        for dimension in range(3):
            margin = margins[dimension]
            if dimension == direction:
                selector.append(slice(margin + offset, extent[dimension] - margin + offset))
            else:
                selector.append(slice(margin, extent[dimension] - margin))
        return padded[tuple(selector)]

    if forward:
        return coef_near * (sample(1) - sample(0)) + coef_far * (sample(2) - sample(-1))
    return coef_near * (sample(0) - sample(-1)) + coef_far * (sample(1) - sample(-2))


def advance_velocity(velocity, stress_pad, buoyancy, margins):
    stress_xx, stress_yy, stress_zz = stress_pad[0], stress_pad[1], stress_pad[2]
    stress_xy, stress_xz, stress_yz = stress_pad[3], stress_pad[4], stress_pad[5]
    accel_x = differ(stress_xx, 2, margins, True) + differ(stress_xy, 1, margins, False) + differ(stress_xz, 0, margins, False)
    accel_y = differ(stress_xy, 2, margins, False) + differ(stress_yy, 1, margins, True) + differ(stress_yz, 0, margins, False)
    accel_z = differ(stress_xz, 2, margins, False) + differ(stress_yz, 1, margins, False) + differ(stress_zz, 0, margins, True)
    return jnp.stack([velocity[0] + courant * buoyancy * accel_x,
                      velocity[1] + courant * buoyancy * accel_y,
                      velocity[2] + courant * buoyancy * accel_z])


def advance_stress(stress, velocity_pad, lame, shear, margins):
    speed_x, speed_y, speed_z = velocity_pad[0], velocity_pad[1], velocity_pad[2]
    strain_x = differ(speed_x, 2, margins, False)
    strain_y = differ(speed_y, 1, margins, False)
    strain_z = differ(speed_z, 0, margins, False)
    trace = strain_x + strain_y + strain_z
    shear_xy = differ(speed_x, 1, margins, True) + differ(speed_y, 2, margins, True)
    shear_xz = differ(speed_x, 0, margins, True) + differ(speed_z, 2, margins, True)
    shear_yz = differ(speed_y, 0, margins, True) + differ(speed_z, 1, margins, True)
    return jnp.stack([stress[0] + courant * (lame * trace + 2.0 * shear * strain_x),
                      stress[1] + courant * (lame * trace + 2.0 * shear * strain_y),
                      stress[2] + courant * (lame * trace + 2.0 * shear * strain_z),
                      stress[3] + courant * shear * shear_xy,
                      stress[4] + courant * shear * shear_xz,
                      stress[5] + courant * shear * shear_yz])


def ocean_level(level, flux_pad, vertical, onehot, wet):
    seafloor = jnp.sum(vertical * onehot, axis=0)
    east = flux_pad[0]
    north = flux_pad[1]
    spread = 0.5 * (east[1:-1, 2:] - east[1:-1, :-2]) + 0.5 * (north[2:, 1:-1] - north[:-2, 1:-1])
    return level + wet * (uplift * seafloor - ocean_rate * spread)


def ocean_flux(fluxes, flux_pad, level_pad, depth, wet):
    slope_x = 0.5 * (level_pad[1:-1, 2:] - level_pad[1:-1, :-2])
    slope_y = 0.5 * (level_pad[2:, 1:-1] - level_pad[:-2, 1:-1])
    laplace = flux_pad[:, 1:-1, 2:] + flux_pad[:, 1:-1, :-2] + flux_pad[:, 2:, 1:-1] + flux_pad[:, :-2, 1:-1] - 4.0 * fluxes
    east = wet * (fluxes[0] - ocean_rate * depth * slope_x + viscous * laplace[0])
    north = wet * (fluxes[1] - ocean_rate * depth * slope_y + viscous * laplace[1])
    return jnp.stack([east, north])


def reference(wave_fields, lame_lambda, shear_modulus, buoyancy, ocean_state, water_depth, seafloor_index, wet_mask):
    wet = wet_mask.astype(jnp.float32)
    layers = jnp.arange(wave_fields.shape[1], dtype=jnp.int32)
    onehot = (layers[:, None, None] == seafloor_index[None, :, :]).astype(jnp.float32)
    fields = wave_fields
    ocean = ocean_state
    for number in range(STEPS):
        velocity = fields[0:3]
        stress = fields[3:9]
        stress_pad = jnp.pad(stress, ((0, 0), (2, 2), (2, 2), (2, 2)))
        velocity = advance_velocity(velocity, stress_pad, buoyancy, (2, 2, 2))
        velocity_pad = jnp.pad(velocity, ((0, 0), (2, 2), (2, 2), (2, 2)))
        stress = advance_stress(stress, velocity_pad, lame_lambda, shear_modulus, (2, 2, 2))
        flux_pad = jnp.pad(ocean[1:3], ((0, 0), (1, 1), (1, 1)))
        level = ocean_level(ocean[0], flux_pad, velocity[2], onehot, wet)
        level_pad = jnp.pad(level, ((1, 1), (1, 1)))
        fluxes = ocean_flux(ocean[1:3], flux_pad, level_pad, water_depth, wet)
        pressed = stress[2] - loading * onehot * (wet * level)[None, :, :]
        stress = jnp.concatenate([stress[0:2], pressed[None], stress[3:6]], axis=0)
        fields = jnp.concatenate([velocity, stress], axis=0)
        ocean = jnp.concatenate([level[None], fluxes], axis=0)
    return fields, ocean
```

```python
import jax
import jax.numpy as jnp
from jax import lax
from jax.experimental import pallas as pl
from jax.experimental.pallas import tpu as pltpu
from jax.sharding import PartitionSpec as P

RATE = 0.3 / 24.0
OCEAN_RATE = 0.3
UPLIFT = 0.5
LOADING = 0.5
VISCOUS = 0.1

ROWS = 8
LANES = 128
EDGE = 8
GROUP = 2 * EDGE
PACK = LANES // GROUP

LEVEL, FLUX_X, FLUX_Y, DEPTH, FLOOR, WET = range(6)
LAME, SHEAR, BUOY = 9, 10, 11
FIELDS = 12


def rolled(x, shift, axis):
    shift %= x.shape[axis]
    return x if shift == 0 else pltpu.roll(x, shift, axis)


def iotas():
    sub = lax.broadcasted_iota(jnp.int32, (ROWS, LANES), 0)
    lane = lax.broadcasted_iota(jnp.int32, (ROWS, LANES), 1)
    return sub, lane


def plane(ref, index):
    return ref[index * ROWS : (index + 1) * ROWS, :]


def row(ref, index):
    return ref[index : index + 1, :]


def store(ref, index, value):
    ref[index * ROWS : (index + 1) * ROWS, :] = value


def near_far(a, b, c, d):
    return 27.0 * (a - b) - (c - d)


class Grid:
    def __init__(self, depth):
        self.depth = depth
        self.per = depth // PACK
        self.planes = depth + 2 * self.per
        self.sub, self.lane = iotas()
        self.inner = self.lane % GROUP
        self.first = self.inner < EDGE
        self.group = self.lane // GROUP
        self.zero = jnp.zeros((ROWS, LANES), jnp.float32)

    def beside(self, field, which):
        left = field(self.depth + which)
        right = field(self.depth + self.per + which)
        return jnp.where(self.first, left, right)

    def besides(self, field):
        return [self.beside(field, which) for which in range(self.per)]

    def edge_of(self, besides, p):
        if p >= self.depth:
            return None
        return rolled(besides[p % self.per], LANES - EDGE - GROUP * (p // self.per), 1)

    def along(self, x, offset, edge):
        if edge is not None:
            lane = self.lane
            keep = {-1: lane == LANES - 1, -2: lane >= LANES - 2, 1: lane == 0, 2: lane <= 1}[offset]
            x = jnp.where(keep, edge, x)
        return rolled(x, -offset, 1)

    def across(self, x, offset, low=None, high=None):
        sub = self.sub
        out = rolled(x, -offset, 0)
        none = self.zero
        low = low or (none, none)
        high = high or (none, none)
        if offset == -1:
            return jnp.where(sub == 0, low[0], out)
        if offset == -2:
            return jnp.where(sub == 0, low[1], jnp.where(sub == 1, low[0], out))
        if offset == 1:
            return jnp.where(sub == ROWS - 1, high[0], out)
        return jnp.where(sub == ROWS - 1, high[1], jnp.where(sub == ROWS - 2, high[0], out))

    def down(self, field, p, offset):
        depth, per = self.depth, self.per
        if p < depth:
            q = p + offset
            return field(q) if 0 <= q < depth else self.zero
        side, which = divmod(p - depth, per)
        base = depth + side * per
        at = which + offset
        if 0 <= at < per:
            return field(base + at)
        if at >= per:
            x = rolled(field(base + at - per), -GROUP, 1)
            return jnp.where(self.lane < LANES - GROUP, x, 0.0)
        x = rolled(field(base + at + per), GROUP, 1)
        return jnp.where(self.lane >= GROUP, x, 0.0)

    def fx(self, x, edge):
        return near_far(self.along(x, 1, edge), x, self.along(x, 2, edge), self.along(x, -1, edge))

    def bx(self, x, edge):
        return near_far(x, self.along(x, -1, edge), self.along(x, 1, edge), self.along(x, -2, edge))

    def fy(self, x, low=None, high=None):
        return near_far(
            self.across(x, 1, low, high), x, self.across(x, 2, low, high), self.across(x, -1, low, high)
        )

    def by(self, x, low=None, high=None):
        return near_far(
            x, self.across(x, -1, low, high), self.across(x, 1, low, high), self.across(x, -2, low, high)
        )

    def fz(self, field, p):
        return near_far(
            self.down(field, p, 1), field(p), self.down(field, p, 2), self.down(field, p, -1)
        )

    def bz(self, field, p):
        return near_far(
            field(p), self.down(field, p, -1), self.down(field, p, 1), self.down(field, p, -2)
        )

    def every_group(self, x):
        shift = GROUP
        while shift < LANES:
            x = x + rolled(x, shift, 1)
            shift *= 2
        return x


def edges_kernel(depth, wave, lame, shear, buoy, ocean, deep, floor, wet, own, own_ocean, to_right, to_left):
    grid = Grid(depth)
    per = grid.per
    masks = [grid.group == g for g in range(PACK)]

    def collect(at):
        out = grid.zero
        for g in range(PACK):
            out = jnp.where(masks[g], rolled(at(g), EDGE + GROUP * g, 1), out)
        return out

    def both(index, one, two):
        store(to_right, index, jnp.where(grid.first, one, rolled(two, EDGE, 1)))
        store(to_left, index, jnp.where(grid.first, rolled(two, -EDGE, 1), one))

    sources = [(wave, f * depth) for f in range(9)] + [(lame, 0), (shear, 0), (buoy, 0)]
    for f in range(0, FIELDS, 2):
        for j in range(per):
            pair = []
            for h in (f, f + 1):
                ref, base = sources[h]
                pair.append(collect(lambda g: plane(ref, base + per * g + j)))
                store(own, h * per + j, pair[-1])
            both((f // 2) * per + j, *pair)
    flat = [plane(ocean, k) for k in range(3)] + [deep[...]]
    flat += [floor[...].astype(jnp.float32), wet[...].astype(jnp.float32)]
    for f in range(0, 6, 2):
        pair = []
        for h in (f, f + 1):
            pair.append(collect(lambda g: flat[h]))
            store(own_ocean, h, pair[-1])
        both((FIELDS // 2) * per + f // 2, *pair)


def partial_velocity(grid, stress, speed, buoy, out):
    sxx, syy, szz, sxy, sxz, syz = stress
    b_xx, b_xy, b_xz = grid.besides(sxx), grid.besides(sxy), grid.besides(sxz)
    for p in list(range(grid.depth, grid.planes)) + list(range(grid.depth)):
        rate = RATE * buoy(p)
        xy, yz, xz = sxy(p), syz(p), sxz(p)
        e_xy, e_xz = grid.edge_of(b_xy, p), grid.edge_of(b_xz, p)
        ax = grid.fx(sxx(p), grid.edge_of(b_xx, p)) + grid.by(xy) + grid.bz(sxz, p)
        store(out, p, speed[0](p) + rate * ax)
        ay = grid.bx(xy, e_xy) + grid.fy(syy(p)) + grid.bz(syz, p)
        store(out, grid.planes + p, speed[1](p) + rate * ay)
        az = grid.bx(xz, e_xz) + grid.by(yz) + grid.fz(szz, p)
        store(out, 2 * grid.planes + p, speed[2](p) + rate * az)


def partial_level(grid, flat, out):
    for k in range(3):
        x, y, wet = flat(FLUX_X, k), flat(FLUX_Y, k), flat(WET, k)
        edge = ocean_edge(grid, lambda q: flat(FLUX_X, q), k)
        spread = 0.5 * (grid.along(x, 1, edge) - grid.along(x, -1, edge))
        spread = spread + 0.5 * (grid.across(y, 1) - grid.across(y, -1))
        store(out, k, flat(LEVEL, k) - OCEAN_RATE * (wet * spread))


def ocean_edge(grid, at, k):
    if k:
        return None
    return rolled(jnp.where(grid.first, at(1), at(2)), LANES - EDGE, 1)


TO_HIGH = ((0, 7), (1, 6), (1, 7), (2, 7), (6, 6), (6, 7), (4, 7), (8, 6), (8, 7))
TO_LOW = ((0, 0), (0, 1), (1, 0), (2, 0), (2, 1), (6, 0), (4, 0), (4, 1), (8, 0))


def send_rows(grid, rows, take, level, flat, edge, out):
    at = 0
    for field, which in rows:
        for piece in take(field, which):
            out[at : at + piece.shape[0], :] = piece
            at += piece.shape[0]
    for which in (None, WET, FLOOR, FLUX_X, FLUX_Y):
        for k in range(3):
            source = level if which is None else flat[which]
            base = k * ROWS if which is None else flat[which, "at"] + k * ROWS
            out[at : at + 1, :] = row(source, base + edge)
            at += 1
    out[at : at + 1, :] = jnp.zeros((1, LANES), jnp.float32)


def start_kernel(
    depth, wave, buoy, own, own_ocean, ocean, deep, floor, wet, left, right,
    windows, flat, partial, level, high, low,
):
    grid = Grid(depth)
    per, planes = grid.per, grid.planes
    for f in range(FIELDS):
        for j in range(per):
            mine = plane(own, f * per + j)
            a = plane(left, (f // 2) * per + j)
            b = plane(right, (f // 2) * per + j)
            if f % 2:
                a, b = rolled(a, -EDGE, 1), rolled(b, EDGE, 1)
            store(windows, f * 2 * per + j, jnp.where(grid.first, a, mine))
            store(windows, f * 2 * per + per + j, jnp.where(grid.first, mine, b))
    whole = [plane(ocean, k) for k in range(3)] + [deep[...]]
    whole += [floor[...].astype(jnp.float32), wet[...].astype(jnp.float32)]
    for f in range(6):
        mine = plane(own_ocean, f)
        a = plane(left, (FIELDS // 2) * per + f // 2)
        b = plane(right, (FIELDS // 2) * per + f // 2)
        if f % 2:
            a, b = rolled(a, -EDGE, 1), rolled(b, EDGE, 1)
        store(flat, 3 * f, whole[f])
        store(flat, 3 * f + 1, jnp.where(grid.first, a, mine))
        store(flat, 3 * f + 2, jnp.where(grid.first, mine, b))

    def field(f):
        ref, base = (buoy, 0) if f == BUOY else (wave, f * depth)
        return lambda p: plane(ref, base + p) if p < depth else plane(windows, f * 2 * per + p - depth)

    partial_velocity(grid, [field(3 + f) for f in range(6)], [field(f) for f in range(3)], field(BUOY), partial)
    partial_level(grid, lambda f, k: plane(flat, 3 * f + k), level)

    def take(f, which):
        if f < 3:
            return [partial[pl.ds(f * planes * ROWS + which, planes, stride=ROWS), :]]
        ref, base = (buoy, 0) if f == BUOY else (wave, f * depth)
        return [
            ref[pl.ds(base * ROWS + which, depth, stride=ROWS), :],
            windows[pl.ds(f * 2 * per * ROWS + which, 2 * per, stride=ROWS), :],
        ]

    flats = {}
    for which in (WET, FLOOR, FLUX_X, FLUX_Y):
        flats[which] = flat
        flats[which, "at"] = 3 * which * ROWS
    send_rows(grid, TO_HIGH + ((BUOY, 6), (BUOY, 7)), take, level, flats, 7, high)
    send_rows(grid, TO_LOW + ((BUOY, 0), (BUOY, 1)), take, level, flats, 0, low)


def finish(grid, stress_rows, buoy, partial, level, now, fixed, low, high, low_buoy, high_buoy, halo, corr, speed, new):
    depth, per, planes = grid.depth, grid.per, grid.planes

    def piece(ref, index, part):
        start, size = part
        return ref[index * planes + start : index * planes + start + size, :]

    for part in ((0, depth), (depth, 2 * per)):
        start, size = part
        lo = lambda index: piece(low, index, part)
        hi = lambda index: piece(high, index, part)
        own = lambda f, which: stress_rows(f, which, part)

        def put(ref, index, value):
            ref[index * planes + start : index * planes + start + size, :] = value

        b1 = RATE * piece(low_buoy, 10, part)
        b2 = RATE * piece(low_buoy, 9, part)
        b8 = RATE * piece(high_buoy, 9, part)
        b9 = RATE * piece(high_buoy, 10, part)
        xy0, xy6, xy7 = own(6, 0), own(6, 6), own(6, 7)
        yz0, yz6, yz7 = own(8, 0), own(8, 6), own(8, 7)
        yy0, yy1, yy7 = own(4, 0), own(4, 1), own(4, 7)
        put(halo, 0, lo(0) - b1 * xy0)
        put(halo, 1, hi(0) + b8 * (xy6 - 27.0 * xy7))
        put(halo, 2, hi(1) + b9 * xy7)
        put(halo, 3, lo(2) + b1 * (27.0 * yy0 - yy1))
        put(halo, 4, lo(1) - b2 * yy0)
        put(halo, 5, hi(2) + b8 * yy7)
        put(halo, 6, lo(3) - b1 * yz0)
        put(halo, 7, hi(3) + b8 * (yz6 - 27.0 * yz7))
        put(halo, 8, hi(4) + b9 * yz7)
        put(corr, 0, lo(4) - 27.0 * lo(5))
        put(corr, 1, lo(5))
        put(corr, 2, -hi(5))
        put(corr, 3, lo(6))
        put(corr, 4, -hi(6))
        put(corr, 5, 27.0 * hi(6) - hi(7))
        put(corr, 6, lo(7) - 27.0 * lo(8))
        put(corr, 7, lo(8))
        put(corr, 8, -hi(8))

    sub = grid.sub
    floor = [fixed(FLOOR, k) for k in range(3)]
    sums = [grid.zero] * 3
    depths = grid.group.astype(jnp.float32) * per
    for p in range(planes):
        rate = RATE * buoy(p)
        c = [row(corr, index * planes + p) for index in range(9)]
        pick = lambda at, r0, r1, r2: jnp.where(
            sub == at[0], r0, jnp.where(sub == at[1], r1, jnp.where(sub == at[2], r2, 0.0))
        )
        store(speed, p, plane(partial, p) + rate * pick((0, 1, 7), c[0], c[1], c[2]))
        store(speed, planes + p, plane(partial, planes + p) + rate * pick((0, 6, 7), c[3], c[4], c[5]))
        vz = plane(partial, 2 * planes + p) + rate * pick((0, 1, 7), c[6], c[7], c[8])
        store(speed, 2 * planes + p, vz)
        if p < depth:
            k, at = 0, float(p)
        else:
            side, which = divmod(p - depth, per)
            k, at = 1 + side, depths + float(which)
        sums[k] = jnp.where(floor[k] == at, vz, sums[k])
    sums[1] = grid.every_group(sums[1])
    sums[2] = grid.every_group(sums[2])

    tail = low.shape[0] - 16
    tail_high = high.shape[0] - 16
    ends = []
    for message, base, index, own_row, sign in ((low, tail, 6, 0, -1.0), (high, tail_high, 7, 7, 1.0)):
        lines = lambda which, k, message=message, base=base: row(message, base + 3 * which + k)
        zs = lax.broadcasted_iota(jnp.int32, (depth, LANES), 0).astype(jnp.float32)
        main = halo[index * planes : index * planes + depth, :]
        floors = [jnp.sum(jnp.where(lines(2, 0) == zs, main, 0.0), axis=0, keepdims=True)]
        side = halo[index * planes + depth : (index + 1) * planes, :]
        half = lax.broadcasted_iota(jnp.int32, (2 * per, LANES), 0)
        group = (lax.broadcasted_iota(jnp.int32, (2 * per, LANES), 1) // GROUP) * per
        where = jnp.where(half < per, lines(2, 1), lines(2, 2))
        side = jnp.where(where == (group + half % per).astype(jnp.float32), side, 0.0)
        side = grid.every_group(side)
        floors.append(jnp.sum(jnp.where(half < per, side, 0.0), axis=0, keepdims=True))
        floors.append(jnp.sum(jnp.where(half < per, 0.0, side), axis=0, keepdims=True))
        end = []
        for k in range(3):
            mine = now(FLUX_Y, k)[own_row : own_row + 1, :]
            wet = lines(1, k)
            end.append(lines(0, k) + wet * (UPLIFT * floors[k] + (sign * 0.5 * OCEAN_RATE) * mine))
        ends.append((end, lines))
    (low_level, low_line), (high_level, high_line) = ends

    levels = []
    for k in range(3):
        wet = fixed(WET, k)
        beside = jnp.where(sub == 0, low_line(4, k), jnp.where(sub == ROWS - 1, -high_line(4, k), 0.0))
        levels.append(
            plane(level, k) + wet * (UPLIFT * sums[k] + (0.5 * OCEAN_RATE) * beside)
        )
        new(LEVEL, k, levels[k])
    for k in range(3):
        wet, deep = fixed(WET, k), fixed(DEPTH, k)
        edge = ocean_edge(grid, lambda q: levels[q], k)
        slope_x = 0.5 * (grid.along(levels[k], 1, edge) - grid.along(levels[k], -1, edge))
        lo, hi = (low_level[k],), (high_level[k],)
        slope_y = 0.5 * (grid.across(levels[k], 1, lo, hi) - grid.across(levels[k], -1, lo, hi))
        for which, line, slope in ((FLUX_X, 3, slope_x), (FLUX_Y, 4, slope_y)):
            x = now(which, k)
            edge = ocean_edge(grid, lambda q: now(which, q), k)
            lo, hi = (low_line(line, k),), (high_line(line, k),)
            laplace = grid.along(x, 1, edge) + grid.along(x, -1, edge)
            laplace = laplace + grid.across(x, 1, lo, hi) + grid.across(x, -1, lo, hi) - 4.0 * x
            new(which, k, wet * (x - OCEAN_RATE * deep * slope + VISCOUS * laplace))
    return levels


def new_stress(grid, todo, stress, lame, shear, speed, halo, levels, fixed, out):
    depth, per, planes = grid.depth, grid.per, grid.planes
    vx, vy, vz = [lambda p, f=f: plane(speed, f * planes + p) for f in range(3)]
    b_x, b_y, b_z = grid.besides(vx), grid.besides(vy), grid.besides(vz)
    press = [LOADING * fixed(WET, k) * levels[k] for k in range(3)]
    floor = [fixed(FLOOR, k) for k in range(3)]
    depths = grid.group.astype(jnp.float32) * per
    for p in todo:
        h = [row(halo, index * planes + p) for index in range(9)]
        x, y, z = vx(p), vy(p), vz(p)
        e_x, e_y, e_z = [grid.edge_of(b, p) for b in (b_x, b_y, b_z)]
        strain_x = grid.bx(x, e_x)
        strain_y = grid.by(y, (h[3], h[4]), (h[5], h[5]))
        strain_z = grid.bz(vz, p)
        mu = RATE * shear(p)
        spread = (RATE * lame(p)) * (strain_x + strain_y + strain_z)
        two = mu + mu
        if p < depth:
            k, at = 0, float(p)
        else:
            side, which = divmod(p - depth, per)
            k, at = 1 + side, depths + float(which)
        out(0, p, stress[0](p) + (spread + two * strain_x))
        out(1, p, stress[1](p) + (spread + two * strain_y))
        out(2, p, stress[2](p) + (spread + two * strain_z) - jnp.where(floor[k] == at, press[k], 0.0))
        xy = grid.fy(x, (h[0], h[0]), (h[1], h[2])) + grid.fx(y, e_y)
        out(3, p, stress[3](p) + mu * xy)
        xz = grid.fz(vx, p) + grid.fx(z, e_z)
        out(4, p, stress[4](p) + mu * xz)
        yz = grid.fz(vy, p) + grid.fy(z, (h[6], h[6]), (h[7], h[8]))
        out(5, p, stress[5](p) + mu * yz)


def middle_kernel(
    depth, wave, lame, shear, buoy, windows, flat, partial, level, from_low, from_high,
    stress_out, ocean_out, partial_out, level_out, high, low,
    halo, corr, speed,
):
    grid = Grid(depth)
    per, planes = grid.per, grid.planes

    def field(f):
        refs = {LAME: lame, SHEAR: shear, BUOY: buoy}
        ref, base = (refs[f], 0) if f in refs else (wave, f * depth)
        return lambda p: plane(ref, base + p) if p < depth else plane(windows, f * 2 * per + p - depth)

    def stress_rows(f, which, part):
        if part[0] == 0:
            return wave[pl.ds(f * depth * ROWS + which, depth, stride=ROWS), :]
        return windows[pl.ds(f * 2 * per * ROWS + which, 2 * per, stride=ROWS), :]

    flats = lambda f, k: plane(flat, 3 * f + k)
    levels = finish(
        grid, stress_rows, field(BUOY), partial, level, flats, flats, from_low, from_high, from_low, from_high,
        halo, corr, speed, lambda which, k, value: store(ocean_out, 3 * which + k, value),
    )
    order = list(range(depth, planes)) + list(range(depth))
    new_stress(
        grid, order, [field(3 + f) for f in range(6)], field(LAME), field(SHEAR), speed, halo, levels, flats,
        lambda f, p, value: store(stress_out, f * planes + p, value),
    )
    stress = [lambda p, f=f: plane(stress_out, f * planes + p) for f in range(6)]
    speeds = [lambda p, f=f: plane(speed, f * planes + p) for f in range(3)]
    partial_velocity(grid, stress, speeds, field(BUOY), partial_out)
    both = lambda f, k: plane(flat if f >= DEPTH else ocean_out, 3 * f + k)
    partial_level(grid, both, level_out)

    def take(f, which):
        ref, f = (partial_out, f) if f < 3 else (stress_out, f - 3)
        return [ref[pl.ds(f * planes * ROWS + which, planes, stride=ROWS), :]]

    rows_of = {}
    for which in (WET, FLOOR, FLUX_X, FLUX_Y):
        rows_of[which] = flat if which >= DEPTH else ocean_out
        rows_of[which, "at"] = 3 * which * ROWS
    send_rows(grid, TO_HIGH, take, level_out, rows_of, 7, high)
    send_rows(grid, TO_LOW, take, level_out, rows_of, 0, low)


def last_kernel(
    depth, lame, shear, buoy, windows, flat, stress_in, ocean, partial, level, low_buoy, high_buoy, from_low, from_high,
    wave_out, ocean_out,
    halo, corr, speed,
):
    grid = Grid(depth)
    per, planes = grid.per, grid.planes

    def field(f):
        ref = {LAME: lame, SHEAR: shear, BUOY: buoy}[f]
        return lambda p: plane(ref, p) if p < depth else plane(windows, f * 2 * per + p - depth)

    def stress_rows(f, which, part):
        start, size = part
        return stress_in[pl.ds(((f - 3) * planes + start) * ROWS + which, size, stride=ROWS), :]

    def new(which, k, value):
        if k == 0:
            store(ocean_out, which, value)

    fixed = lambda f, k: plane(flat, 3 * f + k)
    now = lambda f, k: plane(ocean, 3 * f + k)
    levels = finish(
        grid, stress_rows, field(BUOY), partial, level, now, fixed, from_low, from_high, low_buoy, high_buoy,
        halo, corr, speed, new,
    )
    stress = [lambda p, f=f: plane(stress_in, f * planes + p) for f in range(6)]
    new_stress(
        grid, list(range(depth)), stress, field(LAME), field(SHEAR), speed, halo, levels, fixed,
        lambda f, p, value: store(wave_out, (3 + f) * depth + p, value),
    )
    for f in range(3):
        for p in range(depth):
            store(wave_out, f * depth + p, plane(speed, f * planes + p))


def call(kernel, shapes, scratch, *arguments):
    vmem = pl.BlockSpec(memory_space=pltpu.VMEM)
    return pl.pallas_call(
        kernel,
        out_shape=[jax.ShapeDtypeStruct((n, LANES), jnp.float32) for n in shapes],
        in_specs=[vmem] * len(arguments),
        out_specs=[vmem] * len(shapes),
        scratch_shapes=[pltpu.VMEM((n, LANES), jnp.float32) for n in scratch],
        compiler_params=pltpu.CompilerParams(vmem_limit_bytes=24 * 1024 * 1024),
    )(*arguments)


def exchange(axis, forth, back):
    count = lax.axis_size(axis)
    forward = [(i, i + 1) for i in range(count - 1)]
    backward = [(i + 1, i) for i in range(count - 1)]
    return lax.ppermute(forth, axis, forward), lax.ppermute(back, axis, backward)


def local(wave_fields, lame_lambda, shear_modulus, buoyancy, ocean_state, water_depth, seafloor_index, wet_mask):
    depth = wave_fields.shape[1]
    per = depth // PACK
    planes = depth + 2 * per
    wave = wave_fields.reshape(-1, LANES)
    lame = lame_lambda.reshape(-1, LANES)
    shear = shear_modulus.reshape(-1, LANES)
    buoy = buoyancy.reshape(-1, LANES)
    ocean = ocean_state.reshape(-1, LANES)

    def bind(kernel):
        return lambda *refs: kernel(depth, *refs)

    edge = (FIELDS // 2 * per + 3) * ROWS
    own, own_ocean, to_right, to_left = call(
        bind(edges_kernel), [FIELDS * per * ROWS, 6 * ROWS, edge, edge], [],
        wave, lame, shear, buoy, ocean, water_depth, seafloor_index, wet_mask,
    )
    left, right = exchange("gx", to_right, to_left)
    first = 11 * planes + 16
    later = 9 * planes + 16
    windows, flat, partial, level, high, low = call(
        bind(start_kernel),
        [FIELDS * 2 * per * ROWS, 18 * ROWS, 3 * planes * ROWS, 3 * ROWS, first, first], [],
        wave, buoy, own, own_ocean, ocean, water_depth, seafloor_index, wet_mask, left, right,
    )
    low1, high1 = exchange("gy", high, low)
    scratch = [9 * planes, 9 * planes, 3 * planes * ROWS]
    stress, ocean1, partial, level, high, low = call(
        bind(middle_kernel),
        [6 * planes * ROWS, 9 * ROWS, 3 * planes * ROWS, 3 * ROWS, later, later], scratch,
        wave, lame, shear, buoy, windows, flat, partial, level, low1, high1,
    )
    low2, high2 = exchange("gy", high, low)
    wave_out, ocean_out = call(
        bind(last_kernel), [wave.shape[0], ocean.shape[0]], scratch,
        lame, shear, buoy, windows, flat, stress, ocean1, partial, level, low1, high1, low2, high2,
    )
    return wave_out.reshape(wave_fields.shape), ocean_out.reshape(ocean_state.shape)


def solution(mesh):
    in_specs = (
        P(None, None, "gy", "gx"),
        P(None, "gy", "gx"),
        P(None, "gy", "gx"),
        P(None, "gy", "gx"),
        P(None, "gy", "gx"),
        P("gy", "gx"),
        P("gy", "gx"),
        P("gy", "gx"),
    )
    out_specs = (P(None, None, "gy", "gx"), P(None, "gy", "gx"))
    return jax.shard_map(local, mesh=mesh, in_specs=in_specs, out_specs=out_specs, check_vma=False)
```

```python
import jax
import jax.numpy as jnp
from jax import lax
from jax.experimental import pallas as pl
from jax.experimental.pallas import tpu as pltpu
from jax.sharding import PartitionSpec as P

RATE = 0.3 / 24.0
OCEAN_RATE = 0.3
UPLIFT = 0.5
LOADING = 0.5
VISCOUS = 0.1

ROWS = 8
LANES = 128
EDGE = 8
GROUP = 2 * EDGE
PACK = LANES // GROUP

LEVEL, FLUX_X, FLUX_Y, DEPTH, FLOOR, WET = range(6)
LAME, SHEAR, BUOY = 9, 10, 11
FIELDS = 12


def rolled(x, shift, axis):
    shift %= x.shape[axis]
    return x if shift == 0 else pltpu.roll(x, shift, axis)


def iotas():
    sub = lax.broadcasted_iota(jnp.int32, (ROWS, LANES), 0)
    lane = lax.broadcasted_iota(jnp.int32, (ROWS, LANES), 1)
    return sub, lane


def either(which, take):
    if not isinstance(which, tuple):
        return take(which)
    return jnp.where(which[0], take(which[1]), take(which[2]))


def plane(ref, index):
    if isinstance(ref, tuple):
        return either(ref, lambda one: plane(one, index))
    return ref[index * ROWS : (index + 1) * ROWS, :]


def row(ref, index):
    if isinstance(ref, tuple):
        return either(ref, lambda one: row(one, index))
    return ref[index : index + 1, :]


def store(ref, index, value):
    ref[index * ROWS : (index + 1) * ROWS, :] = value


def near_far(a, b, c, d):
    return 27.0 * (a - b) - (c - d)


class Grid:
    def __init__(self, depth):
        self.depth = depth
        self.per = depth // PACK
        self.planes = depth + 2 * self.per
        self.sub, self.lane = iotas()
        self.inner = self.lane % GROUP
        self.first = self.inner < EDGE
        self.group = self.lane // GROUP
        self.zero = jnp.zeros((ROWS, LANES), jnp.float32)

    def beside(self, field, which):
        left = field(self.depth + which)
        right = field(self.depth + self.per + which)
        return jnp.where(self.first, left, right)

    def besides(self, field):
        return [self.beside(field, which) for which in range(self.per)]

    def edge_of(self, besides, p):
        if p >= self.depth:
            return None
        return rolled(besides[p % self.per], LANES - EDGE - GROUP * (p // self.per), 1)

    def along(self, x, offset, edge):
        if edge is not None:
            lane = self.lane
            keep = {-1: lane == LANES - 1, -2: lane >= LANES - 2, 1: lane == 0, 2: lane <= 1}[offset]
            x = jnp.where(keep, edge, x)
        return rolled(x, -offset, 1)

    def across(self, x, offset, low=None, high=None):
        sub = self.sub
        out = rolled(x, -offset, 0)
        none = self.zero
        low = low or (none, none)
        high = high or (none, none)
        if offset == -1:
            return jnp.where(sub == 0, low[0], out)
        if offset == -2:
            return jnp.where(sub == 0, low[1], jnp.where(sub == 1, low[0], out))
        if offset == 1:
            return jnp.where(sub == ROWS - 1, high[0], out)
        return jnp.where(sub == ROWS - 1, high[1], jnp.where(sub == ROWS - 2, high[0], out))

    def down(self, field, p, offset):
        depth, per = self.depth, self.per
        if p < depth:
            q = p + offset
            return field(q) if 0 <= q < depth else self.zero
        side, which = divmod(p - depth, per)
        base = depth + side * per
        at = which + offset
        if 0 <= at < per:
            return field(base + at)
        if at >= per:
            x = rolled(field(base + at - per), -GROUP, 1)
            return jnp.where(self.lane < LANES - GROUP, x, 0.0)
        x = rolled(field(base + at + per), GROUP, 1)
        return jnp.where(self.lane >= GROUP, x, 0.0)

    def fx(self, x, edge):
        return near_far(self.along(x, 1, edge), x, self.along(x, 2, edge), self.along(x, -1, edge))

    def bx(self, x, edge):
        return near_far(x, self.along(x, -1, edge), self.along(x, 1, edge), self.along(x, -2, edge))

    def fy(self, x, low=None, high=None):
        return near_far(
            self.across(x, 1, low, high), x, self.across(x, 2, low, high), self.across(x, -1, low, high)
        )

    def by(self, x, low=None, high=None):
        return near_far(
            x, self.across(x, -1, low, high), self.across(x, 1, low, high), self.across(x, -2, low, high)
        )

    def fz(self, field, p):
        return near_far(
            self.down(field, p, 1), field(p), self.down(field, p, 2), self.down(field, p, -1)
        )

    def bz(self, field, p):
        return near_far(
            field(p), self.down(field, p, -1), self.down(field, p, 1), self.down(field, p, -2)
        )

    def every_group(self, x):
        shift = GROUP
        while shift < LANES:
            x = x + rolled(x, shift, 1)
            shift *= 2
        return x


def edges_kernel(
    depth, odd_ref, *refs,
):
    hbm, vmem, (own, own_ocean, even_way, odd_way), sem = refs[:8], refs[8:16], refs[16:20], refs[20]
    copies = [
        pltpu.make_async_copy(source, target, sem.at[k]) for k, (source, target) in enumerate(zip(hbm[1:], vmem[1:]))
    ]
    size = depth * ROWS
    waves = [
        pltpu.make_async_copy(
            hbm[0].at[f * size : (f + 1) * size, :], vmem[0].at[f * size : (f + 1) * size, :], sem.at[7 + f]
        )
        for f in range(9)
    ]
    for copy in waves + copies:
        copy.start()
    wave, lame, shear, buoy, ocean, deep, floor, wet = vmem
    odd = (odd_ref[0] & 1) == 1
    grid = Grid(depth)
    per = grid.per
    masks = [grid.group == g for g in range(PACK)]

    def collect(at):
        out = grid.zero
        for g in range(PACK):
            out = jnp.where(masks[g], rolled(at(g), EDGE + GROUP * g, 1), out)
        return out

    def both(index, one, two):
        to_right = jnp.where(grid.first, one, rolled(two, EDGE, 1))
        to_left = jnp.where(grid.first, rolled(two, -EDGE, 1), one)
        store(even_way, index, jnp.where(odd, to_left, to_right))
        store(odd_way, index, jnp.where(odd, to_right, to_left))

    sources = [(wave, f * depth) for f in range(9)] + [(lame, 0), (shear, 0), (buoy, 0)]
    for f in range(0, FIELDS, 2):
        for h in (f, f + 1):
            (waves[h] if h < 9 else copies[h - 9]).wait()
        for j in range(per):
            pair = []
            for h in (f, f + 1):
                ref, base = sources[h]
                pair.append(collect(lambda g: plane(ref, base + per * g + j)))
                store(own, h * per + j, pair[-1])
            both((f // 2) * per + j, *pair)
    for copy in copies[3:]:
        copy.wait()
    flat = [plane(ocean, k) for k in range(3)] + [deep[...]]
    flat += [floor[...].astype(jnp.float32), wet[...].astype(jnp.float32)]
    for f in range(0, 6, 2):
        pair = []
        for h in (f, f + 1):
            pair.append(collect(lambda g: flat[h]))
            store(own_ocean, h, pair[-1])
        both((FIELDS // 2) * per + f // 2, *pair)


def partial_velocity(grid, stress, speed, buoy, out):
    sxx, syy, szz, sxy, sxz, syz = stress
    b_xx, b_xy, b_xz = grid.besides(sxx), grid.besides(sxy), grid.besides(sxz)
    for p in list(range(grid.depth, grid.planes)) + list(range(grid.depth)):
        rate = RATE * buoy(p)
        xy, yz, xz = sxy(p), syz(p), sxz(p)
        e_xy, e_xz = grid.edge_of(b_xy, p), grid.edge_of(b_xz, p)
        ax = grid.fx(sxx(p), grid.edge_of(b_xx, p)) + grid.by(xy) + grid.bz(sxz, p)
        store(out, p, speed[0](p) + rate * ax)
        ay = grid.bx(xy, e_xy) + grid.fy(syy(p)) + grid.bz(syz, p)
        store(out, grid.planes + p, speed[1](p) + rate * ay)
        az = grid.bx(xz, e_xz) + grid.by(yz) + grid.fz(szz, p)
        store(out, 2 * grid.planes + p, speed[2](p) + rate * az)


def partial_level(grid, flat, out):
    for k in range(3):
        x, y, wet = flat(FLUX_X, k), flat(FLUX_Y, k), flat(WET, k)
        edge = ocean_edge(grid, lambda q: flat(FLUX_X, q), k)
        spread = 0.5 * (grid.along(x, 1, edge) - grid.along(x, -1, edge))
        spread = spread + 0.5 * (grid.across(y, 1) - grid.across(y, -1))
        store(out, k, flat(LEVEL, k) - OCEAN_RATE * (wet * spread))


def ocean_edge(grid, at, k):
    if k:
        return None
    return rolled(jnp.where(grid.first, at(1), at(2)), LANES - EDGE, 1)


TO_HIGH = ((0, 7), (1, 6), (1, 7), (2, 7), (6, 6), (6, 7), (4, 7), (8, 6), (8, 7))
TO_LOW = ((0, 0), (0, 1), (1, 0), (2, 0), (2, 1), (6, 0), (4, 0), (4, 1), (8, 0))


def send_rows(grid, rows, take, level, flat, edge, out):
    at = 0
    for field, which in rows:
        for piece in take(field, which):
            out[at : at + piece.shape[0], :] = piece
            at += piece.shape[0]
    for which in (None, WET, FLOOR, FLUX_X, FLUX_Y):
        for k in range(3):
            source = level if which is None else flat[which]
            base = k * ROWS if which is None else flat[which, "at"] + k * ROWS
            out[at : at + 1, :] = row(source, base + edge)
            at += 1
    out[at : at + 1, :] = jnp.zeros((1, LANES), jnp.float32)


def send(grid, odd, more_high, more_low, take, level, flat, even_way, odd_way):
    @pl.when(odd)
    def _():
        send_rows(grid, TO_HIGH + more_high, take, level, flat, ROWS - 1, odd_way)
        send_rows(grid, TO_LOW + more_low, take, level, flat, 0, even_way)

    @pl.when(jnp.logical_not(odd))
    def _():
        send_rows(grid, TO_HIGH + more_high, take, level, flat, ROWS - 1, even_way)
        send_rows(grid, TO_LOW + more_low, take, level, flat, 0, odd_way)


def start_kernel(
    depth, odd_ref, wave, buoy, own, own_ocean, ocean, deep, floor, wet, even_in, odd_in,
    windows, flat, partial, level, even_way, odd_way,
):
    x_odd = (odd_ref[0] & 1) == 1
    left = (x_odd, even_in, odd_in)
    right = (x_odd, odd_in, even_in)
    grid = Grid(depth)
    per, planes = grid.per, grid.planes
    for f in range(FIELDS):
        for j in range(per):
            mine = plane(own, f * per + j)
            a = plane(left, (f // 2) * per + j)
            b = plane(right, (f // 2) * per + j)
            if f % 2:
                a, b = rolled(a, -EDGE, 1), rolled(b, EDGE, 1)
            store(windows, f * 2 * per + j, jnp.where(grid.first, a, mine))
            store(windows, f * 2 * per + per + j, jnp.where(grid.first, mine, b))
    whole = [plane(ocean, k) for k in range(3)] + [deep[...]]
    whole += [floor[...].astype(jnp.float32), wet[...].astype(jnp.float32)]
    for f in range(6):
        mine = plane(own_ocean, f)
        a = plane(left, (FIELDS // 2) * per + f // 2)
        b = plane(right, (FIELDS // 2) * per + f // 2)
        if f % 2:
            a, b = rolled(a, -EDGE, 1), rolled(b, EDGE, 1)
        store(flat, 3 * f, whole[f])
        store(flat, 3 * f + 1, jnp.where(grid.first, a, mine))
        store(flat, 3 * f + 2, jnp.where(grid.first, mine, b))

    def field(f):
        ref, base = (buoy, 0) if f == BUOY else (wave, f * depth)
        return lambda p: plane(ref, base + p) if p < depth else plane(windows, f * 2 * per + p - depth)

    partial_velocity(grid, [field(3 + f) for f in range(6)], [field(f) for f in range(3)], field(BUOY), partial)
    partial_level(grid, lambda f, k: plane(flat, 3 * f + k), level)

    def take(f, which):
        if f < 3:
            return [partial[pl.ds(f * planes * ROWS + which, planes, stride=ROWS), :]]
        ref, base = (buoy, 0) if f == BUOY else (wave, f * depth)
        return [
            ref[pl.ds(base * ROWS + which, depth, stride=ROWS), :],
            windows[pl.ds(f * 2 * per * ROWS + which, 2 * per, stride=ROWS), :],
        ]

    flats = {}
    for which in (WET, FLOOR, FLUX_X, FLUX_Y):
        flats[which] = flat
        flats[which, "at"] = 3 * which * ROWS
    send(grid, (odd_ref[1] & 1) == 1, ((BUOY, 6), (BUOY, 7)), ((BUOY, 0), (BUOY, 1)), take, level, flats, even_way, odd_way)


def finish(grid, stress_rows, buoy, partial, level, now, fixed, low, high, low_buoy, high_buoy, halo, corr, speed, new):
    depth, per, planes = grid.depth, grid.per, grid.planes

    def piece(ref, index, part):
        start, size = part
        return either(ref, lambda one: one[index * planes + start : index * planes + start + size, :])

    for part in ((0, depth), (depth, 2 * per)):
        start, size = part
        lo = lambda index: piece(low, index, part)
        hi = lambda index: piece(high, index, part)
        own = lambda f, which: stress_rows(f, which, part)

        def put(ref, index, value):
            ref[index * planes + start : index * planes + start + size, :] = value

        b1 = RATE * piece(low_buoy, 10, part)
        b2 = RATE * piece(low_buoy, 9, part)
        b8 = RATE * piece(high_buoy, 9, part)
        b9 = RATE * piece(high_buoy, 10, part)
        xy0, xy6, xy7 = own(6, 0), own(6, 6), own(6, 7)
        yz0, yz6, yz7 = own(8, 0), own(8, 6), own(8, 7)
        yy0, yy1, yy7 = own(4, 0), own(4, 1), own(4, 7)
        put(halo, 0, lo(0) - b1 * xy0)
        put(halo, 1, hi(0) + b8 * (xy6 - 27.0 * xy7))
        put(halo, 2, hi(1) + b9 * xy7)
        put(halo, 3, lo(2) + b1 * (27.0 * yy0 - yy1))
        put(halo, 4, lo(1) - b2 * yy0)
        put(halo, 5, hi(2) + b8 * yy7)
        put(halo, 6, lo(3) - b1 * yz0)
        put(halo, 7, hi(3) + b8 * (yz6 - 27.0 * yz7))
        put(halo, 8, hi(4) + b9 * yz7)
        put(corr, 0, lo(4) - 27.0 * lo(5))
        put(corr, 1, lo(5))
        put(corr, 2, -hi(5))
        put(corr, 3, lo(6))
        put(corr, 4, -hi(6))
        put(corr, 5, 27.0 * hi(6) - hi(7))
        put(corr, 6, lo(7) - 27.0 * lo(8))
        put(corr, 7, lo(8))
        put(corr, 8, -hi(8))

    sub = grid.sub
    floor = [fixed(FLOOR, k) for k in range(3)]
    sums = [grid.zero] * 3
    depths = grid.group.astype(jnp.float32) * per
    for p in range(planes):
        rate = RATE * buoy(p)
        c = [row(corr, index * planes + p) for index in range(9)]
        pick = lambda at, r0, r1, r2: jnp.where(
            sub == at[0], r0, jnp.where(sub == at[1], r1, jnp.where(sub == at[2], r2, 0.0))
        )
        store(speed, p, plane(partial, p) + rate * pick((0, 1, 7), c[0], c[1], c[2]))
        store(speed, planes + p, plane(partial, planes + p) + rate * pick((0, 6, 7), c[3], c[4], c[5]))
        vz = plane(partial, 2 * planes + p) + rate * pick((0, 1, 7), c[6], c[7], c[8])
        store(speed, 2 * planes + p, vz)
        if p < depth:
            k, at = 0, float(p)
        else:
            side, which = divmod(p - depth, per)
            k, at = 1 + side, depths + float(which)
        sums[k] = jnp.where(floor[k] == at, vz, sums[k])
    sums[1] = grid.every_group(sums[1])
    sums[2] = grid.every_group(sums[2])

    tail = tail_high = low[1].shape[0] - 16
    ends = []
    for message, base, index, own_row, sign in ((low, tail, 6, 0, -1.0), (high, tail_high, 7, 7, 1.0)):
        lines = lambda which, k, message=message, base=base: row(message, base + 3 * which + k)
        zs = lax.broadcasted_iota(jnp.int32, (depth, LANES), 0).astype(jnp.float32)
        main = halo[index * planes : index * planes + depth, :]
        floors = [jnp.sum(jnp.where(lines(2, 0) == zs, main, 0.0), axis=0, keepdims=True)]
        side = halo[index * planes + depth : (index + 1) * planes, :]
        half = lax.broadcasted_iota(jnp.int32, (2 * per, LANES), 0)
        group = (lax.broadcasted_iota(jnp.int32, (2 * per, LANES), 1) // GROUP) * per
        where = jnp.where(half < per, lines(2, 1), lines(2, 2))
        side = jnp.where(where == (group + half % per).astype(jnp.float32), side, 0.0)
        side = grid.every_group(side)
        floors.append(jnp.sum(jnp.where(half < per, side, 0.0), axis=0, keepdims=True))
        floors.append(jnp.sum(jnp.where(half < per, 0.0, side), axis=0, keepdims=True))
        end = []
        for k in range(3):
            mine = now(FLUX_Y, k)[own_row : own_row + 1, :]
            wet = lines(1, k)
            end.append(lines(0, k) + wet * (UPLIFT * floors[k] + (sign * 0.5 * OCEAN_RATE) * mine))
        ends.append((end, lines))
    (low_level, low_line), (high_level, high_line) = ends

    levels = []
    for k in range(3):
        wet = fixed(WET, k)
        beside = jnp.where(sub == 0, low_line(4, k), jnp.where(sub == ROWS - 1, -high_line(4, k), 0.0))
        levels.append(
            plane(level, k) + wet * (UPLIFT * sums[k] + (0.5 * OCEAN_RATE) * beside)
        )
        new(LEVEL, k, levels[k])
    for k in range(3):
        wet, deep = fixed(WET, k), fixed(DEPTH, k)
        edge = ocean_edge(grid, lambda q: levels[q], k)
        slope_x = 0.5 * (grid.along(levels[k], 1, edge) - grid.along(levels[k], -1, edge))
        lo, hi = (low_level[k],), (high_level[k],)
        slope_y = 0.5 * (grid.across(levels[k], 1, lo, hi) - grid.across(levels[k], -1, lo, hi))
        for which, line, slope in ((FLUX_X, 3, slope_x), (FLUX_Y, 4, slope_y)):
            x = now(which, k)
            edge = ocean_edge(grid, lambda q: now(which, q), k)
            lo, hi = (low_line(line, k),), (high_line(line, k),)
            laplace = grid.along(x, 1, edge) + grid.along(x, -1, edge)
            laplace = laplace + grid.across(x, 1, lo, hi) + grid.across(x, -1, lo, hi) - 4.0 * x
            new(which, k, wet * (x - OCEAN_RATE * deep * slope + VISCOUS * laplace))
    return levels


def new_stress(grid, todo, stress, lame, shear, speed, halo, levels, fixed, out):
    depth, per, planes = grid.depth, grid.per, grid.planes
    vx, vy, vz = [lambda p, f=f: plane(speed, f * planes + p) for f in range(3)]
    b_x, b_y, b_z = grid.besides(vx), grid.besides(vy), grid.besides(vz)
    press = [LOADING * fixed(WET, k) * levels[k] for k in range(3)]
    floor = [fixed(FLOOR, k) for k in range(3)]
    depths = grid.group.astype(jnp.float32) * per
    for p in todo:
        h = [row(halo, index * planes + p) for index in range(9)]
        x, y, z = vx(p), vy(p), vz(p)
        e_x, e_y, e_z = [grid.edge_of(b, p) for b in (b_x, b_y, b_z)]
        strain_x = grid.bx(x, e_x)
        strain_y = grid.by(y, (h[3], h[4]), (h[5], h[5]))
        strain_z = grid.bz(vz, p)
        mu = RATE * shear(p)
        spread = (RATE * lame(p)) * (strain_x + strain_y + strain_z)
        two = mu + mu
        if p < depth:
            k, at = 0, float(p)
        else:
            side, which = divmod(p - depth, per)
            k, at = 1 + side, depths + float(which)
        out(0, p, stress[0](p) + (spread + two * strain_x))
        out(1, p, stress[1](p) + (spread + two * strain_y))
        out(2, p, stress[2](p) + (spread + two * strain_z) - jnp.where(floor[k] == at, press[k], 0.0))
        xy = grid.fy(x, (h[0], h[0]), (h[1], h[2])) + grid.fx(y, e_y)
        out(3, p, stress[3](p) + mu * xy)
        xz = grid.fz(vx, p) + grid.fx(z, e_z)
        out(4, p, stress[4](p) + mu * xz)
        yz = grid.fz(vy, p) + grid.fy(z, (h[6], h[6]), (h[7], h[8]))
        out(5, p, stress[5](p) + mu * yz)


def middle_kernel(
    depth, odd_ref, wave, lame, shear, buoy, windows, flat, partial, level, even_in, odd_in,
    stress_out, ocean_out, partial_out, level_out, even_way, odd_way,
    halo, corr, speed,
):
    odd = (odd_ref[1] & 1) == 1
    from_low, from_high = (odd, even_in, odd_in), (odd, odd_in, even_in)
    grid = Grid(depth)
    per, planes = grid.per, grid.planes

    def field(f):
        refs = {LAME: lame, SHEAR: shear, BUOY: buoy}
        ref, base = (refs[f], 0) if f in refs else (wave, f * depth)
        return lambda p: plane(ref, base + p) if p < depth else plane(windows, f * 2 * per + p - depth)

    def stress_rows(f, which, part):
        if part[0] == 0:
            return wave[pl.ds(f * depth * ROWS + which, depth, stride=ROWS), :]
        return windows[pl.ds(f * 2 * per * ROWS + which, 2 * per, stride=ROWS), :]

    flats = lambda f, k: plane(flat, 3 * f + k)
    levels = finish(
        grid, stress_rows, field(BUOY), partial, level, flats, flats, from_low, from_high, from_low, from_high,
        halo, corr, speed, lambda which, k, value: store(ocean_out, 3 * which + k, value),
    )
    order = list(range(depth, planes)) + list(range(depth))
    new_stress(
        grid, order, [field(3 + f) for f in range(6)], field(LAME), field(SHEAR), speed, halo, levels, flats,
        lambda f, p, value: store(stress_out, f * planes + p, value),
    )
    stress = [lambda p, f=f: plane(stress_out, f * planes + p) for f in range(6)]
    speeds = [lambda p, f=f: plane(speed, f * planes + p) for f in range(3)]
    partial_velocity(grid, stress, speeds, field(BUOY), partial_out)
    both = lambda f, k: plane(flat if f >= DEPTH else ocean_out, 3 * f + k)
    partial_level(grid, both, level_out)

    def take(f, which):
        ref, f = (partial_out, f) if f < 3 else (stress_out, f - 3)
        return [ref[pl.ds(f * planes * ROWS + which, planes, stride=ROWS), :]]

    rows_of = {}
    for which in (WET, FLOOR, FLUX_X, FLUX_Y):
        rows_of[which] = flat if which >= DEPTH else ocean_out
        rows_of[which, "at"] = 3 * which * ROWS
    send(grid, (odd_ref[1] & 1) == 1, (), (), take, level_out, rows_of, even_way, odd_way)


def last_kernel(
    depth, odd_ref, lame, shear, buoy, windows, flat, stress_in, ocean, partial, level,
    even_first, odd_first, even_in, odd_in,
    wave_out, ocean_out,
    halo, corr, speed,
):
    odd = (odd_ref[1] & 1) == 1
    low_buoy, high_buoy = (odd, even_first, odd_first), (odd, odd_first, even_first)
    from_low, from_high = (odd, even_in, odd_in), (odd, odd_in, even_in)
    grid = Grid(depth)
    per, planes = grid.per, grid.planes

    def field(f):
        ref = {LAME: lame, SHEAR: shear, BUOY: buoy}[f]
        return lambda p: plane(ref, p) if p < depth else plane(windows, f * 2 * per + p - depth)

    def stress_rows(f, which, part):
        start, size = part
        return stress_in[pl.ds(((f - 3) * planes + start) * ROWS + which, size, stride=ROWS), :]

    def new(which, k, value):
        if k == 0:
            store(ocean_out, which, value)

    fixed = lambda f, k: plane(flat, 3 * f + k)
    now = lambda f, k: plane(ocean, 3 * f + k)
    levels = finish(
        grid, stress_rows, field(BUOY), partial, level, now, fixed, from_low, from_high, low_buoy, high_buoy,
        halo, corr, speed, new,
    )
    stress = [lambda p, f=f: plane(stress_in, f * planes + p) for f in range(6)]
    new_stress(
        grid, list(range(depth)), stress, field(LAME), field(SHEAR), speed, halo, levels, fixed,
        lambda f, p, value: store(wave_out, (3 + f) * depth + p, value),
    )
    for f in range(3):
        for p in range(depth):
            store(wave_out, f * depth + p, plane(speed, f * planes + p))


VMEM = pl.BlockSpec(memory_space=pltpu.VMEM)
SMEM = pl.BlockSpec(memory_space=pltpu.SMEM)
HBM = pl.BlockSpec(memory_space=pltpu.HBM)


def call(kernel, shapes, scratch, flags, *arguments, place=VMEM):
    return pl.pallas_call(
        kernel,
        out_shape=[s if hasattr(s, "dtype") else jax.ShapeDtypeStruct((s, LANES), jnp.float32) for s in shapes],
        in_specs=[SMEM] + [place] * len(arguments),
        out_specs=[VMEM] * len(shapes),
        scratch_shapes=[pltpu.VMEM((s, LANES), jnp.float32) if isinstance(s, int) else s for s in scratch],
        compiler_params=pltpu.CompilerParams(vmem_limit_bytes=24 * 1024 * 1024),
    )(flags, *arguments)


def exchange(axis, even_way, odd_way, odd_first):
    count = lax.axis_size(axis)

    def swap(x, start):
        pairs = [(i, i + 1) for i in range(start, count - 1, 2)]
        return lax.ppermute(x, axis, pairs + [(j, i) for i, j in pairs])

    if odd_first:
        odd_in = swap(odd_way, 1)
        return swap(even_way, 0), odd_in
    even_in = swap(even_way, 0)
    return even_in, swap(odd_way, 1)


def local(wave_fields, lame_lambda, shear_modulus, buoyancy, ocean_state, water_depth, seafloor_index, wet_mask):
    depth = wave_fields.shape[1]
    per = depth // PACK
    planes = depth + 2 * per
    inputs = [wave_fields, lame_lambda, shear_modulus, buoyancy, ocean_state, water_depth, seafloor_index, wet_mask]
    inputs = [x.reshape(-1, LANES) for x in inputs]
    flags = jnp.stack([lax.axis_index("gx"), lax.axis_index("gy")])

    def bind(kernel):
        return lambda *refs: kernel(depth, *refs)

    edge = (FIELDS // 2 * per + 3) * ROWS
    copies = [jax.ShapeDtypeStruct(x.shape, x.dtype) for x in inputs]
    *inputs, own, own_ocean, even_way, odd_way = call(
        bind(edges_kernel), copies + [FIELDS * per * ROWS, 6 * ROWS, edge, edge], [pltpu.SemaphoreType.DMA((16,))],
        flags, *inputs, place=HBM,
    )
    wave, lame, shear, buoy, ocean, deep, floor, wet = inputs
    x_in = exchange("gx", even_way, odd_way, True)
    first = 11 * planes + 16
    later = 9 * planes + 16
    windows, flat, partial, level, even_way, odd_way = call(
        bind(start_kernel),
        [FIELDS * 2 * per * ROWS, 18 * ROWS, 3 * planes * ROWS, 3 * ROWS, first, first], [],
        flags, wave, buoy, own, own_ocean, ocean, deep, floor, wet, *x_in,
    )
    y_in = exchange("gy", even_way, odd_way, False)
    scratch = [9 * planes, 9 * planes, 3 * planes * ROWS]
    stress, ocean1, partial, level, even_way, odd_way = call(
        bind(middle_kernel),
        [6 * planes * ROWS, 9 * ROWS, 3 * planes * ROWS, 3 * ROWS, later, later], scratch,
        flags, wave, lame, shear, buoy, windows, flat, partial, level, *y_in,
    )
    y_in2 = exchange("gy", even_way, odd_way, False)
    wave_out, ocean_out = call(
        bind(last_kernel), [wave.shape[0], ocean.shape[0]], scratch,
        flags, lame, shear, buoy, windows, flat, stress, ocean1, partial, level, *y_in, *y_in2,
    )
    return wave_out.reshape(wave_fields.shape), ocean_out.reshape(ocean_state.shape)


def solution(mesh):
    in_specs = (
        P(None, None, "gy", "gx"),
        P(None, "gy", "gx"),
        P(None, "gy", "gx"),
        P(None, "gy", "gx"),
        P(None, "gy", "gx"),
        P("gy", "gx"),
        P("gy", "gx"),
        P("gy", "gx"),
    )
    out_specs = (P(None, None, "gy", "gx"), P(None, "gy", "gx"))
    return jax.shard_map(local, mesh=mesh, in_specs=in_specs, out_specs=out_specs, check_vma=False)
```

```python
import jax
import jax.numpy as jnp
from jax import lax
from jax.experimental import pallas as pl
from jax.experimental.pallas import tpu as pltpu
from jax.sharding import PartitionSpec as P

RATE = 0.3 / 24.0
OCEAN_RATE = 0.3
UPLIFT = 0.5
LOADING = 0.5
VISCOUS = 0.1

ROWS = 8
SUB = 8
LANES = 128
EDGE = 8
GROUP = 2 * EDGE
TILES = 4
HALF = TILES * GROUP
SPAN = TILES + 1
WINDOW = TILES

LEVEL, FLUX_X, FLUX_Y, DEPTH, FLOOR, WET = range(6)
VX, VY, VZ, SXX, SYY, SZZ, SXY, SXZ, SYZ, LAME, SHEAR, BUOY = range(12)
FIELDS = 12

OPEN = ((VX, 0), (VX, 1), (VX, 7), (VY, 0), (VY, 6), (VY, 7), (VZ, 0), (VZ, 1), (VZ, 7))
CLOSED = tuple((c, y) for y in range(ROWS) for c in (VX, VY, VZ) if (c, y) not in OPEN)
INNER = (3, 4)
OUTER = tuple(y for y in range(ROWS) if y not in INNER)

SPEED_HIGH = ((VX, 7), (VY, 6), (VY, 7), (VZ, 7))
SPEED_LOW = ((VX, 0), (VX, 1), (VY, 0), (VZ, 0), (VZ, 1))
STRESS_HIGH = ((SXY, 6), (SXY, 7), (SYY, 7), (SYZ, 6), (SYZ, 7))
STRESS_LOW = ((SXY, 0), (SYY, 0), (SYY, 1), (SYZ, 0))
BUOY_HIGH = ((BUOY, 6), (BUOY, 7))
BUOY_LOW = ((BUOY, 0), (BUOY, 1))
LINES = (None, WET, FLOOR, FLUX_X, FLUX_Y)


def rolled(x, shift, axis):
    shift %= x.shape[axis]
    return x if shift == 0 else pltpu.roll(x, shift, axis)


def tile(ref, index):
    return ref[index * SUB : (index + 1) * SUB, :]


def row(ref, index):
    return ref[index : index + 1, :]


def store(ref, index, value):
    ref[index * SUB : (index + 1) * SUB, :] = value


def minus(a, b):
    if b is None:
        return a
    return -b if a is None else a - b


def near_far(a, b, c, d):
    near, far = 27.0 * minus(a, b), minus(c, d)
    return near if c is None and d is None else near - far


class Grid:
    def __init__(self):
        self.sub = lax.broadcasted_iota(jnp.int32, (SUB, LANES), 0)
        self.lane = lax.broadcasted_iota(jnp.int32, (SUB, LANES), 1)
        self.first = self.lane % GROUP < EDGE
        self.left = self.lane < HALF
        self.group = self.lane // GROUP
        self.zero = jnp.zeros((SUB, LANES), jnp.float32)
        depth = [self.sub + SUB * t for t in range(TILES)] + [self.sub + SUB * (self.group % TILES)]
        self.depth = [d.astype(jnp.float32) for d in depth]

    def beside(self, window):
        return jnp.where(self.first, window, rolled(window, HALF, 1))

    def edge(self, beside, t):
        return None if t == WINDOW else rolled(beside, LANES - EDGE - GROUP * t, 1)

    def along(self, x, offset, edge):
        if edge is not None:
            lane = self.lane
            keep = {-1: lane == LANES - 1, -2: lane >= LANES - 2, 1: lane == 0, 2: lane <= 1}[offset]
            x = jnp.where(keep, edge, x)
        return rolled(x, -offset, 1)

    def fx(self, x, edge):
        return near_far(self.along(x, 1, edge), x, self.along(x, 2, edge), self.along(x, -1, edge))

    def bx(self, x, edge):
        return near_far(x, self.along(x, -1, edge), self.along(x, 1, edge), self.along(x, -2, edge))

    def around(self, field, y, t):
        if t == WINDOW:
            x, at = field(y, t), self.lane % HALF
            above = jnp.where(at >= GROUP, rolled(x, GROUP, 1), 0.0)
            return above, x, jnp.where(at < HALF - GROUP, rolled(x, -GROUP, 1), 0.0)
        above = field(y, t - 1) if t else self.zero
        return above, field(y, t), field(y, t + 1) if t + 1 < TILES else self.zero

    def down(self, three, offset):
        above, x, below = three
        sub = self.sub
        keep = {-1: sub == SUB - 1, -2: sub >= SUB - 2, 1: sub == 0, 2: sub <= 1}[offset]
        return rolled(jnp.where(keep, above if offset < 0 else below, x), -offset, 0)

    def fz(self, field, y, t):
        three = self.around(field, y, t)
        return near_far(self.down(three, 1), three[1], self.down(three, 2), self.down(three, -1))

    def bz(self, field, y, t):
        three = self.around(field, y, t)
        return near_far(three[1], self.down(three, -1), self.down(three, 1), self.down(three, -2))

    def fy(self, field, y, t):
        return near_far(field(y + 1, t), field(y, t), field(y + 2, t), field(y - 1, t))

    def by(self, field, y, t):
        return near_far(field(y, t), field(y - 1, t), field(y + 1, t), field(y - 2, t))

    def windows(self, own, from_left, from_right):
        return jnp.where(
            self.left, jnp.where(self.first, from_left, own), jnp.where(self.first, own, from_right)
        )

    def every_group(self, x):
        for shift in (GROUP, 2 * GROUP):
            x = x + jnp.where(self.lane % HALF >= shift, rolled(x, shift, 1), rolled(x, shift - HALF, 1))
        return x

    def across(self, x, offset, beside):
        end = 0 if offset < 0 else ROWS - 1
        return jnp.where(self.sub == end, beside, rolled(x, -offset, 0))


def inside(field):
    return lambda y, t: field(y, t) if 0 <= y < ROWS else None


def fields_of(main, windows):
    def field(f):
        return lambda y, t: tile(windows, f * ROWS + y) if t == WINDOW else tile(main, (f * ROWS + y) * TILES + t)

    return field


def pack(grid, items, odd, even_way, odd_way, index):
    a, b, c, d = items
    first, left = grid.first, grid.left
    right_way = jnp.where(
        left, jnp.where(first, a, rolled(b, EDGE, 1)), jnp.where(first, c, rolled(d, EDGE, 1))
    )
    left_way = jnp.where(
        left, jnp.where(first, rolled(b, -EDGE, 1), a), jnp.where(first, rolled(d, -EDGE, 1), c)
    )
    store(even_way, index, jnp.where(odd, left_way, right_way))
    store(odd_way, index, jnp.where(odd, right_way, left_way))


def unpack(grid, items, odd, even_in, odd_in, index):
    x, y = tile(even_in, index), tile(odd_in, index)
    before, after = jnp.where(odd, x, y), jnp.where(odd, y, x)
    befores = [before, rolled(before, -EDGE, 1), rolled(before, HALF, 1), rolled(before, HALF - EDGE, 1)]
    afters = [rolled(after, HALF, 1), rolled(after, HALF + EDGE, 1), after, rolled(after, EDGE, 1)]
    return [grid.windows(*three) for three in zip(items, befores, afters)]


def edges_kernel(flags, *refs):
    hbm, refs = refs[:8], refs[8:]
    (main, flat, own, own_flat, even_way, odd_way), (wave, lame, shear, buoy, ocean, deep, floor, wet), sem = (
        refs[:6], refs[6:14], refs[14],
    )
    size = wave.shape[0] // 9
    copies = []
    for f in range(9):
        part = slice(f * size, (f + 1) * size)
        copies.append(pltpu.make_async_copy(hbm[0].at[part, :], wave.at[part, :], sem.at[f]))
    for k, target in enumerate((lame, shear, buoy, ocean, deep, floor, wet)):
        copies.append(pltpu.make_async_copy(hbm[1 + k], target, sem.at[9 + k]))
    for copy in copies:
        copy.start()
    grid = Grid()
    odd = (flags[0] & 1) == 1
    sources = [(wave, f) for f in range(9)] + [(lame, 0), (shear, 0), (buoy, 0)]
    for f in range(0, FIELDS, 2):
        copies[f].wait()
        copies[f + 1].wait()
        for q in range(0, ROWS, 2):
            items = []
            for y in (q, q + 1):
                for h in (f, f + 1):
                    ref, base = sources[h]
                    out = grid.zero
                    for t in range(TILES):
                        x = ref[pl.ds(base * size + t * SUB * ROWS + y, SUB, stride=ROWS), :]
                        store(main, (h * ROWS + y) * TILES + t, x)
                        out = jnp.where(grid.group == t, rolled(x, EDGE + GROUP * t, 1), out)
                    out = jnp.where(grid.left, out, rolled(out, HALF, 1))
                    store(own, h * ROWS + y, out)
                    items.append(out)
            pack(grid, items, odd, even_way, odd_way, (f * ROWS // 2 + q) // 2)
    for copy in copies[FIELDS:]:
        copy.wait()
    planes = [tile(ocean, k) for k in range(3)] + [deep[...]]
    planes += [floor[...].astype(jnp.float32), wet[...].astype(jnp.float32)]
    items = []
    for k, x in enumerate(planes):
        store(flat, k, x)
        out = grid.zero
        for g in range(LANES // GROUP):
            out = jnp.where(grid.group == g, rolled(x, EDGE + GROUP * g, 1), out)
        store(own_flat, k, out)
        items.append(out)
    pack(grid, items[:4], odd, even_way, odd_way, FIELDS * ROWS // 4)
    pack(grid, items[4:] * 2, odd, even_way, odd_way, FIELDS * ROWS // 4 + 1)


def speeds(grid, stress, speed, buoy, todo, put):
    sxx, syy, szz, sxy, sxz, syz = stress
    for y in range(ROWS):
        parts = [c for c in (VX, VY, VZ) if (c, y) in todo]
        if not parts:
            continue
        need = {VX: (sxx,), VY: (sxy,), VZ: (sxz,)}
        beside = {c: grid.beside(need[c][0](y, WINDOW)) for c in parts}
        for t in range(SPAN):
            rate = RATE * buoy(y, t)
            for c in parts:
                edge = grid.edge(beside[c], t)
                if c == VX:
                    a = grid.fx(sxx(y, t), edge) + grid.by(sxy, y, t) + grid.bz(sxz, y, t)
                elif c == VY:
                    a = grid.bx(sxy(y, t), edge) + grid.fy(syy, y, t) + grid.bz(syz, y, t)
                else:
                    a = grid.bx(sxz(y, t), edge) + grid.by(syz, y, t) + grid.fz(szz, y, t)
                put(c, y, t, speed(c)(y, t) + rate * a)


def stresses(grid, rows, tiles, speed, stress, lame, shear, put):
    vx, vy, vz = [speed(c) for c in (VX, VY, VZ)]
    for y in rows:
        b_x, b_y, b_z = [grid.beside(v(y, WINDOW)) for v in (vx, vy, vz)]
        for t in range(tiles):
            e_x, e_y, e_z = [grid.edge(b, t) for b in (b_x, b_y, b_z)]
            strain_x = grid.bx(vx(y, t), e_x)
            strain_y = grid.by(vy, y, t)
            strain_z = grid.bz(vz, y, t)
            mu = RATE * shear(y, t)
            spread = (RATE * lame(y, t)) * (strain_x + strain_y + strain_z)
            two = mu + mu
            put(SXX, y, t, stress(SXX)(y, t) + (spread + two * strain_x))
            put(SYY, y, t, stress(SYY)(y, t) + (spread + two * strain_y))
            put(SZZ, y, t, stress(SZZ)(y, t) + (spread + two * strain_z))
            put(SXY, y, t, stress(SXY)(y, t) + mu * (grid.fy(vx, y, t) + grid.fx(vy(y, t), e_y)))
            put(SXZ, y, t, stress(SXZ)(y, t) + mu * (grid.fz(vx, y, t) + grid.fx(vz(y, t), e_z)))
            put(SYZ, y, t, stress(SYZ)(y, t) + mu * (grid.fz(vy, y, t) + grid.fy(vz, y, t)))


def flat_edge(grid, at, k):
    return grid.edge(grid.beside(at(1)), 0) if k == 0 else None


def partial_level(grid, flat, put):
    for k in range(2):
        x, y = flat(FLUX_X, k), flat(FLUX_Y, k)
        edge = flat_edge(grid, lambda q: flat(FLUX_X, q), k)
        spread = 0.5 * (grid.along(x, 1, edge) - grid.along(x, -1, edge))
        spread = spread + 0.5 * (grid.across(y, 1, 0.0) - grid.across(y, -1, 0.0))
        put(k, flat(LEVEL, k) - OCEAN_RATE * (flat(WET, k) * spread))


class Message:
    def __init__(self, rows, thin):
        self.at, size = [], 0
        for f, _ in rows:
            self.at.append(size)
            size += TILES if thin and f < 3 else SPAN
        self.tiles = self.at[1:] + [size]
        self.tiles = [b - a for a, b in zip(self.at, self.tiles)]
        self.rows = rows
        self.base = size * SUB
        self.size = self.base + 2 * SUB


def messages(first):
    high = SPEED_HIGH + STRESS_HIGH + (BUOY_HIGH if first else ())
    low = SPEED_LOW + STRESS_LOW + (BUOY_LOW if first else ())
    return Message(high, not first), Message(low, not first)


def message_size(first):
    return max(m.size for m in messages(first))


def send(first, odd, field, line, even_way, odd_way):
    high, low = messages(first)

    def fill(message, edge, out):
        for (f, y), at, tiles in zip(message.rows, message.at, message.tiles):
            for t in range(tiles):
                store(out, at + t, field(f)(y, t))
        at = message.base
        for which in LINES:
            for k in range(2):
                out[at : at + 1, :] = line(which, k, edge)
                at += 1
        out[at : at + 6, :] = jnp.zeros((6, LANES), jnp.float32)
        tail = out.shape[0]
        if message.size < tail:
            out[message.size : tail, :] = jnp.zeros((tail - message.size, LANES), jnp.float32)

    @pl.when(odd)
    def _():
        fill(high, ROWS - 1, odd_way)
        fill(low, 0, even_way)

    @pl.when(jnp.logical_not(odd))
    def _():
        fill(high, ROWS - 1, even_way)
        fill(low, 0, odd_way)


class Received:
    def __init__(self, message, odd, if_odd, if_even):
        self.message, self.odd, self.refs = message, odd, (if_odd, if_even)

    def pick(self, take):
        return jnp.where(self.odd, take(self.refs[0]), take(self.refs[1]))

    def __call__(self, index, t):
        return self.pick(lambda ref: tile(ref, self.message.at[index] + t))

    def line(self, which, k):
        at = self.message.base + 2 * LINES.index(which) + k
        return self.pick(lambda ref: row(ref, at))


def received(first, odd, even_in, odd_in):
    high, low = messages(first)
    return Received(high, odd, even_in, odd_in), Received(low, odd, odd_in, even_in)


AROUND = ROWS + 4


def finish(grid, tiles, partial, stress, buoy, lo, hi, lo_buoy, hi_buoy, speed):
    sxy, syy, syz = [stress(f) for f in (SXY, SYY, SYZ)]

    def put(c, y, t, value):
        store(speed, (c * AROUND + y + 2) * SPAN + t, value)

    for t in range(SPAN):
        sends = {"xy": (4, 5), "yz": (7, 8)}
        for c, key, at in ((VX, "xy", 5), (VZ, "yz", 8)):
            two, one = lo(sends[key][0], t), lo(sends[key][1], t)
            rate = [RATE * buoy(y, t) for y in (0, 1, 7)]
            put(c, 0, t, partial(c, 0, t) + rate[0] * (two - 27.0 * one))
            put(c, 1, t, partial(c, 1, t) + rate[1] * one)
            put(c, 7, t, partial(c, 7, t) - rate[2] * hi(at, t))
        h8, h9 = hi(6, t), hi(7, t)
        put(VY, 0, t, partial(VY, 0, t) + (RATE * buoy(0, t)) * lo(6, t))
        put(VY, 6, t, partial(VY, 6, t) - (RATE * buoy(6, t)) * h8)
        put(VY, 7, t, partial(VY, 7, t) + (RATE * buoy(7, t)) * (27.0 * h8 - h9))
    for t in range(tiles):
        b2, b1 = RATE * lo_buoy(9, t), RATE * lo_buoy(10, t)
        b8, b9 = RATE * hi_buoy(9, t), RATE * hi_buoy(10, t)
        put(VX, -1, t, lo(0, t) - b1 * sxy(0, t))
        put(VY, -2, t, lo(1, t) - b2 * syy(0, t))
        put(VY, -1, t, lo(2, t) + b1 * (27.0 * syy(0, t) - syy(1, t)))
        put(VZ, -1, t, lo(3, t) - b1 * syz(0, t))
        put(VX, 8, t, hi(0, t) + b8 * (sxy(6, t) - 27.0 * sxy(7, t)))
        put(VX, 9, t, hi(1, t) + b9 * sxy(7, t))
        put(VY, 8, t, hi(2, t) + b8 * syy(7, t))
        put(VZ, 8, t, hi(3, t) + b8 * (syz(6, t) - 27.0 * syz(7, t)))
        put(VZ, 9, t, hi(4, t) + b9 * syz(7, t))


def seafloor(grid, vz, y, floors, out, index):
    total = None
    for t in range(TILES):
        part = jnp.where(floors[0] == grid.depth[t], vz(y, t), 0.0)
        total = part if total is None else total + part
    out[index : index + 1, :] = jnp.sum(total, axis=0, keepdims=True)
    if len(floors) > 1:
        part = jnp.where(floors[1] == grid.depth[WINDOW], vz(y, WINDOW), 0.0)
        out[2 * SUB + index : 2 * SUB + index + 1, :] = jnp.sum(part, axis=0, keepdims=True)


def sea(grid, speed, level, now, fixed, line, lo, hi, sums, new, last):
    vz = speed(VZ)
    for y in range(ROWS):
        seafloor(grid, vz, y, [line(FLOOR, k, y) for k in range(2)], sums, y)
    ends = 1 if last else 2
    for y, side, at in ((-1, lo, ROWS), (ROWS, hi, ROWS + 1)):
        seafloor(grid, vz, y, [side.line(FLOOR, k) for k in range(ends)], sums, at)
    floors, beyond = [tile(sums, 0), grid.every_group(tile(sums, 2))], [tile(sums, 1), None]
    if not last:
        beyond[1] = grid.every_group(tile(sums, 3))
    sub = grid.sub
    levels, lows, highs = [], [], []
    for k in range(2):
        near = jnp.where(sub == 0, lo.line(FLUX_Y, k), jnp.where(sub == ROWS - 1, -hi.line(FLUX_Y, k), 0.0))
        levels.append(level(k) + fixed(WET, k) * (UPLIFT * floors[k] + (0.5 * OCEAN_RATE) * near))
        new(LEVEL, k, levels[k])
        if k < ends:
            for side, at, y, sign, out in ((lo, 0, 0, -1.0, lows), (hi, 1, ROWS - 1, 1.0, highs)):
                mine = (sign * 0.5 * OCEAN_RATE) * line(FLUX_Y, k, y)
                rest = UPLIFT * beyond[k][at : at + 1, :] + mine
                out.append(side.line(None, k) + side.line(WET, k) * rest)
    for k in range(ends):
        wet, deep = fixed(WET, k), fixed(DEPTH, k)
        edge = flat_edge(grid, lambda q: levels[q], k)
        slope_x = 0.5 * (grid.along(levels[k], 1, edge) - grid.along(levels[k], -1, edge))
        slope_y = 0.5 * (grid.across(levels[k], 1, highs[k]) - grid.across(levels[k], -1, lows[k]))
        for which, slope in ((FLUX_X, slope_x), (FLUX_Y, slope_y)):
            x = now(which, k)
            edge = flat_edge(grid, lambda q: now(which, q), k)
            laplace = grid.along(x, 1, edge) + grid.along(x, -1, edge) - 4.0 * x
            laplace = laplace + grid.across(x, 1, hi.line(which, k)) + grid.across(x, -1, lo.line(which, k))
            new(which, k, wet * (x - OCEAN_RATE * deep * slope + VISCOUS * laplace))
    return levels


def press(grid, levels, fixed, line, pressure):
    for k in range(2):
        store(pressure, k, LOADING * fixed(WET, k) * levels[k])

    def load(y, t):
        k = 1 if t == WINDOW else 0
        return jnp.where(line(FLOOR, k, y) == grid.depth[t], row(pressure, k * ROWS + y), 0.0)

    return load


def edge_index(c, y):
    return OPEN.index((c, y)) * SPAN


def block_index(c, y):
    return (c * ROWS + y) * SPAN


def start_kernel(
    flags, main, flat, own, own_flat, even_in, odd_in,
    windows, flat_windows, partial, level, even_way, odd_way,
):
    grid = Grid()
    odd = (flags[0] & 1) == 1
    for f in range(0, FIELDS, 2):
        for q in range(0, ROWS, 2):
            places = [h * ROWS + y for y in (q, q + 1) for h in (f, f + 1)]
            items = [tile(own, p) for p in places]
            for p, x in zip(places, unpack(grid, items, odd, even_in, odd_in, (f * ROWS // 2 + q) // 2)):
                store(windows, p, x)
    items = [tile(own_flat, k) for k in range(6)]
    base = FIELDS * ROWS // 4
    for k, x in enumerate(unpack(grid, items[:4], odd, even_in, odd_in, base)):
        store(flat_windows, k, x)
    for k, x in enumerate(unpack(grid, items[4:] * 2, odd, even_in, odd_in, base + 1)[:2]):
        store(flat_windows, 4 + k, x)

    field = fields_of(main, windows)
    speeds(
        grid, [inside(field(f)) for f in range(SXX, SYZ + 1)], field, field(BUOY), OPEN,
        lambda c, y, t, value: store(partial, edge_index(c, y) + t, value),
    )
    flats = (flat, flat_windows)
    partial_level(grid, lambda f, k: tile(flats[k], f), lambda k, value: store(level, k, value))

    def rows_of(f):
        return (lambda y, t: tile(partial, edge_index(f, y) + t)) if f < 3 else field(f)

    def line(which, k, y):
        return row(level, k * ROWS + y) if which is None else row(flats[k], which * ROWS + y)

    send(True, (flags[1] & 1) == 1, rows_of, line, even_way, odd_way)


def start_rest_kernel(main, windows, speed_out, stress_out):
    grid = Grid()
    field = fields_of(main, windows)
    speeds(
        grid, [inside(field(f)) for f in range(SXX, SYZ + 1)], field, field(BUOY), CLOSED,
        lambda c, y, t, value: store(speed_out, block_index(c, y) + t, value),
    )
    stresses(
        grid, INNER, SPAN, lambda c: lambda y, t: tile(speed_out, block_index(c, y) + t), field,
        field(LAME), field(SHEAR),
        lambda f, y, t, value: store(stress_out, block_index(f - SXX, y) + t, value),
    )


def speed_reader(around, block):
    def speed(c):
        def read(y, t):
            if (c, y) in CLOSED:
                return tile(block, block_index(c, y) + t)
            return tile(around, (c * AROUND + y + 2) * SPAN + t)

        return read

    return speed


def middle_kernel(
    flags, main, windows, flat, flat_windows, partial, level, speed_in, stress_in, even_in, odd_in,
    speed_out, stress_out, ocean, partial_out, level_out, even_way, odd_way,
    sums, pressure,
):
    grid = Grid()
    odd = (flags[1] & 1) == 1
    lo, hi = received(True, odd, even_in, odd_in)
    field = fields_of(main, windows)
    finish(
        grid, SPAN, lambda c, y, t: tile(partial, edge_index(c, y) + t), field, field(BUOY), lo, hi, lo, hi, speed_out
    )
    speed = speed_reader(speed_out, speed_in)
    flats = (flat, flat_windows)
    fixed = lambda f, k: tile(flats[k], f)
    line = lambda f, k, y: row(flats[k], f * ROWS + y)

    def new(f, k, value):
        store(ocean, 3 * k + f, value)

    levels = sea(grid, speed, lambda k: tile(level, k), fixed, fixed, line, lo, hi, sums, new, False)
    load = press(grid, levels, fixed, line, pressure)

    def put(f, y, t, value):
        store(stress_out, block_index(f - SXX, y) + t, value - load(y, t) if f == SZZ else value)

    stresses(grid, OUTER, SPAN, speed, field, field(LAME), field(SHEAR), put)
    for f in range(SXX, SYZ + 1):
        for y in INNER:
            for t in range(SPAN):
                put(f, y, t, tile(stress_in, block_index(f - SXX, y) + t))
    stress = lambda f: lambda y, t: tile(stress_out, block_index(f - SXX, y) + t)
    speeds(
        grid, [inside(stress(f)) for f in range(SXX, SYZ + 1)], speed, field(BUOY), OPEN,
        lambda c, y, t, value: store(partial_out, edge_index(c, y) + t, value),
    )
    moving = lambda f, k: tile(flats[k], f) if f >= DEPTH else tile(ocean, 3 * k + f)
    partial_level(grid, moving, lambda k, value: store(level_out, k, value))

    def rows_of(f):
        return (lambda y, t: tile(partial_out, edge_index(f, y) + t)) if f < 3 else stress(f)

    def line_out(which, k, y):
        if which is None:
            return row(level_out, k * ROWS + y)
        return line(which, k, y) if which >= DEPTH else row(ocean, (3 * k + which) * ROWS + y)

    send(False, odd, rows_of, line_out, even_way, odd_way)


def middle_rest_kernel(main, windows, around, speed_in, stress_in, speed_out, stress_out):
    grid = Grid()
    field = fields_of(main, windows)
    stress = lambda f: lambda y, t: tile(stress_in, block_index(f - SXX, y) + t)
    speeds(
        grid, [inside(stress(f)) for f in range(SXX, SYZ + 1)], speed_reader(around, speed_in), field(BUOY), CLOSED,
        lambda c, y, t, value: store(speed_out, block_index(c, y) + t, value),
    )
    stresses(
        grid, INNER, TILES, lambda c: lambda y, t: tile(speed_out, block_index(c, y) + t), stress,
        field(LAME), field(SHEAR),
        lambda f, y, t, value: store(stress_out, block_index(f - SXX, y) + t, value),
    )


def last_kernel(
    flags, main, windows, flat, flat_windows, stress_in, ocean_in, partial, level, speed_in, inner_in,
    even_first, odd_first, even_in, odd_in,
    wave_hbm, ocean_out,
    sums, pressure, around, wave, sem,
):
    grid = Grid()
    odd = (flags[1] & 1) == 1
    lo, hi = received(False, odd, even_in, odd_in)
    lo_buoy, hi_buoy = received(True, odd, even_first, odd_first)
    field = fields_of(main, windows)
    stress = lambda f: lambda y, t: tile(stress_in, block_index(f - SXX, y) + t)
    finish(
        grid, TILES, lambda c, y, t: tile(partial, edge_index(c, y) + t), stress, field(BUOY),
        lo, hi, lo_buoy, hi_buoy, around,
    )
    speed = speed_reader(around, speed_in)
    size = wave.shape[0] // 9

    def put_out(f, y, t, value):
        wave[pl.ds(f * size + t * SUB * ROWS + y, SUB, stride=ROWS), :] = value

    def copy(f):
        part = slice(f * size, (f + 1) * size)
        return pltpu.make_async_copy(wave.at[part, :], wave_hbm.at[part, :], sem.at[f])

    for c in (VX, VY, VZ):
        for y in range(ROWS):
            for t in range(TILES):
                put_out(c, y, t, speed(c)(y, t))
        copy(c).start()
    flats = (flat, flat_windows)
    fixed = lambda f, k: tile(flats[k], f)

    def line(f, k, y):
        return row(flats[k], f * ROWS + y) if f >= DEPTH else row(ocean_in, (3 * k + f) * ROWS + y)

    def new(f, k, value):
        if k == 0:
            store(ocean_out, f, value)

    levels = sea(
        grid, speed, lambda k: tile(level, k), lambda f, k: tile(ocean_in, 3 * k + f), fixed, line, lo, hi, sums, new, True
    )
    load = press(grid, levels, fixed, line, pressure)

    def put(f, y, t, value):
        put_out(f, y, t, value - load(y, t) if f == SZZ else value)

    stresses(grid, OUTER, TILES, speed, stress, field(LAME), field(SHEAR), put)
    for f in range(SXX, SYZ + 1):
        for y in INNER:
            for t in range(TILES):
                put(f, y, t, tile(inner_in, block_index(f - SXX, y) + t))
        copy(f).start()
    for f in range(9):
        copy(f).wait()


IN_VMEM = pl.BlockSpec(memory_space=pltpu.VMEM)
IN_SMEM = pl.BlockSpec(memory_space=pltpu.SMEM)
IN_HBM = pl.BlockSpec(memory_space=pltpu.HBM)


def call(kernel, tiles, scratch, *arguments, flags=None, place=IN_VMEM, out_places=None, work=1):
    specs = [place] * len(arguments)
    if flags is not None:
        arguments, specs = (flags, *arguments), [IN_SMEM] + specs
    moved = sum(x.size for x in arguments) + sum(tiles) * SUB * LANES
    return pl.pallas_call(
        kernel,
        out_shape=[jax.ShapeDtypeStruct((n * SUB, LANES), jnp.float32) for n in tiles],
        in_specs=specs,
        out_specs=out_places or [IN_VMEM] * len(tiles),
        scratch_shapes=scratch,
        cost_estimate=pl.CostEstimate(flops=work * 1000000, bytes_accessed=4 * moved, transcendentals=0),
        compiler_params=pltpu.CompilerParams(vmem_limit_bytes=24 * 1024 * 1024),
    )(*arguments)


def planes(n):
    return pltpu.VMEM((n * SUB, LANES), jnp.float32)


def exchange(axis, even_way, odd_way):
    count = lax.axis_size(axis)

    def swap(x, start):
        pairs = [(i, i + 1) for i in range(start, count - 1, 2)]
        return lax.ppermute(x, axis, pairs + [(j, i) for i, j in pairs])

    return swap(even_way, 0), swap(odd_way, 1)


def local(*arguments):
    wave_fields, ocean_state = arguments[0], arguments[4]
    inputs = [pltpu.with_memory_space_constraint(x.reshape(-1, LANES), pltpu.HBM) for x in arguments]
    flags = jnp.stack([lax.axis_index("gx"), lax.axis_index("gy")])

    message = FIELDS * ROWS // 4 + 2
    main, flat, own, own_flat, even_way, odd_way = call(
        edges_kernel, [FIELDS * ROWS * TILES, 6, FIELDS * ROWS, 6, message, message],
        [pltpu.VMEM(x.shape, x.dtype) for x in inputs] + [pltpu.SemaphoreType.DMA((16,))],
        *inputs, flags=flags, place=IN_HBM,
    )
    x_in = exchange("gx", even_way, odd_way)
    first, later = [message_size(which) // SUB for which in (True, False)]
    edges, block = len(OPEN) * SPAN, ROWS * SPAN
    windows, flat_windows, partial, level, even_way, odd_way = call(
        start_kernel, [FIELDS * ROWS, 6, edges, 2, first, first], [],
        main, flat, own, own_flat, *x_in, flags=flags,
    )
    y_in = exchange("gy", even_way, odd_way)
    speed, inner = call(start_rest_kernel, [3 * block, 6 * block], [], main, windows, work=4)
    around, stress, ocean, partial, level, even_way, odd_way = call(
        middle_kernel, [3 * AROUND * SPAN, 6 * block, 6, edges, 2, later, later], [planes(4), planes(2)],
        main, windows, flat, flat_windows, partial, level, speed, inner, *y_in, flags=flags,
    )
    y_in2 = exchange("gy", even_way, odd_way)
    speed, inner = call(
        middle_rest_kernel, [3 * block, 6 * block], [], main, windows, around, speed, stress, work=4
    )
    wave_out, ocean_out = call(
        last_kernel, [9 * ROWS * TILES, 3],
        [planes(4), planes(2), planes(3 * AROUND * SPAN), planes(9 * ROWS * TILES), pltpu.SemaphoreType.DMA((9,))],
        main, windows, flat, flat_windows, stress, ocean, partial, level, speed, inner, *y_in, *y_in2,
        flags=flags, out_places=[IN_HBM, IN_VMEM],
    )
    return wave_out.reshape(wave_fields.shape), ocean_out.reshape(ocean_state.shape)


def solution(mesh):
    in_specs = (
        P(None, None, "gy", "gx"),
        P(None, "gy", "gx"),
        P(None, "gy", "gx"),
        P(None, "gy", "gx"),
        P(None, "gy", "gx"),
        P("gy", "gx"),
        P("gy", "gx"),
        P("gy", "gx"),
    )
    out_specs = (P(None, None, "gy", "gx"), P(None, "gy", "gx"))
    return jax.shard_map(local, mesh=mesh, in_specs=in_specs, out_specs=out_specs, check_vma=False)
```

```python
import jax
import jax.numpy as jnp
from jax import lax
from jax.experimental import pallas as pl
from jax.experimental.pallas import tpu as pltpu
from jax.sharding import PartitionSpec as P

RATE = 0.3 / 24.0
OCEAN_RATE = 0.3
UPLIFT = 0.5
LOADING = 0.5
VISCOUS = 0.1

ROWS = 8
SUB = 8
LANES = 128
EDGE = 8
GROUP = 2 * EDGE
TILES = 4
HALF = TILES * GROUP
SPAN = TILES + 1
WINDOW = TILES

LEVEL, FLUX_X, FLUX_Y, DEPTH, FLOOR, WET = range(6)
VX, VY, VZ, SXX, SYY, SZZ, SXY, SXZ, SYZ, LAME, SHEAR, BUOY = range(12)
FIELDS = 12

OPEN = ((VX, 0), (VX, 1), (VX, 7), (VY, 0), (VY, 6), (VY, 7), (VZ, 0), (VZ, 1), (VZ, 7))
CLOSED = tuple((c, y) for y in range(ROWS) for c in (VX, VY, VZ) if (c, y) not in OPEN)
INNER = (3, 4)
OUTER = tuple(y for y in range(ROWS) if y not in INNER)

SPEED_HIGH = ((VX, 7), (VY, 6), (VY, 7), (VZ, 7))
SPEED_LOW = ((VX, 0), (VX, 1), (VY, 0), (VZ, 0), (VZ, 1))
STRESS_HIGH = ((SXY, 6), (SXY, 7), (SYY, 7), (SYZ, 6), (SYZ, 7))
STRESS_LOW = ((SXY, 0), (SYY, 0), (SYY, 1), (SYZ, 0))
BUOY_HIGH = ((BUOY, 6), (BUOY, 7))
BUOY_LOW = ((BUOY, 0), (BUOY, 1))
LINES = (None, WET, FLOOR, FLUX_X, FLUX_Y)


def rolled(x, shift, axis):
    shift %= x.shape[axis]
    return x if shift == 0 else pltpu.roll(x, shift, axis)


def tile(ref, index, start=None):
    if start is None:
        return ref[index * SUB : (index + 1) * SUB, :]
    return ref[pl.ds(start + index * SUB, SUB), :]


def row(ref, index):
    return ref[index : index + 1, :]


def store(ref, index, value):
    ref[index * SUB : (index + 1) * SUB, :] = value


def split(x, parts):
    out = []
    for part in range(parts):
        out.append(x.astype(jnp.bfloat16))
        if part + 1 < parts:
            x = x - out[-1].astype(jnp.float32)
    return jnp.concatenate(out, axis=1)


def minus(a, b):
    if b is None:
        return a
    return -b if a is None else a - b


def near_far(a, b, c, d):
    near, far = 27.0 * minus(a, b), minus(c, d)
    return near if c is None and d is None else near - far


class Grid:
    def __init__(self, origin=None, before=None, after=None):
        self.origin, self.before, self.after = origin, before, after
        self.sub = lax.broadcasted_iota(jnp.int32, (SUB, LANES), 0)
        self.lane = lax.broadcasted_iota(jnp.int32, (SUB, LANES), 1)
        self.first = self.lane % GROUP < EDGE
        self.left = self.lane < HALF
        self.group = self.lane // GROUP
        self.zero = jnp.zeros((SUB, LANES), jnp.float32)
        depth = [self.sub + SUB * t for t in range(TILES)] + [self.sub + SUB * (self.group % TILES)]
        self.depth = [d.astype(jnp.float32) for d in depth]

    def beside(self, window):
        return jnp.where(self.first, window, rolled(window, HALF, 1))

    def edge(self, beside, t):
        return None if t == WINDOW else rolled(beside, LANES - EDGE - GROUP * t, 1)

    def along(self, x, offset, edge):
        if edge is not None:
            lane = self.lane
            keep = {-1: lane == LANES - 1, -2: lane >= LANES - 2, 1: lane == 0, 2: lane <= 1}[offset]
            x = jnp.where(keep, edge, x)
        return rolled(x, -offset, 1)

    def down(self, field, y, t, offset):
        if t < WINDOW:
            x = field(y, t, self.origin + offset)
            if t == 0 and offset < 0:
                return jnp.where(self.sub >= -offset, x, 0.0)
            if t == TILES - 1 and offset > 0:
                return jnp.where(self.sub < SUB - offset, x, 0.0)
            return x
        x, at = field(y, t), self.lane % HALF
        if offset < 0:
            beyond, far = jnp.where(at >= GROUP, rolled(x, GROUP, 1), 0.0), self.sub >= SUB + offset
        else:
            beyond, far = jnp.where(at < HALF - GROUP, rolled(x, -GROUP, 1), 0.0), self.sub < offset
        return rolled(jnp.where(far, beyond, x), -offset, 0)

    def fz(self, field, y, t):
        down = lambda offset: self.down(field, y, t, offset)
        return near_far(down(1), field(y, t), down(2), down(-1))

    def bz(self, field, y, t):
        down = lambda offset: self.down(field, y, t, offset)
        return near_far(field(y, t), down(-1), down(1), down(-2))

    def along_rows(self, matrix, rows):
        main = split(jnp.concatenate([f(y, t) for f, y in rows for t in range(TILES)], axis=0), 2)
        sides = [f(y, WINDOW) for f, y in rows]
        side = split(jnp.concatenate(sides + sides[: len(sides) % 2], axis=0), 2)
        main = jnp.dot(main, matrix[:, :LANES], preferred_element_type=jnp.float32)
        side = jnp.dot(side, matrix[...], preferred_element_type=jnp.float32)
        out = []
        for i in range(len(rows)):
            part = side[i * SUB : (i + 1) * SUB, :]
            parts = [part[:, t * LANES : (t + 1) * LANES] for t in range(SPAN)]
            tiles = [
                main[(i * TILES + t) * SUB : (i * TILES + t + 1) * SUB, :] + parts[1 + t] for t in range(TILES)
            ]
            out.append(tiles + parts[:1])
        return out

    def fy(self, field, y, t):
        return near_far(field(y + 1, t), field(y, t), field(y + 2, t), field(y - 1, t))

    def by(self, field, y, t):
        return near_far(field(y, t), field(y - 1, t), field(y + 1, t), field(y - 2, t))

    def windows(self, own, from_left, from_right):
        return jnp.where(
            self.left, jnp.where(self.first, from_left, own), jnp.where(self.first, own, from_right)
        )

    def every_group(self, x):
        for shift in (GROUP, 2 * GROUP):
            x = x + jnp.where(self.lane % HALF >= shift, rolled(x, shift, 1), rolled(x, shift - HALF, 1))
        return x

    def across(self, x, offset, beside):
        end = 0 if offset < 0 else ROWS - 1
        return jnp.where(self.sub == end, beside, rolled(x, -offset, 0))


def inside(field):
    return lambda y, t, *start: field(y, t, *start) if 0 <= y < ROWS else None


def fields_of(main, windows):
    def field(f):
        def read(y, t, *start):
            return tile(windows, f * ROWS + y) if t == WINDOW else tile(main, (f * ROWS + y) * TILES + t, *start)

        return read

    return field


def pack(grid, items, odd, even_way, odd_way, index):
    a, b, c, d = items
    first, left = grid.first, grid.left
    right_way = jnp.where(
        left, jnp.where(first, a, rolled(b, EDGE, 1)), jnp.where(first, c, rolled(d, EDGE, 1))
    )
    left_way = jnp.where(
        left, jnp.where(first, rolled(b, -EDGE, 1), a), jnp.where(first, rolled(d, -EDGE, 1), c)
    )
    store(even_way, index, jnp.where(odd, left_way, right_way))
    store(odd_way, index, jnp.where(odd, right_way, left_way))


def unpack(grid, items, odd, even_in, odd_in, index):
    x, y = tile(even_in, index), tile(odd_in, index)
    before, after = jnp.where(odd, x, y), jnp.where(odd, y, x)
    befores = [before, rolled(before, -EDGE, 1), rolled(before, HALF, 1), rolled(before, HALF - EDGE, 1)]
    afters = [rolled(after, HALF, 1), rolled(after, HALF + EDGE, 1), after, rolled(after, EDGE, 1)]
    return [grid.windows(*three) for three in zip(items, befores, afters)]


def difference_matrix(out, weights, offsets):
    shape = (LANES, LANES)
    k, n = [lax.broadcasted_iota(jnp.int32, shape, axis) for axis in range(2)]

    def weight(apart):
        total = jnp.zeros(shape, jnp.float32)
        for w, offset in zip(weights, offsets):
            total = jnp.where(apart == offset, w, total)
        return total

    inner, left = k % GROUP, k < HALF
    column = jnp.where(left, inner - EDGE, LANES - EDGE + inner)
    outside = (left & (inner < EDGE)) | (jnp.logical_not(left) & (inner >= EDGE))
    beside = jnp.where(outside, weight(n - column), 0.0)
    parts = [weight(n - k)]
    parts += [jnp.where(k % HALF // GROUP == t, beside, 0.0) for t in range(TILES)]
    for p, x in enumerate(parts):
        for half in range(2):
            out[half * LANES : (half + 1) * LANES, p * LANES : (p + 1) * LANES] = x.astype(jnp.bfloat16)


def picker(t):
    k, n = [lax.broadcasted_iota(jnp.int32, (LANES, LANES), axis) for axis in range(2)]
    column = (n % GROUP - EDGE) % LANES
    one = jnp.where((n % HALF // GROUP == t) & (k == column), 1.0, 0.0).astype(jnp.bfloat16)
    return jnp.concatenate([one] * 3, axis=0)


def edges_kernel(flags, *refs):
    hbm, refs = refs[:8], refs[8:]
    (before, after, main, flat, own, own_flat, even_way, odd_way), refs = refs[:8], refs[8:]
    (wave, lame, shear, buoy, ocean, deep, floor, wet), sem = refs[:8], refs[8]
    size = wave.shape[0] // 9
    copies = []
    for f in range(9):
        part = slice(f * size, (f + 1) * size)
        copies.append(pltpu.make_async_copy(hbm[0].at[part, :], wave.at[part, :], sem.at[f]))
    for k, target in enumerate((lame, shear, buoy, ocean, deep, floor, wet)):
        copies.append(pltpu.make_async_copy(hbm[1 + k], target, sem.at[9 + k]))
    for copy in copies:
        copy.start()
    difference_matrix(before, (27.0, -27.0, -1.0, 1.0), (0, 1, -1, 2))
    difference_matrix(after, (27.0, -27.0, -1.0, 1.0), (-1, 0, -2, 1))
    pickers = [picker(t) for t in range(TILES)]
    grid = Grid()
    odd = (flags[0] & 1) == 1
    sources = [(wave, f) for f in range(9)] + [(lame, 0), (shear, 0), (buoy, 0)]
    for f in range(0, FIELDS, 2):
        copies[f].wait()
        copies[f + 1].wait()
        totals = []
        for h in (f, f + 1):
            ref, base = sources[h]
            total = None
            for t in range(TILES):
                tiles = []
                for y in range(ROWS):
                    x = ref[pl.ds(base * size + t * SUB * ROWS + y, SUB, stride=ROWS), :]
                    store(main, (h * ROWS + y) * TILES + t, x)
                    tiles.append(x)
                part = split(jnp.concatenate(tiles, axis=0), 3)
                part = jnp.dot(part, pickers[t], preferred_element_type=jnp.float32)
                total = part if total is None else total + part
            own[h * ROWS * SUB : (h + 1) * ROWS * SUB, :] = total
            totals.append(total)
        for q in range(0, ROWS, 2):
            items = [total[y * SUB : (y + 1) * SUB, :] for y in (q, q + 1) for total in totals]
            pack(grid, items, odd, even_way, odd_way, (f * ROWS // 2 + q) // 2)
    for copy in copies[FIELDS:]:
        copy.wait()
    planes = [tile(ocean, k) for k in range(3)] + [deep[...]]
    planes += [floor[...].astype(jnp.float32), wet[...].astype(jnp.float32)]
    items = []
    for k, x in enumerate(planes):
        store(flat, k, x)
        out = grid.zero
        for g in range(LANES // GROUP):
            out = jnp.where(grid.group == g, rolled(x, EDGE + GROUP * g, 1), out)
        store(own_flat, k, out)
        items.append(out)
    pack(grid, items[:4], odd, even_way, odd_way, FIELDS * ROWS // 4)
    pack(grid, items[4:] * 2, odd, even_way, odd_way, FIELDS * ROWS // 4 + 1)


def speeds(grid, stress, speed, buoy, todo, put):
    sxx, syy, szz, sxy, sxz, syz = stress
    forth = [(VX, y) for c, y in todo if c == VX]
    back = [(c, y) for c, y in todo if c != VX]
    change = dict(zip(forth, grid.along_rows(grid.after, [(sxx, y) for _, y in forth])))
    change.update(zip(back, grid.along_rows(grid.before, [(sxy if c == VY else sxz, y) for c, y in back])))
    for y in range(ROWS):
        parts = [c for c in (VX, VY, VZ) if (c, y) in todo]
        if not parts:
            continue
        for t in range(SPAN):
            rate = RATE * buoy(y, t)
            for c in parts:
                a = change[c, y][t]
                if c == VX:
                    a = a + grid.by(sxy, y, t) + grid.bz(sxz, y, t)
                elif c == VY:
                    a = a + grid.fy(syy, y, t) + grid.bz(syz, y, t)
                else:
                    a = a + grid.by(syz, y, t) + grid.fz(szz, y, t)
                put(c, y, t, speed(c)(y, t) + rate * a)


def stresses(grid, rows, tiles, speed, stress, lame, shear, put):
    vx, vy, vz = [speed(c) for c in (VX, VY, VZ)]
    back = grid.along_rows(grid.before, [(vx, y) for y in rows])
    forth = grid.along_rows(grid.after, [(v, y) for v in (vy, vz) for y in rows])
    for i, y in enumerate(rows):
        for t in range(tiles):
            strain_x = back[i][t]
            strain_y = grid.by(vy, y, t)
            strain_z = grid.bz(vz, y, t)
            mu = RATE * shear(y, t)
            spread = (RATE * lame(y, t)) * (strain_x + strain_y + strain_z)
            two = mu + mu
            put(SXX, y, t, stress(SXX)(y, t) + (spread + two * strain_x))
            put(SYY, y, t, stress(SYY)(y, t) + (spread + two * strain_y))
            put(SZZ, y, t, stress(SZZ)(y, t) + (spread + two * strain_z))
            put(SXY, y, t, stress(SXY)(y, t) + mu * (grid.fy(vx, y, t) + forth[i][t]))
            put(SXZ, y, t, stress(SXZ)(y, t) + mu * (grid.fz(vx, y, t) + forth[len(rows) + i][t]))
            put(SYZ, y, t, stress(SYZ)(y, t) + mu * (grid.fz(vy, y, t) + grid.fy(vz, y, t)))


def flat_edge(grid, at, k):
    return grid.edge(grid.beside(at(1)), 0) if k == 0 else None


def partial_level(grid, flat, put):
    for k in range(2):
        x, y = flat(FLUX_X, k), flat(FLUX_Y, k)
        edge = flat_edge(grid, lambda q: flat(FLUX_X, q), k)
        spread = 0.5 * (grid.along(x, 1, edge) - grid.along(x, -1, edge))
        spread = spread + 0.5 * (grid.across(y, 1, 0.0) - grid.across(y, -1, 0.0))
        put(k, flat(LEVEL, k) - OCEAN_RATE * (flat(WET, k) * spread))


class Message:
    def __init__(self, rows, thin):
        self.at, size = [], 0
        for f, _ in rows:
            self.at.append(size)
            size += TILES if thin and f < 3 else SPAN
        self.tiles = self.at[1:] + [size]
        self.tiles = [b - a for a, b in zip(self.at, self.tiles)]
        self.rows = rows
        self.base = size * SUB
        self.size = self.base + 2 * SUB


def messages(first):
    high = SPEED_HIGH + STRESS_HIGH + (BUOY_HIGH if first else ())
    low = SPEED_LOW + STRESS_LOW + (BUOY_LOW if first else ())
    return Message(high, not first), Message(low, not first)


def message_size(first):
    return max(m.size for m in messages(first))


def send(first, odd, field, line, even_way, odd_way):
    high, low = messages(first)

    def fill(message, edge, out):
        for (f, y), at, tiles in zip(message.rows, message.at, message.tiles):
            for t in range(tiles):
                store(out, at + t, field(f)(y, t))
        at = message.base
        for which in LINES:
            for k in range(2):
                out[at : at + 1, :] = line(which, k, edge)
                at += 1
        out[at : at + 6, :] = jnp.zeros((6, LANES), jnp.float32)
        tail = out.shape[0]
        if message.size < tail:
            out[message.size : tail, :] = jnp.zeros((tail - message.size, LANES), jnp.float32)

    @pl.when(odd)
    def _():
        fill(high, ROWS - 1, odd_way)
        fill(low, 0, even_way)

    @pl.when(jnp.logical_not(odd))
    def _():
        fill(high, ROWS - 1, even_way)
        fill(low, 0, odd_way)


class Received:
    def __init__(self, message, odd, if_odd, if_even):
        self.message, self.odd, self.refs = message, odd, (if_odd, if_even)

    def pick(self, take):
        return jnp.where(self.odd, take(self.refs[0]), take(self.refs[1]))

    def __call__(self, index, t):
        return self.pick(lambda ref: tile(ref, self.message.at[index] + t))

    def line(self, which, k):
        at = self.message.base + 2 * LINES.index(which) + k
        return self.pick(lambda ref: row(ref, at))


def received(first, odd, even_in, odd_in):
    high, low = messages(first)
    return Received(high, odd, even_in, odd_in), Received(low, odd, odd_in, even_in)


AROUND = ROWS + 4


def finish(grid, tiles, partial, stress, buoy, lo, hi, lo_buoy, hi_buoy, speed):
    sxy, syy, syz = [stress(f) for f in (SXY, SYY, SYZ)]

    def put(c, y, t, value):
        store(speed, (c * AROUND + y + 2) * SPAN + t, value)

    for t in range(SPAN):
        sends = {"xy": (4, 5), "yz": (7, 8)}
        for c, key, at in ((VX, "xy", 5), (VZ, "yz", 8)):
            two, one = lo(sends[key][0], t), lo(sends[key][1], t)
            rate = [RATE * buoy(y, t) for y in (0, 1, 7)]
            put(c, 0, t, partial(c, 0, t) + rate[0] * (two - 27.0 * one))
            put(c, 1, t, partial(c, 1, t) + rate[1] * one)
            put(c, 7, t, partial(c, 7, t) - rate[2] * hi(at, t))
        h8, h9 = hi(6, t), hi(7, t)
        put(VY, 0, t, partial(VY, 0, t) + (RATE * buoy(0, t)) * lo(6, t))
        put(VY, 6, t, partial(VY, 6, t) - (RATE * buoy(6, t)) * h8)
        put(VY, 7, t, partial(VY, 7, t) + (RATE * buoy(7, t)) * (27.0 * h8 - h9))
    for t in range(tiles):
        b2, b1 = RATE * lo_buoy(9, t), RATE * lo_buoy(10, t)
        b8, b9 = RATE * hi_buoy(9, t), RATE * hi_buoy(10, t)
        put(VX, -1, t, lo(0, t) - b1 * sxy(0, t))
        put(VY, -2, t, lo(1, t) - b2 * syy(0, t))
        put(VY, -1, t, lo(2, t) + b1 * (27.0 * syy(0, t) - syy(1, t)))
        put(VZ, -1, t, lo(3, t) - b1 * syz(0, t))
        put(VX, 8, t, hi(0, t) + b8 * (sxy(6, t) - 27.0 * sxy(7, t)))
        put(VX, 9, t, hi(1, t) + b9 * sxy(7, t))
        put(VY, 8, t, hi(2, t) + b8 * syy(7, t))
        put(VZ, 8, t, hi(3, t) + b8 * (syz(6, t) - 27.0 * syz(7, t)))
        put(VZ, 9, t, hi(4, t) + b9 * syz(7, t))


def seafloor(grid, vz, y, floors, out, index):
    total = None
    for t in range(TILES):
        part = jnp.where(floors[0] == grid.depth[t], vz(y, t), 0.0)
        total = part if total is None else total + part
    out[index : index + 1, :] = jnp.sum(total, axis=0, keepdims=True)
    if len(floors) > 1:
        part = jnp.where(floors[1] == grid.depth[WINDOW], vz(y, WINDOW), 0.0)
        out[2 * SUB + index : 2 * SUB + index + 1, :] = jnp.sum(part, axis=0, keepdims=True)


def sea(grid, speed, level, now, fixed, line, lo, hi, sums, new, last):
    vz = speed(VZ)
    for y in range(ROWS):
        seafloor(grid, vz, y, [line(FLOOR, k, y) for k in range(2)], sums, y)
    ends = 1 if last else 2
    for y, side, at in ((-1, lo, ROWS), (ROWS, hi, ROWS + 1)):
        seafloor(grid, vz, y, [side.line(FLOOR, k) for k in range(ends)], sums, at)
    floors, beyond = [tile(sums, 0), grid.every_group(tile(sums, 2))], [tile(sums, 1), None]
    if not last:
        beyond[1] = grid.every_group(tile(sums, 3))
    sub = grid.sub
    levels, lows, highs = [], [], []
    for k in range(2):
        near = jnp.where(sub == 0, lo.line(FLUX_Y, k), jnp.where(sub == ROWS - 1, -hi.line(FLUX_Y, k), 0.0))
        levels.append(level(k) + fixed(WET, k) * (UPLIFT * floors[k] + (0.5 * OCEAN_RATE) * near))
        new(LEVEL, k, levels[k])
        if k < ends:
            for side, at, y, sign, out in ((lo, 0, 0, -1.0, lows), (hi, 1, ROWS - 1, 1.0, highs)):
                mine = (sign * 0.5 * OCEAN_RATE) * line(FLUX_Y, k, y)
                rest = UPLIFT * beyond[k][at : at + 1, :] + mine
                out.append(side.line(None, k) + side.line(WET, k) * rest)
    for k in range(ends):
        wet, deep = fixed(WET, k), fixed(DEPTH, k)
        edge = flat_edge(grid, lambda q: levels[q], k)
        slope_x = 0.5 * (grid.along(levels[k], 1, edge) - grid.along(levels[k], -1, edge))
        slope_y = 0.5 * (grid.across(levels[k], 1, highs[k]) - grid.across(levels[k], -1, lows[k]))
        for which, slope in ((FLUX_X, slope_x), (FLUX_Y, slope_y)):
            x = now(which, k)
            edge = flat_edge(grid, lambda q: now(which, q), k)
            laplace = grid.along(x, 1, edge) + grid.along(x, -1, edge) - 4.0 * x
            laplace = laplace + grid.across(x, 1, hi.line(which, k)) + grid.across(x, -1, lo.line(which, k))
            new(which, k, wet * (x - OCEAN_RATE * deep * slope + VISCOUS * laplace))
    return levels


def press(grid, levels, fixed, line, pressure):
    for k in range(2):
        store(pressure, k, LOADING * fixed(WET, k) * levels[k])

    def load(y, t):
        k = 1 if t == WINDOW else 0
        return jnp.where(line(FLOOR, k, y) == grid.depth[t], row(pressure, k * ROWS + y), 0.0)

    return load


def edge_index(c, y):
    return OPEN.index((c, y)) * SPAN


def block_index(c, y):
    return (c * ROWS + y) * SPAN


def start_kernel(
    flags, before, after, main, flat, own, own_flat, even_in, odd_in,
    windows, flat_windows, partial, level, even_way, odd_way,
):
    grid = Grid(flags[2], before, after)
    odd = (flags[0] & 1) == 1
    for f in range(0, FIELDS, 2):
        for q in range(0, ROWS, 2):
            places = [h * ROWS + y for y in (q, q + 1) for h in (f, f + 1)]
            items = [tile(own, p) for p in places]
            for p, x in zip(places, unpack(grid, items, odd, even_in, odd_in, (f * ROWS // 2 + q) // 2)):
                store(windows, p, x)
    items = [tile(own_flat, k) for k in range(6)]
    base = FIELDS * ROWS // 4
    for k, x in enumerate(unpack(grid, items[:4], odd, even_in, odd_in, base)):
        store(flat_windows, k, x)
    for k, x in enumerate(unpack(grid, items[4:] * 2, odd, even_in, odd_in, base + 1)[:2]):
        store(flat_windows, 4 + k, x)

    field = fields_of(main, windows)
    speeds(
        grid, [inside(field(f)) for f in range(SXX, SYZ + 1)], field, field(BUOY), OPEN,
        lambda c, y, t, value: store(partial, edge_index(c, y) + t, value),
    )
    flats = (flat, flat_windows)
    partial_level(grid, lambda f, k: tile(flats[k], f), lambda k, value: store(level, k, value))

    def rows_of(f):
        return (lambda y, t: tile(partial, edge_index(f, y) + t)) if f < 3 else field(f)

    def line(which, k, y):
        return row(level, k * ROWS + y) if which is None else row(flats[k], which * ROWS + y)

    send(True, (flags[1] & 1) == 1, rows_of, line, even_way, odd_way)


def start_rest_kernel(flags, before, after, main, windows, speed_out, stress_out):
    grid = Grid(flags[2], before, after)
    field = fields_of(main, windows)
    speeds(
        grid, [inside(field(f)) for f in range(SXX, SYZ + 1)], field, field(BUOY), CLOSED,
        lambda c, y, t, value: store(speed_out, block_index(c, y) + t, value),
    )
    stresses(
        grid, INNER, SPAN, block_reader(speed_out, VX), field,
        field(LAME), field(SHEAR),
        lambda f, y, t, value: store(stress_out, block_index(f - SXX, y) + t, value),
    )


def block_reader(ref, least):
    return lambda f: lambda y, t, *start: tile(ref, block_index(f - least, y) + t, *start)


def speed_reader(around, block):
    def speed(c):
        def read(y, t, *start):
            if (c, y) in CLOSED:
                return tile(block, block_index(c, y) + t, *start)
            return tile(around, (c * AROUND + y + 2) * SPAN + t, *start)

        return read

    return speed


def middle_kernel(
    flags, before, after, main, windows, flat, flat_windows, partial, level, speed_in, stress_in, even_in, odd_in,
    speed_out, stress_out, ocean, partial_out, level_out, even_way, odd_way,
    sums, pressure,
):
    grid = Grid(flags[2], before, after)
    odd = (flags[1] & 1) == 1
    lo, hi = received(True, odd, even_in, odd_in)
    field = fields_of(main, windows)
    finish(
        grid, SPAN, lambda c, y, t: tile(partial, edge_index(c, y) + t), field, field(BUOY), lo, hi, lo, hi, speed_out
    )
    speed = speed_reader(speed_out, speed_in)
    flats = (flat, flat_windows)
    fixed = lambda f, k: tile(flats[k], f)
    line = lambda f, k, y: row(flats[k], f * ROWS + y)

    def new(f, k, value):
        store(ocean, 3 * k + f, value)

    levels = sea(grid, speed, lambda k: tile(level, k), fixed, fixed, line, lo, hi, sums, new, False)
    load = press(grid, levels, fixed, line, pressure)

    def put(f, y, t, value):
        store(stress_out, block_index(f - SXX, y) + t, value - load(y, t) if f == SZZ else value)

    stresses(grid, OUTER, SPAN, speed, field, field(LAME), field(SHEAR), put)
    for f in range(SXX, SYZ + 1):
        for y in INNER:
            for t in range(SPAN):
                put(f, y, t, tile(stress_in, block_index(f - SXX, y) + t))
    stress = block_reader(stress_out, SXX)
    speeds(
        grid, [inside(stress(f)) for f in range(SXX, SYZ + 1)], speed, field(BUOY), OPEN,
        lambda c, y, t, value: store(partial_out, edge_index(c, y) + t, value),
    )
    moving = lambda f, k: tile(flats[k], f) if f >= DEPTH else tile(ocean, 3 * k + f)
    partial_level(grid, moving, lambda k, value: store(level_out, k, value))

    def rows_of(f):
        return (lambda y, t: tile(partial_out, edge_index(f, y) + t)) if f < 3 else stress(f)

    def line_out(which, k, y):
        if which is None:
            return row(level_out, k * ROWS + y)
        return line(which, k, y) if which >= DEPTH else row(ocean, (3 * k + which) * ROWS + y)

    send(False, odd, rows_of, line_out, even_way, odd_way)


def middle_rest_kernel(flags, before, after, main, windows, around, speed_in, stress_in, speed_out, stress_out):
    grid = Grid(flags[2], before, after)
    field = fields_of(main, windows)
    stress = block_reader(stress_in, SXX)
    speeds(
        grid, [inside(stress(f)) for f in range(SXX, SYZ + 1)], speed_reader(around, speed_in), field(BUOY), CLOSED,
        lambda c, y, t, value: store(speed_out, block_index(c, y) + t, value),
    )
    stresses(
        grid, INNER, TILES, block_reader(speed_out, VX), stress,
        field(LAME), field(SHEAR),
        lambda f, y, t, value: store(stress_out, block_index(f - SXX, y) + t, value),
    )


def last_kernel(
    flags, before, after, main, windows, flat, flat_windows, stress_in, ocean_in, partial, level, speed_in, inner_in,
    even_first, odd_first, even_in, odd_in,
    wave_hbm, ocean_out,
    sums, pressure, around, wave, sem,
):
    grid = Grid(flags[2], before, after)
    odd = (flags[1] & 1) == 1
    lo, hi = received(False, odd, even_in, odd_in)
    lo_buoy, hi_buoy = received(True, odd, even_first, odd_first)
    field = fields_of(main, windows)
    stress = block_reader(stress_in, SXX)
    finish(
        grid, TILES, lambda c, y, t: tile(partial, edge_index(c, y) + t), stress, field(BUOY),
        lo, hi, lo_buoy, hi_buoy, around,
    )
    speed = speed_reader(around, speed_in)
    size = wave.shape[0] // 9

    def put_out(f, y, t, value):
        wave[pl.ds(f * size + t * SUB * ROWS + y, SUB, stride=ROWS), :] = value

    def copy(f):
        part = slice(f * size, (f + 1) * size)
        return pltpu.make_async_copy(wave.at[part, :], wave_hbm.at[part, :], sem.at[f])

    for c in (VX, VY, VZ):
        for y in range(ROWS):
            for t in range(TILES):
                put_out(c, y, t, speed(c)(y, t))
        copy(c).start()
    flats = (flat, flat_windows)
    fixed = lambda f, k: tile(flats[k], f)

    def line(f, k, y):
        return row(flats[k], f * ROWS + y) if f >= DEPTH else row(ocean_in, (3 * k + f) * ROWS + y)

    def new(f, k, value):
        if k == 0:
            store(ocean_out, f, value)

    levels = sea(
        grid, speed, lambda k: tile(level, k), lambda f, k: tile(ocean_in, 3 * k + f), fixed, line, lo, hi, sums, new, True
    )
    load = press(grid, levels, fixed, line, pressure)

    def put(f, y, t, value):
        put_out(f, y, t, value - load(y, t) if f == SZZ else value)

    stresses(grid, OUTER, TILES, speed, stress, field(LAME), field(SHEAR), put)
    for f in range(SXX, SYZ + 1):
        for y in INNER:
            for t in range(TILES):
                put(f, y, t, tile(inner_in, block_index(f - SXX, y) + t))
        copy(f).start()
    for f in range(9):
        copy(f).wait()


IN_VMEM = pl.BlockSpec(memory_space=pltpu.VMEM)
IN_SMEM = pl.BlockSpec(memory_space=pltpu.SMEM)
IN_HBM = pl.BlockSpec(memory_space=pltpu.HBM)


def call(kernel, tiles, scratch, *arguments, flags=None, place=IN_VMEM, out_places=None, work=1):
    specs = [place] * len(arguments)
    if flags is not None:
        arguments, specs = (flags, *arguments), [IN_SMEM] + specs
    moved = sum(x.size for x in arguments) + sum(n for n in tiles if isinstance(n, int)) * SUB * LANES
    return pl.pallas_call(
        kernel,
        out_shape=[n if hasattr(n, "dtype") else jax.ShapeDtypeStruct((n * SUB, LANES), jnp.float32) for n in tiles],
        in_specs=specs,
        out_specs=out_places or [IN_VMEM] * len(tiles),
        scratch_shapes=scratch,
        cost_estimate=pl.CostEstimate(flops=work * 1000000, bytes_accessed=4 * moved, transcendentals=0),
        compiler_params=pltpu.CompilerParams(vmem_limit_bytes=24 * 1024 * 1024),
    )(*arguments)


def planes(n):
    return pltpu.VMEM((n * SUB, LANES), jnp.float32)


def exchange(axis, even_way, odd_way):
    count = lax.axis_size(axis)

    def swap(x, start):
        pairs = [(i, i + 1) for i in range(start, count - 1, 2)]
        return lax.ppermute(x, axis, pairs + [(j, i) for i, j in pairs])

    return swap(even_way, 0), swap(odd_way, 1)


def local(*arguments):
    wave_fields, ocean_state = arguments[0], arguments[4]
    inputs = [pltpu.with_memory_space_constraint(x.reshape(-1, LANES), pltpu.HBM) for x in arguments]
    flags = jnp.stack([lax.axis_index("gx"), lax.axis_index("gy"), 0])
    matrix = jax.ShapeDtypeStruct((2 * LANES, SPAN * LANES), jnp.bfloat16)

    message = FIELDS * ROWS // 4 + 2
    before, after, main, flat, own, own_flat, even_way, odd_way = call(
        edges_kernel, [matrix, matrix, FIELDS * ROWS * TILES, 6, FIELDS * ROWS, 6, message, message],
        [pltpu.VMEM(x.shape, x.dtype) for x in inputs] + [pltpu.SemaphoreType.DMA((16,))],
        *inputs, flags=flags, place=IN_HBM,
    )
    x_in = exchange("gx", even_way, odd_way)
    first, later = [message_size(which) // SUB for which in (True, False)]
    edges, block = len(OPEN) * SPAN, ROWS * SPAN
    windows, flat_windows, partial, level, even_way, odd_way = call(
        start_kernel, [FIELDS * ROWS, 6, edges, 2, first, first], [],
        before, after, main, flat, own, own_flat, *x_in, flags=flags,
    )
    y_in = exchange("gy", even_way, odd_way)
    speed, inner = call(start_rest_kernel, [3 * block, 6 * block], [], before, after, main, windows, flags=flags, work=4)
    around, stress, ocean, partial, level, even_way, odd_way = call(
        middle_kernel, [3 * AROUND * SPAN, 6 * block, 6, edges, 2, later, later], [planes(4), planes(2)],
        before, after, main, windows, flat, flat_windows, partial, level, speed, inner, *y_in, flags=flags,
    )
    y_in2 = exchange("gy", even_way, odd_way)
    speed, inner = call(
        middle_rest_kernel, [3 * block, 6 * block], [], before, after, main, windows, around, speed, stress, flags=flags, work=4
    )
    wave_out, ocean_out = call(
        last_kernel, [9 * ROWS * TILES, 3],
        [planes(4), planes(2), planes(3 * AROUND * SPAN), planes(9 * ROWS * TILES), pltpu.SemaphoreType.DMA((9,))],
        before, after, main, windows, flat, flat_windows, stress, ocean, partial, level, speed, inner, *y_in, *y_in2,
        flags=flags, out_places=[IN_HBM, IN_VMEM],
    )
    return wave_out.reshape(wave_fields.shape), ocean_out.reshape(ocean_state.shape)


def solution(mesh):
    in_specs = (
        P(None, None, "gy", "gx"),
        P(None, "gy", "gx"),
        P(None, "gy", "gx"),
        P(None, "gy", "gx"),
        P(None, "gy", "gx"),
        P("gy", "gx"),
        P("gy", "gx"),
        P("gy", "gx"),
    )
    out_specs = (P(None, None, "gy", "gx"), P(None, "gy", "gx"))
    return jax.shard_map(local, mesh=mesh, in_specs=in_specs, out_specs=out_specs, check_vma=False)
```

```python
import jax
import jax.numpy as jnp
from jax import lax
from jax.experimental import pallas as pl
from jax.experimental.pallas import tpu as pltpu
from jax.sharding import PartitionSpec as P

RATE = 0.3 / 24.0
OCEAN_RATE = 0.3
UPLIFT = 0.5
LOADING = 0.5
VISCOUS = 0.1

ROWS = 8
SUB = 8
LANES = 128
EDGE = 8
GROUP = 2 * EDGE
TILES = 4
HALF = TILES * GROUP
SPAN = TILES + 1
WINDOW = TILES

LEVEL, FLUX_X, FLUX_Y, DEPTH, FLOOR, WET = range(6)
VX, VY, VZ, SXX, SYY, SZZ, SXY, SXZ, SYZ, LAME, SHEAR, BUOY = range(12)
FIELDS = 12

OPEN = ((VX, 0), (VX, 1), (VX, 7), (VY, 0), (VY, 6), (VY, 7), (VZ, 0), (VZ, 1), (VZ, 7))
CLOSED = tuple((c, y) for y in range(ROWS) for c in (VX, VY, VZ) if (c, y) not in OPEN)
INNER = (3, 4)
OUTER = tuple(y for y in range(ROWS) if y not in INNER)

SPEED_HIGH = ((VX, 7), (VY, 6), (VY, 7), (VZ, 7))
SPEED_LOW = ((VX, 0), (VX, 1), (VY, 0), (VZ, 0), (VZ, 1))
STRESS_HIGH = ((SXY, 6), (SXY, 7), (SYY, 7), (SYZ, 6), (SYZ, 7))
STRESS_LOW = ((SXY, 0), (SYY, 0), (SYY, 1), (SYZ, 0))
BUOY_HIGH = ((BUOY, 6), (BUOY, 7))
BUOY_LOW = ((BUOY, 0), (BUOY, 1))
LINES = (None, WET, FLOOR, FLUX_X, FLUX_Y)


def rolled(x, shift, axis):
    shift %= x.shape[axis]
    return x if shift == 0 else pltpu.roll(x, shift, axis)


def tile(ref, index, start=None):
    if start is None:
        return ref[index * SUB : (index + 1) * SUB, :]
    return ref[pl.ds(start + index * SUB, SUB), :]


def row(ref, index):
    return ref[index : index + 1, :]


def store(ref, index, value):
    ref[index * SUB : (index + 1) * SUB, :] = value


def split(x, parts):
    out = []
    for part in range(parts):
        out.append(x.astype(jnp.bfloat16))
        if part + 1 < parts:
            x = x - out[-1].astype(jnp.float32)
    return jnp.concatenate(out, axis=1)


def minus(a, b):
    if b is None:
        return a
    return -b if a is None else a - b


def near_far(a, b, c, d):
    near, far = 27.0 * minus(a, b), minus(c, d)
    return near if c is None and d is None else near - far


class Grid:
    def __init__(self, origin=None, before=None, after=None):
        self.origin, self.before, self.after = origin, before, after
        self.sub = lax.broadcasted_iota(jnp.int32, (SUB, LANES), 0)
        self.lane = lax.broadcasted_iota(jnp.int32, (SUB, LANES), 1)
        self.first = self.lane % GROUP < EDGE
        self.left = self.lane < HALF
        self.group = self.lane // GROUP
        self.zero = jnp.zeros((SUB, LANES), jnp.float32)
        depth = [self.sub + SUB * t for t in range(TILES)] + [self.sub + SUB * (self.group % TILES)]
        self.depth = [d.astype(jnp.float32) for d in depth]

    def beside(self, window):
        return jnp.where(self.first, window, rolled(window, HALF, 1))

    def edge(self, beside, t):
        return None if t == WINDOW else rolled(beside, LANES - EDGE - GROUP * t, 1)

    def along(self, x, offset, edge):
        if edge is not None:
            lane = self.lane
            keep = {-1: lane == LANES - 1, -2: lane >= LANES - 2, 1: lane == 0, 2: lane <= 1}[offset]
            x = jnp.where(keep, edge, x)
        return rolled(x, -offset, 1)

    def down(self, field, y, t, offset):
        if t < WINDOW:
            x = field(y, t, self.origin + offset)
            if t == 0 and offset < 0:
                return jnp.where(self.sub >= -offset, x, 0.0)
            if t == TILES - 1 and offset > 0:
                return jnp.where(self.sub < SUB - offset, x, 0.0)
            return x
        x, at = field(y, t), self.lane % HALF
        if offset < 0:
            beyond, far = jnp.where(at >= GROUP, rolled(x, GROUP, 1), 0.0), self.sub >= SUB + offset
        else:
            beyond, far = jnp.where(at < HALF - GROUP, rolled(x, -GROUP, 1), 0.0), self.sub < offset
        return rolled(jnp.where(far, beyond, x), -offset, 0)

    def fz(self, field, y, t):
        down = lambda offset: self.down(field, y, t, offset)
        return near_far(down(1), field(y, t), down(2), down(-1))

    def bz(self, field, y, t):
        down = lambda offset: self.down(field, y, t, offset)
        return near_far(field(y, t), down(-1), down(1), down(-2))

    def along_rows(self, matrix, rows):
        main = split(jnp.concatenate([f(y, t) for f, y in rows for t in range(TILES)], axis=0), 2)
        sides = [f(y, WINDOW) for f, y in rows]
        side = split(jnp.concatenate(sides + sides[: len(sides) % 2], axis=0), 2)
        main = jnp.dot(main, matrix[:, :LANES], preferred_element_type=jnp.float32)
        side = jnp.dot(side, matrix[...], preferred_element_type=jnp.float32)
        out = []
        for i in range(len(rows)):
            part = side[i * SUB : (i + 1) * SUB, :]
            parts = [part[:, t * LANES : (t + 1) * LANES] for t in range(SPAN)]
            tiles = [
                main[(i * TILES + t) * SUB : (i * TILES + t + 1) * SUB, :] + parts[1 + t] for t in range(TILES)
            ]
            out.append(tiles + parts[:1])
        return out

    def fy(self, field, y, t):
        return near_far(field(y + 1, t), field(y, t), field(y + 2, t), field(y - 1, t))

    def by(self, field, y, t):
        return near_far(field(y, t), field(y - 1, t), field(y + 1, t), field(y - 2, t))

    def windows(self, own, from_left, from_right):
        return jnp.where(
            self.left, jnp.where(self.first, from_left, own), jnp.where(self.first, own, from_right)
        )

    def every_group(self, x):
        for shift in (GROUP, 2 * GROUP):
            x = x + jnp.where(self.lane % HALF >= shift, rolled(x, shift, 1), rolled(x, shift - HALF, 1))
        return x

    def across(self, x, offset, beside):
        end = 0 if offset < 0 else ROWS - 1
        return jnp.where(self.sub == end, beside, rolled(x, -offset, 0))


def inside(field):
    return lambda y, t, *start: field(y, t, *start) if 0 <= y < ROWS else None


def fields_of(main, windows):
    def field(f):
        def read(y, t, *start):
            return tile(windows, f * ROWS + y) if t == WINDOW else tile(main, (f * ROWS + y) * TILES + t, *start)

        return read

    return field


def pack(grid, groups, to_right, out):
    for index, (a, b, c, d) in enumerate(groups):
        if to_right:
            one, two = jnp.where(grid.first, a, rolled(b, EDGE, 1)), jnp.where(grid.first, c, rolled(d, EDGE, 1))
        else:
            one, two = jnp.where(grid.first, rolled(b, -EDGE, 1), a), jnp.where(grid.first, rolled(d, -EDGE, 1), c)
        store(out, index, jnp.where(grid.left, one, two))


def pack_edges(grid, own, own_flat, to_right, out):
    @pl.when(to_right)
    def _():
        pack(grid, edge_groups(own, own_flat), True, out)

    @pl.when(jnp.logical_not(to_right))
    def _():
        pack(grid, edge_groups(own, own_flat), False, out)


def edge_groups(own, own_flat):
    groups = [
        [tile(own, h * ROWS + y) for y in (q, q + 1) for h in (f, f + 1)]
        for f in range(0, FIELDS, 2)
        for q in range(0, ROWS, 2)
    ]
    flat = [tile(own_flat, k) for k in range(6)]
    return groups + [flat[:4], flat[4:] * 2]


def unpack(grid, items, odd, even_in, odd_in, index):
    x, y = tile(even_in, index), tile(odd_in, index)
    before, after = jnp.where(odd, x, y), jnp.where(odd, y, x)
    befores = [before, rolled(before, -EDGE, 1), rolled(before, HALF, 1), rolled(before, HALF - EDGE, 1)]
    afters = [rolled(after, HALF, 1), rolled(after, HALF + EDGE, 1), after, rolled(after, EDGE, 1)]
    return [grid.windows(*three) for three in zip(items, befores, afters)]


def difference_matrix(out, weights, offsets):
    shape = (LANES, LANES)
    k, n = [lax.broadcasted_iota(jnp.int32, shape, axis) for axis in range(2)]

    def weight(apart):
        total = jnp.zeros(shape, jnp.float32)
        for w, offset in zip(weights, offsets):
            total = jnp.where(apart == offset, w, total)
        return total

    inner, left = k % GROUP, k < HALF
    column = jnp.where(left, inner - EDGE, LANES - EDGE + inner)
    outside = (left & (inner < EDGE)) | (jnp.logical_not(left) & (inner >= EDGE))
    beside = jnp.where(outside, weight(n - column), 0.0)
    parts = [weight(n - k)]
    parts += [jnp.where(k % HALF // GROUP == t, beside, 0.0) for t in range(TILES)]
    for p, x in enumerate(parts):
        for half in range(2):
            out[half * LANES : (half + 1) * LANES, p * LANES : (p + 1) * LANES] = x.astype(jnp.bfloat16)


def picker(t):
    k, n = [lax.broadcasted_iota(jnp.int32, (LANES, LANES), axis) for axis in range(2)]
    column = (n % GROUP - EDGE) % LANES
    one = jnp.where((n % HALF // GROUP == t) & (k == column), 1.0, 0.0).astype(jnp.bfloat16)
    return jnp.concatenate([one] * 3, axis=0)


def edges_kernel(flags, *refs):
    hbm, refs = refs[:8], refs[8:]
    (before, after, main, flat, own, own_flat, odd_way), (ocean, deep, floor, wet, sem) = refs[:7], refs[7:]
    ready = {}
    at = 0
    for source, first, count in ((0, 0, 3), (0, 3, 3), (0, 6, 3), (1, LAME, 1), (2, SHEAR, 1), (3, BUOY, 1)):
        copies = []
        for y in range(ROWS):
            if source:
                pair = hbm[source].at[:, y, :], main.at[first, y]
            else:
                pair = hbm[0].at[first : first + count, :, y, :], main.at[first : first + count, y]
            copies.append(pltpu.make_async_copy(*pair, sem.at[at]))
            at += 1
        ready[first] = copies
    flats = [pltpu.make_async_copy(hbm[4 + k], target, sem.at[at + k]) for k, target in enumerate((ocean, deep, floor, wet))]
    for copies in list(ready.values()) + [flats]:
        for copy in copies:
            copy.start()
    difference_matrix(before, (27.0, -27.0, -1.0, 1.0), (0, 1, -1, 2))
    difference_matrix(after, (27.0, -27.0, -1.0, 1.0), (-1, 0, -2, 1))
    pickers = [picker(t) for t in range(TILES)]
    grid = Grid()
    for f in range(FIELDS):
        for copy in ready.get(f, ()):
            copy.wait()
        total = None
        for t in range(TILES):
            tiles = [main[f, y, t * SUB : (t + 1) * SUB, :] for y in range(ROWS)]
            part = jnp.dot(split(jnp.concatenate(tiles, axis=0), 3), pickers[t], preferred_element_type=jnp.float32)
            total = part if total is None else total + part
        own[f * ROWS * SUB : (f + 1) * ROWS * SUB, :] = total
    for copy in flats:
        copy.wait()
    planes = [ocean[k] for k in range(3)] + [deep[...]]
    planes += [floor[...].astype(jnp.float32), wet[...].astype(jnp.float32)]
    for k, x in enumerate(planes):
        store(flat, k, x)
        out = grid.zero
        for g in range(LANES // GROUP):
            out = jnp.where(grid.group == g, rolled(x, EDGE + GROUP * g, 1), out)
        store(own_flat, k, out)
    pack_edges(grid, own, own_flat, (flags[0] & 1) == 1, odd_way)


def edges_rest_kernel(flags, own, own_flat, even_way):
    pack_edges(Grid(), own, own_flat, (flags[0] & 1) == 0, even_way)


def speeds(grid, stress, speed, buoy, todo, put):
    sxx, syy, szz, sxy, sxz, syz = stress
    forth = [(VX, y) for c, y in todo if c == VX]
    back = [(c, y) for c, y in todo if c != VX]
    change = dict(zip(forth, grid.along_rows(grid.after, [(sxx, y) for _, y in forth])))
    change.update(zip(back, grid.along_rows(grid.before, [(sxy if c == VY else sxz, y) for c, y in back])))
    for y in range(ROWS):
        parts = [c for c in (VX, VY, VZ) if (c, y) in todo]
        if not parts:
            continue
        for t in range(SPAN):
            rate = RATE * buoy(y, t)
            for c in parts:
                a = change[c, y][t]
                if c == VX:
                    a = a + grid.by(sxy, y, t) + grid.bz(sxz, y, t)
                elif c == VY:
                    a = a + grid.fy(syy, y, t) + grid.bz(syz, y, t)
                else:
                    a = a + grid.by(syz, y, t) + grid.fz(szz, y, t)
                put(c, y, t, speed(c)(y, t) + rate * a)


def stresses(grid, rows, tiles, speed, stress, lame, shear, put):
    vx, vy, vz = [speed(c) for c in (VX, VY, VZ)]
    back = grid.along_rows(grid.before, [(vx, y) for y in rows])
    forth = grid.along_rows(grid.after, [(v, y) for v in (vy, vz) for y in rows])
    for i, y in enumerate(rows):
        for t in range(tiles):
            strain_x = back[i][t]
            strain_y = grid.by(vy, y, t)
            strain_z = grid.bz(vz, y, t)
            mu = RATE * shear(y, t)
            spread = (RATE * lame(y, t)) * (strain_x + strain_y + strain_z)
            two = mu + mu
            put(SXX, y, t, stress(SXX)(y, t) + (spread + two * strain_x))
            put(SYY, y, t, stress(SYY)(y, t) + (spread + two * strain_y))
            put(SZZ, y, t, stress(SZZ)(y, t) + (spread + two * strain_z))
            put(SXY, y, t, stress(SXY)(y, t) + mu * (grid.fy(vx, y, t) + forth[i][t]))
            put(SXZ, y, t, stress(SXZ)(y, t) + mu * (grid.fz(vx, y, t) + forth[len(rows) + i][t]))
            put(SYZ, y, t, stress(SYZ)(y, t) + mu * (grid.fz(vy, y, t) + grid.fy(vz, y, t)))


def flat_edge(grid, at, k):
    return grid.edge(grid.beside(at(1)), 0) if k == 0 else None


def partial_level(grid, flat, put):
    for k in range(2):
        x, y = flat(FLUX_X, k), flat(FLUX_Y, k)
        edge = flat_edge(grid, lambda q: flat(FLUX_X, q), k)
        spread = 0.5 * (grid.along(x, 1, edge) - grid.along(x, -1, edge))
        spread = spread + 0.5 * (grid.across(y, 1, 0.0) - grid.across(y, -1, 0.0))
        put(k, flat(LEVEL, k) - OCEAN_RATE * (flat(WET, k) * spread))


def cells(rows, tiles):
    return [(f, y, t) for f, y in rows for t in tiles]


class Message:
    def __init__(self, tiles):
        self.at = {which: i for i, which in enumerate(tiles)}
        self.base = len(tiles) * SUB
        self.size = self.base + 2 * SUB


ALL, INSIDE = range(SPAN), range(TILES)
FIRST = [
    Message(cells(rows, ALL))
    for rows in (SPEED_HIGH + STRESS_HIGH + BUOY_HIGH, SPEED_LOW + STRESS_LOW + BUOY_LOW)
]
LATER = [
    Message(cells(speed, INSIDE) + cells(rest, ALL))
    for speed, rest in ((SPEED_HIGH, STRESS_HIGH), (SPEED_LOW, STRESS_LOW))
]


def message_tiles(kind):
    return max(m.size for m in kind) // SUB


def send(kind, odd, field, line, even_way, odd_way):
    high, low = kind

    def fill(message, edge, out):
        for (f, y, t), at in message.at.items():
            store(out, at, field(f)(y, t))
        at = message.base
        for which in LINES:
            for k in range(2):
                out[at : at + 1, :] = line(which, k, edge)
                at += 1
        out[at : at + 6, :] = jnp.zeros((6, LANES), jnp.float32)
        tail = out.shape[0]
        if message.size < tail:
            out[message.size : tail, :] = jnp.zeros((tail - message.size, LANES), jnp.float32)

    @pl.when(odd)
    def _():
        fill(high, ROWS - 1, odd_way)
        fill(low, 0, even_way)

    @pl.when(jnp.logical_not(odd))
    def _():
        fill(high, ROWS - 1, even_way)
        fill(low, 0, odd_way)


class Received:
    def __init__(self, message, odd, if_odd, if_even):
        self.message, self.odd, self.if_odd, self.if_even = message, odd, if_odd, if_even

    def __call__(self, f, y, t):
        at = self.message.at[f, y, t]
        return jnp.where(self.odd, tile(self.if_odd, at), tile(self.if_even, at))

    def line(self, which, k):
        at = self.message.base + 2 * LINES.index(which) + k
        return jnp.where(self.odd, row(self.if_odd, at), row(self.if_even, at))


def received(kind, odd, odd_in, even_in):
    return Received(kind[0], odd, even_in, odd_in), Received(kind[1], odd, odd_in, even_in)


AROUND = ROWS + 4


def finish(grid, tiles, partial, stress, buoy, lo, hi, lo_buoy, hi_buoy, speed):
    sxy, syy, syz = [stress(f) for f in (SXY, SYY, SYZ)]

    def put(c, y, t, value):
        store(speed, (c * AROUND + y + 2) * SPAN + t, value)

    for t in range(SPAN):
        for c, f in ((VX, SXY), (VZ, SYZ)):
            two, one = lo(f, 6, t), lo(f, 7, t)
            rate = [RATE * buoy(y, t) for y in (0, 1, 7)]
            put(c, 0, t, partial(c, 0, t) + rate[0] * (two - 27.0 * one))
            put(c, 1, t, partial(c, 1, t) + rate[1] * one)
            put(c, 7, t, partial(c, 7, t) - rate[2] * hi(f, 0, t))
        h8, h9 = hi(SYY, 0, t), hi(SYY, 1, t)
        put(VY, 0, t, partial(VY, 0, t) + (RATE * buoy(0, t)) * lo(SYY, 7, t))
        put(VY, 6, t, partial(VY, 6, t) - (RATE * buoy(6, t)) * h8)
        put(VY, 7, t, partial(VY, 7, t) + (RATE * buoy(7, t)) * (27.0 * h8 - h9))
    for t in range(tiles):
        b2, b1 = RATE * lo_buoy(BUOY, 6, t), RATE * lo_buoy(BUOY, 7, t)
        b8, b9 = RATE * hi_buoy(BUOY, 0, t), RATE * hi_buoy(BUOY, 1, t)
        put(VX, -1, t, lo(VX, 7, t) - b1 * sxy(0, t))
        put(VY, -2, t, lo(VY, 6, t) - b2 * syy(0, t))
        put(VY, -1, t, lo(VY, 7, t) + b1 * (27.0 * syy(0, t) - syy(1, t)))
        put(VZ, -1, t, lo(VZ, 7, t) - b1 * syz(0, t))
        put(VX, 8, t, hi(VX, 0, t) + b8 * (sxy(6, t) - 27.0 * sxy(7, t)))
        put(VX, 9, t, hi(VX, 1, t) + b9 * sxy(7, t))
        put(VY, 8, t, hi(VY, 0, t) + b8 * syy(7, t))
        put(VZ, 8, t, hi(VZ, 0, t) + b8 * (syz(6, t) - 27.0 * syz(7, t)))
        put(VZ, 9, t, hi(VZ, 1, t) + b9 * syz(7, t))


def seafloor(grid, vz, y, floors, out, index):
    total = None
    for t in range(TILES):
        part = jnp.where(floors[0] == grid.depth[t], vz(y, t), 0.0)
        total = part if total is None else total + part
    out[index : index + 1, :] = jnp.sum(total, axis=0, keepdims=True)
    if len(floors) > 1:
        part = jnp.where(floors[1] == grid.depth[WINDOW], vz(y, WINDOW), 0.0)
        out[2 * SUB + index : 2 * SUB + index + 1, :] = jnp.sum(part, axis=0, keepdims=True)


def sea(grid, speed, level, now, fixed, line, lo, hi, sums, new, last):
    vz = speed(VZ)
    for y in range(ROWS):
        seafloor(grid, vz, y, [line(FLOOR, k, y) for k in range(2)], sums, y)
    ends = 1 if last else 2
    for y, side, at in ((-1, lo, ROWS), (ROWS, hi, ROWS + 1)):
        seafloor(grid, vz, y, [side.line(FLOOR, k) for k in range(ends)], sums, at)
    floors, beyond = [tile(sums, 0), grid.every_group(tile(sums, 2))], [tile(sums, 1), None]
    if not last:
        beyond[1] = grid.every_group(tile(sums, 3))
    sub = grid.sub
    levels, lows, highs = [], [], []
    for k in range(2):
        near = jnp.where(sub == 0, lo.line(FLUX_Y, k), jnp.where(sub == ROWS - 1, -hi.line(FLUX_Y, k), 0.0))
        levels.append(level(k) + fixed(WET, k) * (UPLIFT * floors[k] + (0.5 * OCEAN_RATE) * near))
        new(LEVEL, k, levels[k])
        if k < ends:
            for side, at, y, sign, out in ((lo, 0, 0, -1.0, lows), (hi, 1, ROWS - 1, 1.0, highs)):
                mine = (sign * 0.5 * OCEAN_RATE) * line(FLUX_Y, k, y)
                rest = UPLIFT * beyond[k][at : at + 1, :] + mine
                out.append(side.line(None, k) + side.line(WET, k) * rest)
    for k in range(ends):
        wet, deep = fixed(WET, k), fixed(DEPTH, k)
        edge = flat_edge(grid, lambda q: levels[q], k)
        slope_x = 0.5 * (grid.along(levels[k], 1, edge) - grid.along(levels[k], -1, edge))
        slope_y = 0.5 * (grid.across(levels[k], 1, highs[k]) - grid.across(levels[k], -1, lows[k]))
        for which, slope in ((FLUX_X, slope_x), (FLUX_Y, slope_y)):
            x = now(which, k)
            edge = flat_edge(grid, lambda q: now(which, q), k)
            laplace = grid.along(x, 1, edge) + grid.along(x, -1, edge) - 4.0 * x
            laplace = laplace + grid.across(x, 1, hi.line(which, k)) + grid.across(x, -1, lo.line(which, k))
            new(which, k, wet * (x - OCEAN_RATE * deep * slope + VISCOUS * laplace))
    return levels


def press(grid, levels, fixed, line, pressure):
    for k in range(2):
        store(pressure, k, LOADING * fixed(WET, k) * levels[k])

    def load(y, t):
        k = 1 if t == WINDOW else 0
        return jnp.where(line(FLOOR, k, y) == grid.depth[t], row(pressure, k * ROWS + y), 0.0)

    return load


def edge_index(c, y):
    return OPEN.index((c, y)) * SPAN


def block_index(c, y):
    return (c * ROWS + y) * SPAN


def start_kernel(
    flags, before, after, main, flat, own, own_flat, odd_in, even_in,
    windows, flat_windows, partial, level, even_way, odd_way,
):
    grid = Grid(flags[2], before, after)
    odd = (flags[0] & 1) == 1
    for f in range(0, FIELDS, 2):
        for q in range(0, ROWS, 2):
            places = [h * ROWS + y for y in (q, q + 1) for h in (f, f + 1)]
            items = [tile(own, p) for p in places]
            for p, x in zip(places, unpack(grid, items, odd, even_in, odd_in, (f * ROWS // 2 + q) // 2)):
                store(windows, p, x)
    items = [tile(own_flat, k) for k in range(6)]
    base = FIELDS * ROWS // 4
    for k, x in enumerate(unpack(grid, items[:4], odd, even_in, odd_in, base)):
        store(flat_windows, k, x)
    for k, x in enumerate(unpack(grid, items[4:] * 2, odd, even_in, odd_in, base + 1)[:2]):
        store(flat_windows, 4 + k, x)

    field = fields_of(main, windows)
    speeds(
        grid, [inside(field(f)) for f in range(SXX, SYZ + 1)], field, field(BUOY), OPEN,
        lambda c, y, t, value: store(partial, edge_index(c, y) + t, value),
    )
    flats = (flat, flat_windows)
    partial_level(grid, lambda f, k: tile(flats[k], f), lambda k, value: store(level, k, value))

    def rows_of(f):
        return (lambda y, t: tile(partial, edge_index(f, y) + t)) if f < 3 else field(f)

    def line(which, k, y):
        return row(level, k * ROWS + y) if which is None else row(flats[k], which * ROWS + y)

    send(FIRST, (flags[1] & 1) == 1, rows_of, line, even_way, odd_way)


def start_rest_kernel(flags, before, after, main, windows, speed_out, stress_out):
    grid = Grid(flags[2], before, after)
    field = fields_of(main, windows)
    speeds(
        grid, [inside(field(f)) for f in range(SXX, SYZ + 1)], field, field(BUOY), CLOSED,
        lambda c, y, t, value: store(speed_out, block_index(c, y) + t, value),
    )
    stresses(
        grid, INNER, SPAN, block_reader(speed_out, VX), field,
        field(LAME), field(SHEAR),
        lambda f, y, t, value: store(stress_out, block_index(f - SXX, y) + t, value),
    )


def block_reader(ref, least):
    return lambda f: lambda y, t, *start: tile(ref, block_index(f - least, y) + t, *start)


def speed_reader(around, block):
    def speed(c):
        def read(y, t, *start):
            if (c, y) in CLOSED:
                return tile(block, block_index(c, y) + t, *start)
            return tile(around, (c * AROUND + y + 2) * SPAN + t, *start)

        return read

    return speed


def middle_kernel(
    flags, before, after, main, windows, flat, flat_windows, partial, level, speed_in, stress_in,
    odd_in, even_in,
    speed_out, stress_out, ocean, partial_out, level_out, even_way, odd_way,
    sums, pressure,
):
    grid = Grid(flags[2], before, after)
    odd = (flags[1] & 1) == 1
    lo, hi = received(FIRST, odd, odd_in, even_in)
    field = fields_of(main, windows)
    finish(
        grid, SPAN, lambda c, y, t: tile(partial, edge_index(c, y) + t), field, field(BUOY), lo, hi, lo, hi, speed_out
    )
    speed = speed_reader(speed_out, speed_in)
    flats = (flat, flat_windows)
    fixed = lambda f, k: tile(flats[k], f)
    line = lambda f, k, y: row(flats[k], f * ROWS + y)

    def new(f, k, value):
        store(ocean, 3 * k + f, value)

    levels = sea(grid, speed, lambda k: tile(level, k), fixed, fixed, line, lo, hi, sums, new, False)
    load = press(grid, levels, fixed, line, pressure)

    def put(f, y, t, value):
        store(stress_out, block_index(f - SXX, y) + t, value - load(y, t) if f == SZZ else value)

    stresses(grid, OUTER, SPAN, speed, field, field(LAME), field(SHEAR), put)
    for f in range(SXX, SYZ + 1):
        for y in INNER:
            for t in range(SPAN):
                put(f, y, t, tile(stress_in, block_index(f - SXX, y) + t))
    stress = block_reader(stress_out, SXX)
    speeds(
        grid, [inside(stress(f)) for f in range(SXX, SYZ + 1)], speed, field(BUOY), OPEN,
        lambda c, y, t, value: store(partial_out, edge_index(c, y) + t, value),
    )
    moving = lambda f, k: tile(flats[k], f) if f >= DEPTH else tile(ocean, 3 * k + f)
    partial_level(grid, moving, lambda k, value: store(level_out, k, value))

    def rows_of(f):
        return (lambda y, t: tile(partial_out, edge_index(f, y) + t)) if f < 3 else stress(f)

    def line_out(which, k, y):
        if which is None:
            return row(level_out, k * ROWS + y)
        return line(which, k, y) if which >= DEPTH else row(ocean, (3 * k + which) * ROWS + y)

    send(LATER, odd, rows_of, line_out, even_way, odd_way)


def middle_rest_kernel(flags, before, after, main, windows, around, speed_in, stress_in, speed_out, stress_out):
    grid = Grid(flags[2], before, after)
    field = fields_of(main, windows)
    stress = block_reader(stress_in, SXX)
    speeds(
        grid, [inside(stress(f)) for f in range(SXX, SYZ + 1)], speed_reader(around, speed_in), field(BUOY), CLOSED,
        lambda c, y, t, value: store(speed_out, block_index(c, y) + t, value),
    )
    stresses(
        grid, INNER, TILES, block_reader(speed_out, VX), stress,
        field(LAME), field(SHEAR),
        lambda f, y, t, value: store(stress_out, block_index(f - SXX, y) + t, value),
    )


def last_kernel(
    flags, before, after, main, windows, flat, flat_windows, stress_in, ocean_in, partial, level, speed_in, inner_in,
    odd_first, even_first, odd_in, even_in,
    wave_hbm, ocean_out,
    sums, pressure, around, wave, sem,
):
    grid = Grid(flags[2], before, after)
    odd = (flags[1] & 1) == 1
    lo, hi = received(LATER, odd, odd_in, even_in)
    lo_buoy, hi_buoy = received(FIRST, odd, odd_first, even_first)
    field = fields_of(main, windows)
    stress = block_reader(stress_in, SXX)
    finish(
        grid, TILES, lambda c, y, t: tile(partial, edge_index(c, y) + t), stress, field(BUOY),
        lo, hi, lo_buoy, hi_buoy, around,
    )
    speed = speed_reader(around, speed_in)
    sent = []

    def copy(source, target):
        sent.append(pltpu.make_async_copy(source, target, sem.at[len(sent)]))
        sent[-1].start()

    def copy_row(ref, index, f, y):
        copy(ref.at[index * SUB : (index + TILES) * SUB, :], wave_hbm.at[f, :, y, :])

    for c, y in CLOSED:
        copy_row(speed_in, block_index(c, y), c, y)
    for f in (SXX, SYY, SXY, SXZ, SYZ):
        for y in INNER:
            copy_row(inner_in, block_index(f - SXX, y), f, y)
    for c, y in OPEN:
        copy_row(around, (c * AROUND + y + 2) * SPAN, c, y)
    flats = (flat, flat_windows)
    fixed = lambda f, k: tile(flats[k], f)

    def line(f, k, y):
        return row(flats[k], f * ROWS + y) if f >= DEPTH else row(ocean_in, (3 * k + f) * ROWS + y)

    def new(f, k, value):
        if k == 0:
            store(ocean_out, f, value)

    levels = sea(
        grid, speed, lambda k: tile(level, k), lambda f, k: tile(ocean_in, 3 * k + f), fixed, line, lo, hi, sums, new, True
    )
    load = press(grid, levels, fixed, line, pressure)

    def put(f, y, t, value):
        wave[f - SXX, y, t * SUB : (t + 1) * SUB, :] = value - load(y, t) if f == SZZ else value

    for y in INNER:
        for t in range(TILES):
            put(SZZ, y, t, tile(inner_in, block_index(SZZ - SXX, y) + t))
        copy(wave.at[SZZ - SXX, y], wave_hbm.at[SZZ, :, y, :])
    for y in OUTER:
        stresses(grid, (y,), TILES, speed, stress, field(LAME), field(SHEAR), put)
        copy(wave.at[:, y], wave_hbm.at[SXX : SYZ + 1, :, y, :])
    for one in sent:
        one.wait()


IN_VMEM = pl.BlockSpec(memory_space=pltpu.VMEM)
IN_SMEM = pl.BlockSpec(memory_space=pltpu.SMEM)
IN_HBM = pl.BlockSpec(memory_space=pltpu.HBM)


def call(kernel, tiles, scratch, *arguments, flags=None, place=IN_VMEM, out_places=None, work=1):
    specs = [place] * len(arguments)
    if flags is not None:
        arguments, specs = (flags, *arguments), [IN_SMEM] + specs
    moved = sum(x.size for x in arguments) + sum(n for n in tiles if isinstance(n, int)) * SUB * LANES
    return pl.pallas_call(
        kernel,
        out_shape=[n if hasattr(n, "dtype") else jax.ShapeDtypeStruct((n * SUB, LANES), jnp.float32) for n in tiles],
        in_specs=specs,
        out_specs=out_places or [IN_VMEM] * len(tiles),
        scratch_shapes=scratch,
        cost_estimate=pl.CostEstimate(flops=work * 1000000, bytes_accessed=4 * moved, transcendentals=0),
        compiler_params=pltpu.CompilerParams(vmem_limit_bytes=24 * 1024 * 1024),
    )(*arguments)


def planes(n):
    return pltpu.VMEM((n * SUB, LANES), jnp.float32)


def swap(x, axis, start):
    pairs = [(i, i + 1) for i in range(start, lax.axis_size(axis) - 1, 2)]
    return lax.ppermute(x, axis, pairs + [(j, i) for i, j in pairs])


def local(*arguments):
    ocean_state = arguments[4]
    inputs = [pltpu.with_memory_space_constraint(x, pltpu.HBM) for x in arguments]
    flags = jnp.stack([lax.axis_index("gx"), lax.axis_index("gy"), 0])
    matrix = jax.ShapeDtypeStruct((2 * LANES, SPAN * LANES), jnp.bfloat16)
    cells4 = jax.ShapeDtypeStruct((FIELDS, ROWS, TILES * SUB, LANES), jnp.float32)

    edge = FIELDS * ROWS // 4 + 2
    before, after, main, flat, own, own_flat, odd_way = call(
        edges_kernel, [matrix, matrix, cells4, 6, FIELDS * ROWS, 6, edge],
        [pltpu.VMEM(x.shape, x.dtype) for x in inputs[4:]] + [pltpu.SemaphoreType.DMA((6 * ROWS + 4,))],
        *inputs, flags=flags, place=IN_HBM,
    )
    main = main.reshape(-1, LANES)
    odd_in = swap(odd_way, "gx", 1)
    first, later = [message_tiles(kind) for kind in (FIRST, LATER)]
    (even_way,) = call(edges_rest_kernel, [edge], [], own, own_flat, flags=flags, work=400)
    even_in = swap(even_way, "gx", 0)
    edges, block = len(OPEN) * SPAN, ROWS * SPAN
    windows, flat_windows, partial, level, even_way, odd_way = call(
        start_kernel, [FIELDS * ROWS, 6, edges, 2, first, first], [],
        before, after, main, flat, own, own_flat, odd_in, even_in, flags=flags,
    )
    y_first = swap(odd_way, "gy", 1), swap(even_way, "gy", 0)
    speed, inner = call(start_rest_kernel, [3 * block, 6 * block], [], before, after, main, windows, flags=flags, work=4)
    around, stress, ocean, partial, level, even_way, odd_way = call(
        middle_kernel, [3 * AROUND * SPAN, 6 * block, 6, edges, 2, later, later], [planes(4), planes(2)],
        before, after, main, windows, flat, flat_windows, partial, level, speed, inner, *y_first, flags=flags,
    )
    y_in = swap(odd_way, "gy", 1), swap(even_way, "gy", 0)
    speed, inner = call(
        middle_rest_kernel, [3 * block, 6 * block], [], before, after, main, windows, around, speed, stress, flags=flags, work=4
    )
    copies = len(CLOSED) + len(OPEN) + 5 * len(INNER) + len(INNER) + len(OUTER)
    wave_out, ocean_out = call(
        last_kernel, [jax.ShapeDtypeStruct(arguments[0].shape, jnp.float32), 3],
        [
            planes(4), planes(2), planes(3 * AROUND * SPAN), pltpu.VMEM((6, *cells4.shape[1:]), jnp.float32),
            pltpu.SemaphoreType.DMA((copies,)),
        ],
        before, after, main, windows, flat, flat_windows, stress, ocean, partial, level, speed, inner, *y_first, *y_in,
        flags=flags, out_places=[IN_HBM, IN_VMEM],
    )
    return wave_out, ocean_out.reshape(ocean_state.shape)


def solution(mesh):
    in_specs = (
        P(None, None, "gy", "gx"),
        P(None, "gy", "gx"),
        P(None, "gy", "gx"),
        P(None, "gy", "gx"),
        P(None, "gy", "gx"),
        P("gy", "gx"),
        P("gy", "gx"),
        P("gy", "gx"),
    )
    out_specs = (P(None, None, "gy", "gx"), P(None, "gy", "gx"))
    return jax.shard_map(local, mesh=mesh, in_specs=in_specs, out_specs=out_specs, check_vma=False)
```

```python
import jax
import jax.numpy as jnp
from jax import lax
from jax.experimental import pallas as pl
from jax.experimental.pallas import tpu as pltpu
from jax.sharding import PartitionSpec as P

RATE = 0.3 / 24.0
OCEAN_RATE = 0.3
UPLIFT = 0.5
LOADING = 0.5
VISCOUS = 0.1

ROWS = 8
SUB = 8
LANES = 128
EDGE = 8
GROUP = 2 * EDGE
TILES = 4
HALF = TILES * GROUP
SPAN = TILES + 1
WINDOW = TILES

LEVEL, FLUX_X, FLUX_Y, DEPTH, FLOOR, WET = range(6)
VX, VY, VZ, SXX, SYY, SZZ, SXY, SXZ, SYZ, LAME, SHEAR, BUOY = range(12)
FIELDS = 12

OPEN = ((VX, 0), (VX, 1), (VX, 7), (VY, 0), (VY, 6), (VY, 7), (VZ, 0), (VZ, 1), (VZ, 7))
CLOSED = tuple((c, y) for y in range(ROWS) for c in (VX, VY, VZ) if (c, y) not in OPEN)
INNER = (3, 4)
OUTER = tuple(y for y in range(ROWS) if y not in INNER)

SPEED_HIGH = ((VX, 7), (VY, 6), (VY, 7), (VZ, 7))
SPEED_LOW = ((VX, 0), (VX, 1), (VY, 0), (VZ, 0), (VZ, 1))
STRESS_HIGH = ((SXY, 6), (SXY, 7), (SYY, 7), (SYZ, 6), (SYZ, 7))
STRESS_LOW = ((SXY, 0), (SYY, 0), (SYY, 1), (SYZ, 0))
BUOY_HIGH = ((BUOY, 6), (BUOY, 7))
BUOY_LOW = ((BUOY, 0), (BUOY, 1))
LINES = (None, WET, FLOOR, FLUX_X, FLUX_Y)


def rolled(x, shift, axis):
    shift %= x.shape[axis]
    return x if shift == 0 else pltpu.roll(x, shift, axis)


def tile(ref, index, start=None):
    if start is None:
        return ref[index * SUB : (index + 1) * SUB, :]
    return ref[pl.ds(start + index * SUB, SUB), :]


def row(ref, index):
    return ref[index : index + 1, :]


def store(ref, index, value):
    ref[index * SUB : (index + 1) * SUB, :] = value


def split(x, parts):
    out = []
    for part in range(parts):
        out.append(x.astype(jnp.bfloat16))
        if part + 1 < parts:
            x = x - out[-1].astype(jnp.float32)
    return jnp.concatenate(out, axis=1)


def minus(a, b):
    if b is None:
        return a
    return -b if a is None else a - b


def near_far(a, b, c, d):
    near, far = 27.0 * minus(a, b), minus(c, d)
    return near if c is None and d is None else near - far


class Grid:
    def __init__(self, origin=None, before=None, after=None):
        self.origin, self.before, self.after = origin, before, after
        self.sub = lax.broadcasted_iota(jnp.int32, (SUB, LANES), 0)
        self.lane = lax.broadcasted_iota(jnp.int32, (SUB, LANES), 1)
        self.first = self.lane % GROUP < EDGE
        self.left = self.lane < HALF
        self.group = self.lane // GROUP
        self.zero = jnp.zeros((SUB, LANES), jnp.float32)
        depth = [self.sub + SUB * t for t in range(TILES)] + [self.sub + SUB * (self.group % TILES)]
        self.depth = [d.astype(jnp.float32) for d in depth]

    def beside(self, window):
        return jnp.where(self.first, window, rolled(window, HALF, 1))

    def edge(self, beside, t):
        return None if t == WINDOW else rolled(beside, LANES - EDGE - GROUP * t, 1)

    def along(self, x, offset, edge):
        if edge is not None:
            lane = self.lane
            keep = {-1: lane == LANES - 1, -2: lane >= LANES - 2, 1: lane == 0, 2: lane <= 1}[offset]
            x = jnp.where(keep, edge, x)
        return rolled(x, -offset, 1)

    def down(self, field, y, t, offset):
        if t < WINDOW:
            x = field(y, t, self.origin + offset)
            if t == 0 and offset < 0:
                return jnp.where(self.sub >= -offset, x, 0.0)
            if t == TILES - 1 and offset > 0:
                return jnp.where(self.sub < SUB - offset, x, 0.0)
            return x
        x, at = field(y, t), self.lane % HALF
        if offset < 0:
            beyond, far = jnp.where(at >= GROUP, rolled(x, GROUP, 1), 0.0), self.sub >= SUB + offset
        else:
            beyond, far = jnp.where(at < HALF - GROUP, rolled(x, -GROUP, 1), 0.0), self.sub < offset
        return rolled(jnp.where(far, beyond, x), -offset, 0)

    def fz(self, field, y, t):
        down = lambda offset: self.down(field, y, t, offset)
        return near_far(down(1), field(y, t), down(2), down(-1))

    def bz(self, field, y, t):
        down = lambda offset: self.down(field, y, t, offset)
        return near_far(field(y, t), down(-1), down(1), down(-2))

    def along_rows(self, matrix, rows):
        main = split(jnp.concatenate([f(y, t) for f, y in rows for t in range(TILES)], axis=0), 2)
        sides = [f(y, WINDOW) for f, y in rows]
        side = split(jnp.concatenate(sides + sides[: len(sides) % 2], axis=0), 2)
        main = jnp.dot(main, matrix[:, :LANES], preferred_element_type=jnp.float32)
        side = jnp.dot(side, matrix[...], preferred_element_type=jnp.float32)
        out = []
        for i in range(len(rows)):
            part = side[i * SUB : (i + 1) * SUB, :]
            parts = [part[:, t * LANES : (t + 1) * LANES] for t in range(SPAN)]
            tiles = [
                main[(i * TILES + t) * SUB : (i * TILES + t + 1) * SUB, :] + parts[1 + t] for t in range(TILES)
            ]
            out.append(tiles + parts[:1])
        return out

    def fy(self, field, y, t):
        return near_far(field(y + 1, t), field(y, t), field(y + 2, t), field(y - 1, t))

    def by(self, field, y, t):
        return near_far(field(y, t), field(y - 1, t), field(y + 1, t), field(y - 2, t))

    def windows(self, own, from_left, from_right):
        return jnp.where(
            self.left, jnp.where(self.first, from_left, own), jnp.where(self.first, own, from_right)
        )

    def every_group(self, x):
        for shift in (GROUP, 2 * GROUP):
            x = x + jnp.where(self.lane % HALF >= shift, rolled(x, shift, 1), rolled(x, shift - HALF, 1))
        return x

    def across(self, x, offset, beside):
        end = 0 if offset < 0 else ROWS - 1
        return jnp.where(self.sub == end, beside, rolled(x, -offset, 0))


def inside(field):
    return lambda y, t, *start: field(y, t, *start) if 0 <= y < ROWS else None


def fields_of(main, windows):
    def field(f):
        def read(y, t, *start):
            return tile(windows, f * ROWS + y) if t == WINDOW else tile(main, (f * ROWS + y) * TILES + t, *start)

        return read

    return field


def pack(grid, groups, to_right, out):
    for index, (a, b, c, d) in enumerate(groups):
        if to_right:
            one, two = jnp.where(grid.first, a, rolled(b, EDGE, 1)), jnp.where(grid.first, c, rolled(d, EDGE, 1))
        else:
            one, two = jnp.where(grid.first, rolled(b, -EDGE, 1), a), jnp.where(grid.first, rolled(d, -EDGE, 1), c)
        store(out, index, jnp.where(grid.left, one, two))


def edge_groups(own, own_flat):
    groups = [
        [tile(own, h * ROWS + y) for y in (q, q + 1) for h in (f, f + 1)]
        for f in range(0, FIELDS, 2)
        for q in range(0, ROWS, 2)
    ]
    flat = [tile(own_flat, k) for k in range(6)]
    return groups + [flat[:4], flat[4:] * 2]


def unpack(grid, items, odd, even_in, odd_in, index):
    x, y = tile(even_in, index), tile(odd_in, index)
    before, after = jnp.where(odd, x, y), jnp.where(odd, y, x)
    befores = [before, rolled(before, -EDGE, 1), rolled(before, HALF, 1), rolled(before, HALF - EDGE, 1)]
    afters = [rolled(after, HALF, 1), rolled(after, HALF + EDGE, 1), after, rolled(after, EDGE, 1)]
    return [grid.windows(*three) for three in zip(items, befores, afters)]


def difference_matrix(out, weights, offsets):
    shape = (LANES, LANES)
    k, n = [lax.broadcasted_iota(jnp.int32, shape, axis) for axis in range(2)]

    def weight(apart):
        total = jnp.zeros(shape, jnp.float32)
        for w, offset in zip(weights, offsets):
            total = jnp.where(apart == offset, w, total)
        return total

    inner, left = k % GROUP, k < HALF
    column = jnp.where(left, inner - EDGE, LANES - EDGE + inner)
    outside = (left & (inner < EDGE)) | (jnp.logical_not(left) & (inner >= EDGE))
    beside = jnp.where(outside, weight(n - column), 0.0)
    parts = [weight(n - k)]
    parts += [jnp.where(k % HALF // GROUP == t, beside, 0.0) for t in range(TILES)]
    for p, x in enumerate(parts):
        for half in range(2):
            out[half * LANES : (half + 1) * LANES, p * LANES : (p + 1) * LANES] = x.astype(jnp.bfloat16)


def picker(t):
    k, n = [lax.broadcasted_iota(jnp.int32, (LANES, LANES), axis) for axis in range(2)]
    column = (n % GROUP - EDGE) % LANES
    one = jnp.where((n % HALF // GROUP == t) & (k == column), 1.0, 0.0).astype(jnp.bfloat16)
    return jnp.concatenate([one] * 2, axis=0)


def edges_kernel(flags, *refs):
    hbm, (before, after, flat, own, own_flat, even_way, odd_way), refs = refs[:8], refs[8:15], refs[15:]
    fields, picked, ocean, deep, floor, wet, sem = refs
    sources = [hbm[0].at[f] for f in range(9)] + [hbm[1], hbm[2], hbm[3]]
    copies = [pltpu.make_async_copy(x, fields.at[f], sem.at[f]) for f, x in enumerate(sources)]
    copies += [
        pltpu.make_async_copy(hbm[4 + k], x, sem.at[FIELDS + k]) for k, x in enumerate((ocean, deep, floor, wet))
    ]
    for copy in copies:
        copy.start()
    difference_matrix(before, (27.0, -27.0, -1.0, 1.0), (0, 1, -1, 2))
    difference_matrix(after, (27.0, -27.0, -1.0, 1.0), (-1, 0, -2, 1))
    pickers = [picker(t) for t in range(TILES)]
    grid = Grid()
    for f in range(FIELDS):
        copies[f].wait()
        total = None
        for t in range(TILES):
            x = fields[f, t * SUB : (t + 1) * SUB].reshape(SUB * ROWS, LANES)
            part = jnp.dot(split(x, 2), pickers[t], preferred_element_type=jnp.float32)
            total = part if total is None else total + part
        size = SUB * ROWS
        picked[f * size : (f + 1) * size, :] = total
        for y in range(ROWS):
            store(own, f * ROWS + y, picked[pl.ds(f * size + y, SUB, stride=ROWS), :])
    for copy in copies[FIELDS:]:
        copy.wait()
    planes = [ocean[k] for k in range(3)] + [deep[...]]
    planes += [floor[...].astype(jnp.float32), wet[...].astype(jnp.float32)]
    for k, x in enumerate(planes):
        store(flat, k, x)
        out = grid.zero
        for g in range(LANES // GROUP):
            out = jnp.where(grid.group == g, rolled(x, EDGE + GROUP * g, 1), out)
        store(own_flat, k, out)

    @pl.when((flags[0] & 1) == 1)
    def _():
        pack(grid, edge_groups(own, own_flat), True, odd_way)
        pack(grid, edge_groups(own, own_flat), False, even_way)

    @pl.when((flags[0] & 1) == 0)
    def _():
        pack(grid, edge_groups(own, own_flat), False, odd_way)
        pack(grid, edge_groups(own, own_flat), True, even_way)


def turn_kernel(flat, *refs):
    hbm, main, sem = refs[:4], refs[4], refs[5]
    copies = []
    for y in range(ROWS):
        for source, target in [(hbm[0].at[:, :, y, :], main.at[:LAME, y])] + [
            (hbm[1 + k].at[:, y, :], main.at[LAME + k, y]) for k in range(3)
        ]:
            copies.append(pltpu.make_async_copy(source, target, sem.at[len(copies)]))
            copies[-1].start()
    for copy in copies:
        copy.wait()


def speeds(grid, stress, speed, buoy, todo, put):
    sxx, syy, szz, sxy, sxz, syz = stress
    forth = [(VX, y) for c, y in todo if c == VX]
    back = [(c, y) for c, y in todo if c != VX]
    change = dict(zip(forth, grid.along_rows(grid.after, [(sxx, y) for _, y in forth])))
    change.update(zip(back, grid.along_rows(grid.before, [(sxy if c == VY else sxz, y) for c, y in back])))
    for y in range(ROWS):
        parts = [c for c in (VX, VY, VZ) if (c, y) in todo]
        if not parts:
            continue
        for t in range(SPAN):
            rate = RATE * buoy(y, t)
            for c in parts:
                a = change[c, y][t]
                if c == VX:
                    a = a + grid.by(sxy, y, t) + grid.bz(sxz, y, t)
                elif c == VY:
                    a = a + grid.fy(syy, y, t) + grid.bz(syz, y, t)
                else:
                    a = a + grid.by(syz, y, t) + grid.fz(szz, y, t)
                put(c, y, t, speed(c)(y, t) + rate * a)


def stresses(grid, rows, tiles, speed, stress, lame, shear, put):
    vx, vy, vz = [speed(c) for c in (VX, VY, VZ)]
    back = grid.along_rows(grid.before, [(vx, y) for y in rows])
    forth = grid.along_rows(grid.after, [(v, y) for v in (vy, vz) for y in rows])
    for i, y in enumerate(rows):
        for t in range(tiles):
            strain_x = back[i][t]
            strain_y = grid.by(vy, y, t)
            strain_z = grid.bz(vz, y, t)
            mu = RATE * shear(y, t)
            spread = (RATE * lame(y, t)) * (strain_x + strain_y + strain_z)
            two = mu + mu
            put(SXX, y, t, stress(SXX)(y, t) + (spread + two * strain_x))
            put(SYY, y, t, stress(SYY)(y, t) + (spread + two * strain_y))
            put(SZZ, y, t, stress(SZZ)(y, t) + (spread + two * strain_z))
            put(SXY, y, t, stress(SXY)(y, t) + mu * (grid.fy(vx, y, t) + forth[i][t]))
            put(SXZ, y, t, stress(SXZ)(y, t) + mu * (grid.fz(vx, y, t) + forth[len(rows) + i][t]))
            put(SYZ, y, t, stress(SYZ)(y, t) + mu * (grid.fz(vy, y, t) + grid.fy(vz, y, t)))


def flat_edge(grid, at, k):
    return grid.edge(grid.beside(at(1)), 0) if k == 0 else None


def partial_level(grid, flat, put):
    for k in range(2):
        x, y = flat(FLUX_X, k), flat(FLUX_Y, k)
        edge = flat_edge(grid, lambda q: flat(FLUX_X, q), k)
        spread = 0.5 * (grid.along(x, 1, edge) - grid.along(x, -1, edge))
        spread = spread + 0.5 * (grid.across(y, 1, 0.0) - grid.across(y, -1, 0.0))
        put(k, flat(LEVEL, k) - OCEAN_RATE * (flat(WET, k) * spread))


def cells(rows, tiles):
    return [(f, y, t) for f, y in rows for t in tiles]


class Message:
    def __init__(self, tiles):
        self.at = {which: i for i, which in enumerate(tiles)}
        self.base = len(tiles) * SUB
        self.size = self.base + 2 * SUB


ALL, INSIDE = range(SPAN), range(TILES)
FIRST = [
    Message(cells(rows, ALL))
    for rows in (SPEED_HIGH + STRESS_HIGH + BUOY_HIGH, SPEED_LOW + STRESS_LOW + BUOY_LOW)
]
LATER = [
    Message(cells(speed, INSIDE) + cells(rest, ALL))
    for speed, rest in ((SPEED_HIGH, STRESS_HIGH), (SPEED_LOW, STRESS_LOW))
]


def message_tiles(kind):
    return max(m.size for m in kind) // SUB


def send(kind, odd, field, line, even_way, odd_way):
    high, low = kind

    def fill(message, edge, out):
        for (f, y, t), at in message.at.items():
            store(out, at, field(f)(y, t))
        at = message.base
        for which in LINES:
            for k in range(2):
                out[at : at + 1, :] = line(which, k, edge)
                at += 1
        out[at : at + 6, :] = jnp.zeros((6, LANES), jnp.float32)
        tail = out.shape[0]
        if message.size < tail:
            out[message.size : tail, :] = jnp.zeros((tail - message.size, LANES), jnp.float32)

    @pl.when(odd)
    def _():
        fill(high, ROWS - 1, odd_way)
        fill(low, 0, even_way)

    @pl.when(jnp.logical_not(odd))
    def _():
        fill(high, ROWS - 1, even_way)
        fill(low, 0, odd_way)


class Received:
    def __init__(self, message, odd, if_odd, if_even):
        self.message, self.odd, self.if_odd, self.if_even = message, odd, if_odd, if_even

    def __call__(self, f, y, t):
        at = self.message.at[f, y, t]
        return jnp.where(self.odd, tile(self.if_odd, at), tile(self.if_even, at))

    def line(self, which, k):
        at = self.message.base + 2 * LINES.index(which) + k
        return jnp.where(self.odd, row(self.if_odd, at), row(self.if_even, at))


def received(kind, odd, even_in, odd_in):
    return Received(kind[0], odd, even_in, odd_in), Received(kind[1], odd, odd_in, even_in)


AROUND = ROWS + 4


def finish(grid, tiles, partial, stress, buoy, lo, hi, lo_buoy, hi_buoy, speed):
    sxy, syy, syz = [stress(f) for f in (SXY, SYY, SYZ)]

    def put(c, y, t, value):
        store(speed, (c * AROUND + y + 2) * SPAN + t, value)

    for t in range(SPAN):
        for c, f in ((VX, SXY), (VZ, SYZ)):
            two, one = lo(f, 6, t), lo(f, 7, t)
            rate = [RATE * buoy(y, t) for y in (0, 1, 7)]
            put(c, 0, t, partial(c, 0, t) + rate[0] * (two - 27.0 * one))
            put(c, 1, t, partial(c, 1, t) + rate[1] * one)
            put(c, 7, t, partial(c, 7, t) - rate[2] * hi(f, 0, t))
        h8, h9 = hi(SYY, 0, t), hi(SYY, 1, t)
        put(VY, 0, t, partial(VY, 0, t) + (RATE * buoy(0, t)) * lo(SYY, 7, t))
        put(VY, 6, t, partial(VY, 6, t) - (RATE * buoy(6, t)) * h8)
        put(VY, 7, t, partial(VY, 7, t) + (RATE * buoy(7, t)) * (27.0 * h8 - h9))
    for t in range(tiles):
        b2, b1 = RATE * lo_buoy(BUOY, 6, t), RATE * lo_buoy(BUOY, 7, t)
        b8, b9 = RATE * hi_buoy(BUOY, 0, t), RATE * hi_buoy(BUOY, 1, t)
        put(VX, -1, t, lo(VX, 7, t) - b1 * sxy(0, t))
        put(VY, -2, t, lo(VY, 6, t) - b2 * syy(0, t))
        put(VY, -1, t, lo(VY, 7, t) + b1 * (27.0 * syy(0, t) - syy(1, t)))
        put(VZ, -1, t, lo(VZ, 7, t) - b1 * syz(0, t))
        put(VX, 8, t, hi(VX, 0, t) + b8 * (sxy(6, t) - 27.0 * sxy(7, t)))
        put(VX, 9, t, hi(VX, 1, t) + b9 * sxy(7, t))
        put(VY, 8, t, hi(VY, 0, t) + b8 * syy(7, t))
        put(VZ, 8, t, hi(VZ, 0, t) + b8 * (syz(6, t) - 27.0 * syz(7, t)))
        put(VZ, 9, t, hi(VZ, 1, t) + b9 * syz(7, t))


def seafloor(grid, vz, y, floors, out, index):
    total = None
    for t in range(TILES):
        part = jnp.where(floors[0] == grid.depth[t], vz(y, t), 0.0)
        total = part if total is None else total + part
    out[index : index + 1, :] = jnp.sum(total, axis=0, keepdims=True)
    if len(floors) > 1:
        part = jnp.where(floors[1] == grid.depth[WINDOW], vz(y, WINDOW), 0.0)
        out[2 * SUB + index : 2 * SUB + index + 1, :] = jnp.sum(part, axis=0, keepdims=True)


def sea(grid, speed, level, now, fixed, line, lo, hi, sums, new, last):
    vz = speed(VZ)
    for y in range(ROWS):
        seafloor(grid, vz, y, [line(FLOOR, k, y) for k in range(2)], sums, y)
    ends = 1 if last else 2
    for y, side, at in ((-1, lo, ROWS), (ROWS, hi, ROWS + 1)):
        seafloor(grid, vz, y, [side.line(FLOOR, k) for k in range(ends)], sums, at)
    floors, beyond = [tile(sums, 0), grid.every_group(tile(sums, 2))], [tile(sums, 1), None]
    if not last:
        beyond[1] = grid.every_group(tile(sums, 3))
    sub = grid.sub
    levels, lows, highs = [], [], []
    for k in range(2):
        near = jnp.where(sub == 0, lo.line(FLUX_Y, k), jnp.where(sub == ROWS - 1, -hi.line(FLUX_Y, k), 0.0))
        levels.append(level(k) + fixed(WET, k) * (UPLIFT * floors[k] + (0.5 * OCEAN_RATE) * near))
        new(LEVEL, k, levels[k])
        if k < ends:
            for side, at, y, sign, out in ((lo, 0, 0, -1.0, lows), (hi, 1, ROWS - 1, 1.0, highs)):
                mine = (sign * 0.5 * OCEAN_RATE) * line(FLUX_Y, k, y)
                rest = UPLIFT * beyond[k][at : at + 1, :] + mine
                out.append(side.line(None, k) + side.line(WET, k) * rest)
    for k in range(ends):
        wet, deep = fixed(WET, k), fixed(DEPTH, k)
        edge = flat_edge(grid, lambda q: levels[q], k)
        slope_x = 0.5 * (grid.along(levels[k], 1, edge) - grid.along(levels[k], -1, edge))
        slope_y = 0.5 * (grid.across(levels[k], 1, highs[k]) - grid.across(levels[k], -1, lows[k]))
        for which, slope in ((FLUX_X, slope_x), (FLUX_Y, slope_y)):
            x = now(which, k)
            edge = flat_edge(grid, lambda q: now(which, q), k)
            laplace = grid.along(x, 1, edge) + grid.along(x, -1, edge) - 4.0 * x
            laplace = laplace + grid.across(x, 1, hi.line(which, k)) + grid.across(x, -1, lo.line(which, k))
            new(which, k, wet * (x - OCEAN_RATE * deep * slope + VISCOUS * laplace))
    return levels


def press(grid, levels, fixed, line, pressure):
    for k in range(2):
        store(pressure, k, LOADING * fixed(WET, k) * levels[k])

    def load(y, t):
        k = 1 if t == WINDOW else 0
        return jnp.where(line(FLOOR, k, y) == grid.depth[t], row(pressure, k * ROWS + y), 0.0)

    return load


def edge_index(c, y):
    return OPEN.index((c, y)) * SPAN


def block_index(c, y):
    return (c * ROWS + y) * SPAN


def start_kernel(
    flags, before, after, main, flat, own, own_flat, even_in, odd_in,
    windows, flat_windows, partial, level, even_way, odd_way,
):
    grid = Grid(flags[2], before, after)
    odd = (flags[0] & 1) == 1
    for f in range(0, FIELDS, 2):
        for q in range(0, ROWS, 2):
            places = [h * ROWS + y for y in (q, q + 1) for h in (f, f + 1)]
            items = [tile(own, p) for p in places]
            for p, x in zip(places, unpack(grid, items, odd, even_in, odd_in, (f * ROWS // 2 + q) // 2)):
                store(windows, p, x)
    items = [tile(own_flat, k) for k in range(6)]
    base = FIELDS * ROWS // 4
    for k, x in enumerate(unpack(grid, items[:4], odd, even_in, odd_in, base)):
        store(flat_windows, k, x)
    for k, x in enumerate(unpack(grid, items[4:] * 2, odd, even_in, odd_in, base + 1)[:2]):
        store(flat_windows, 4 + k, x)

    field = fields_of(main, windows)
    speeds(
        grid, [inside(field(f)) for f in range(SXX, SYZ + 1)], field, field(BUOY), OPEN,
        lambda c, y, t, value: store(partial, edge_index(c, y) + t, value),
    )
    flats = (flat, flat_windows)
    partial_level(grid, lambda f, k: tile(flats[k], f), lambda k, value: store(level, k, value))

    def rows_of(f):
        return (lambda y, t: tile(partial, edge_index(f, y) + t)) if f < 3 else field(f)

    def line(which, k, y):
        return row(level, k * ROWS + y) if which is None else row(flats[k], which * ROWS + y)

    send(FIRST, (flags[1] & 1) == 1, rows_of, line, even_way, odd_way)


def start_rest_kernel(flags, before, after, main, windows, speed_out, stress_out):
    grid = Grid(flags[2], before, after)
    field = fields_of(main, windows)
    speeds(
        grid, [inside(field(f)) for f in range(SXX, SYZ + 1)], field, field(BUOY), CLOSED,
        lambda c, y, t, value: store(speed_out, block_index(c, y) + t, value),
    )
    stresses(
        grid, INNER, SPAN, block_reader(speed_out, VX), field,
        field(LAME), field(SHEAR),
        lambda f, y, t, value: store(stress_out, block_index(f - SXX, y) + t, value),
    )


def block_reader(ref, least):
    return lambda f: lambda y, t, *start: tile(ref, block_index(f - least, y) + t, *start)


def speed_reader(around, block):
    def speed(c):
        def read(y, t, *start):
            if (c, y) in CLOSED:
                return tile(block, block_index(c, y) + t, *start)
            return tile(around, (c * AROUND + y + 2) * SPAN + t, *start)

        return read

    return speed


def middle_kernel(
    flags, before, after, main, windows, flat, flat_windows, partial, level, speed_in, stress_in,
    even_in, odd_in,
    speed_out, stress_out, ocean, partial_out, level_out, even_way, odd_way,
    sums, pressure,
):
    grid = Grid(flags[2], before, after)
    odd = (flags[1] & 1) == 1
    lo, hi = received(FIRST, odd, even_in, odd_in)
    field = fields_of(main, windows)
    finish(
        grid, SPAN, lambda c, y, t: tile(partial, edge_index(c, y) + t), field, field(BUOY), lo, hi, lo, hi, speed_out
    )
    speed = speed_reader(speed_out, speed_in)
    flats = (flat, flat_windows)
    fixed = lambda f, k: tile(flats[k], f)
    line = lambda f, k, y: row(flats[k], f * ROWS + y)

    def new(f, k, value):
        store(ocean, 3 * k + f, value)

    levels = sea(grid, speed, lambda k: tile(level, k), fixed, fixed, line, lo, hi, sums, new, False)
    load = press(grid, levels, fixed, line, pressure)

    def put(f, y, t, value):
        store(stress_out, block_index(f - SXX, y) + t, value - load(y, t) if f == SZZ else value)

    stresses(grid, OUTER, SPAN, speed, field, field(LAME), field(SHEAR), put)
    for f in range(SXX, SYZ + 1):
        for y in INNER:
            for t in range(SPAN):
                put(f, y, t, tile(stress_in, block_index(f - SXX, y) + t))
    stress = block_reader(stress_out, SXX)
    speeds(
        grid, [inside(stress(f)) for f in range(SXX, SYZ + 1)], speed, field(BUOY), OPEN,
        lambda c, y, t, value: store(partial_out, edge_index(c, y) + t, value),
    )
    moving = lambda f, k: tile(flats[k], f) if f >= DEPTH else tile(ocean, 3 * k + f)
    partial_level(grid, moving, lambda k, value: store(level_out, k, value))

    def rows_of(f):
        return (lambda y, t: tile(partial_out, edge_index(f, y) + t)) if f < 3 else stress(f)

    def line_out(which, k, y):
        if which is None:
            return row(level_out, k * ROWS + y)
        return line(which, k, y) if which >= DEPTH else row(ocean, (3 * k + which) * ROWS + y)

    send(LATER, odd, rows_of, line_out, even_way, odd_way)


def middle_rest_kernel(flags, before, after, main, windows, around, speed_in, stress_in, speed_out, stress_out):
    grid = Grid(flags[2], before, after)
    field = fields_of(main, windows)
    stress = block_reader(stress_in, SXX)
    speeds(
        grid, [inside(stress(f)) for f in range(SXX, SYZ + 1)], speed_reader(around, speed_in), field(BUOY), CLOSED,
        lambda c, y, t, value: store(speed_out, block_index(c, y) + t, value),
    )
    stresses(
        grid, INNER, TILES, block_reader(speed_out, VX), stress,
        field(LAME), field(SHEAR),
        lambda f, y, t, value: store(stress_out, block_index(f - SXX, y) + t, value),
    )


def last_kernel(
    flags, before, after, main, windows, flat, flat_windows, stress_in, ocean_in, partial, level, speed_in, inner_in,
    even_first, odd_first, even_in, odd_in,
    wave_hbm, ocean_out,
    sums, pressure, around, wave, sem,
):
    grid = Grid(flags[2], before, after)
    odd = (flags[1] & 1) == 1
    lo, hi = received(LATER, odd, even_in, odd_in)
    lo_buoy, hi_buoy = received(FIRST, odd, even_first, odd_first)
    field = fields_of(main, windows)
    stress = block_reader(stress_in, SXX)
    finish(
        grid, TILES, lambda c, y, t: tile(partial, edge_index(c, y) + t), stress, field(BUOY),
        lo, hi, lo_buoy, hi_buoy, around,
    )
    speed = speed_reader(around, speed_in)
    sent = []

    def copy(source, target):
        sent.append(pltpu.make_async_copy(source, target, sem.at[len(sent)]))
        sent[-1].start()

    def copy_row(ref, index, f, y):
        copy(ref.at[index * SUB : (index + TILES) * SUB, :], wave_hbm.at[f, :, y, :])

    for c, y in CLOSED:
        copy_row(speed_in, block_index(c, y), c, y)
    for c, y in OPEN:
        copy_row(around, (c * AROUND + y + 2) * SPAN, c, y)
    flats = (flat, flat_windows)
    fixed = lambda f, k: tile(flats[k], f)

    def line(f, k, y):
        return row(flats[k], f * ROWS + y) if f >= DEPTH else row(ocean_in, (3 * k + f) * ROWS + y)

    def new(f, k, value):
        if k == 0:
            store(ocean_out, f, value)

    levels = sea(
        grid, speed, lambda k: tile(level, k), lambda f, k: tile(ocean_in, 3 * k + f), fixed, line, lo, hi, sums, new, True
    )
    load = press(grid, levels, fixed, line, pressure)

    def put(f, y, t, value):
        size = TILES * SUB * ROWS
        if f == SZZ:
            value = value - load(y, t)
        wave[pl.ds((f - SXX) * size + t * SUB * ROWS + y, SUB, stride=ROWS), :] = value

    for f in range(SXX, SYZ + 1):
        for y in INNER:
            for t in range(TILES):
                put(f, y, t, tile(inner_in, block_index(f - SXX, y) + t))
    stresses(grid, OUTER, TILES, speed, stress, field(LAME), field(SHEAR), put)
    for f in range(SXX, SYZ + 1):
        size = TILES * SUB
        for z in range(0, size, size // 2):
            at = ((f - SXX) * size + z) * ROWS
            target = wave_hbm.at[f, z : z + size // 2].reshape(size // 2 * ROWS, LANES)
            copy(wave.at[at : at + size // 2 * ROWS, :], target)
    for one in sent:
        one.wait()


IN_VMEM = pl.BlockSpec(memory_space=pltpu.VMEM)
IN_SMEM = pl.BlockSpec(memory_space=pltpu.SMEM)
IN_HBM = pl.BlockSpec(memory_space=pltpu.HBM)


def call(kernel, tiles, scratch, *arguments, flags=None, place=IN_VMEM, out_places=None, work=1):
    specs = place if isinstance(place, list) else [place] * len(arguments)
    if flags is not None:
        arguments, specs = (flags, *arguments), [IN_SMEM] + specs
    moved = sum(x.size for x in arguments) + sum(n for n in tiles if isinstance(n, int)) * SUB * LANES
    return pl.pallas_call(
        kernel,
        out_shape=[n if hasattr(n, "dtype") else jax.ShapeDtypeStruct((n * SUB, LANES), jnp.float32) for n in tiles],
        in_specs=specs,
        out_specs=out_places or [IN_VMEM] * len(tiles),
        scratch_shapes=scratch,
        cost_estimate=pl.CostEstimate(flops=work * 1000000, bytes_accessed=4 * moved, transcendentals=0),
        compiler_params=pltpu.CompilerParams(vmem_limit_bytes=24 * 1024 * 1024),
    )(*arguments)


def planes(n):
    return pltpu.VMEM((n * SUB, LANES), jnp.float32)


def swap(x, axis, start):
    pairs = [(i, i + 1) for i in range(start, lax.axis_size(axis) - 1, 2)]
    return lax.ppermute(x, axis, pairs + [(j, i) for i, j in pairs])


def local(*arguments):
    ocean_state = arguments[4]
    inputs = [pltpu.with_memory_space_constraint(x, pltpu.HBM) for x in arguments]
    flags = jnp.stack([lax.axis_index("gx"), lax.axis_index("gy"), 0])
    matrix = jax.ShapeDtypeStruct((2 * LANES, SPAN * LANES), jnp.bfloat16)
    cells4 = jax.ShapeDtypeStruct((FIELDS, ROWS, TILES * SUB, LANES), jnp.float32)

    edge = FIELDS * ROWS // 4 + 2
    before, after, flat, own, own_flat, even_way, odd_way = call(
        edges_kernel, [matrix, matrix, 6, FIELDS * ROWS, 6, edge, edge],
        [pltpu.VMEM((FIELDS, *arguments[1].shape), jnp.float32), planes(FIELDS * SUB)]
        + [pltpu.VMEM(x.shape, x.dtype) for x in inputs[4:]] + [pltpu.SemaphoreType.DMA((FIELDS + 4,))],
        *inputs, flags=flags, place=IN_HBM,
    )
    even_in, odd_in = swap(even_way, "gx", 0), swap(odd_way, "gx", 1)
    (main,) = call(
        turn_kernel, [cells4], [pltpu.SemaphoreType.DMA((4 * ROWS,))], flat, *inputs[:4],
        place=[IN_VMEM] + [IN_HBM] * 4, work=4,
    )
    main = main.reshape(-1, LANES)
    first, later = [message_tiles(kind) for kind in (FIRST, LATER)]
    edges, block = len(OPEN) * SPAN, ROWS * SPAN
    windows, flat_windows, partial, level, even_way, odd_way = call(
        start_kernel, [FIELDS * ROWS, 6, edges, 2, first, first], [],
        before, after, main, flat, own, own_flat, even_in, odd_in, flags=flags,
    )
    y_first = swap(even_way, "gy", 0), swap(odd_way, "gy", 1)
    speed, inner = call(start_rest_kernel, [3 * block, 6 * block], [], before, after, main, windows, flags=flags, work=4)
    around, stress, ocean, partial, level, even_way, odd_way = call(
        middle_kernel, [3 * AROUND * SPAN, 6 * block, 6, edges, 2, later, later], [planes(4), planes(2)],
        before, after, main, windows, flat, flat_windows, partial, level, speed, inner, *y_first, flags=flags,
    )
    y_in = swap(even_way, "gy", 0), swap(odd_way, "gy", 1)
    speed, inner = call(
        middle_rest_kernel, [3 * block, 6 * block], [], before, after, main, windows, around, speed, stress, flags=flags, work=4
    )
    copies = len(CLOSED) + len(OPEN) + 2 * 6
    wave_out, ocean_out = call(
        last_kernel, [jax.ShapeDtypeStruct(arguments[0].shape, jnp.float32), 3],
        [
            planes(4), planes(2), planes(3 * AROUND * SPAN), planes(6 * ROWS * TILES),
            pltpu.SemaphoreType.DMA((copies,)),
        ],
        before, after, main, windows, flat, flat_windows, stress, ocean, partial, level, speed, inner, *y_first, *y_in,
        flags=flags, out_places=[IN_HBM, IN_VMEM],
    )
    return wave_out, ocean_out.reshape(ocean_state.shape)


def solution(mesh):
    in_specs = (
        P(None, None, "gy", "gx"),
        P(None, "gy", "gx"),
        P(None, "gy", "gx"),
        P(None, "gy", "gx"),
        P(None, "gy", "gx"),
        P("gy", "gx"),
        P("gy", "gx"),
        P("gy", "gx"),
    )
    out_specs = (P(None, None, "gy", "gx"), P(None, "gy", "gx"))
    return jax.shard_map(local, mesh=mesh, in_specs=in_specs, out_specs=out_specs, check_vma=False)
```

```python
import jax
import jax.numpy as jnp
from jax import lax
from jax.experimental import pallas as pl
from jax.experimental.pallas import tpu as pltpu
from jax.sharding import PartitionSpec as P

RATE = 0.3 / 24.0
OCEAN_RATE = 0.3
UPLIFT = 0.5
LOADING = 0.5
VISCOUS = 0.1

ROWS = 8
SUB = 8
LANES = 128
EDGE = 8
GROUP = 2 * EDGE
TILES = 4
HALF = TILES * GROUP
SPAN = TILES + 1
WINDOW = TILES

LEVEL, FLUX_X, FLUX_Y, DEPTH, FLOOR, WET = range(6)
VX, VY, VZ, SXX, SYY, SZZ, SXY, SXZ, SYZ, LAME, SHEAR, BUOY = range(12)
FIELDS = 12

OPEN = ((VX, 0), (VX, 1), (VX, 7), (VY, 0), (VY, 6), (VY, 7), (VZ, 0), (VZ, 1), (VZ, 7))
CLOSED = tuple((c, y) for y in range(ROWS) for c in (VX, VY, VZ) if (c, y) not in OPEN)
INNER = (3, 4)
OUTER = tuple(y for y in range(ROWS) if y not in INNER)

SPEED_HIGH = ((VX, 7), (VY, 6), (VY, 7), (VZ, 7))
SPEED_LOW = ((VX, 0), (VX, 1), (VY, 0), (VZ, 0), (VZ, 1))
STRESS_HIGH = ((SXY, 6), (SXY, 7), (SYY, 7), (SYZ, 6), (SYZ, 7))
STRESS_LOW = ((SXY, 0), (SYY, 0), (SYY, 1), (SYZ, 0))
BUOY_HIGH = ((BUOY, 6), (BUOY, 7))
BUOY_LOW = ((BUOY, 0), (BUOY, 1))
LINES = (None, WET, FLOOR, FLUX_X, FLUX_Y)


def rolled(x, shift, axis):
    shift %= x.shape[axis]
    return x if shift == 0 else pltpu.roll(x, shift, axis)


def tile(ref, index, start=None):
    if start is None:
        return ref[index * SUB : (index + 1) * SUB, :]
    return ref[pl.ds(start + index * SUB, SUB), :]


def row(ref, index):
    return ref[index : index + 1, :]


def store(ref, index, value):
    ref[index * SUB : (index + 1) * SUB, :] = value


def split(x, parts):
    out = []
    for part in range(parts):
        out.append(x.astype(jnp.bfloat16))
        if part + 1 < parts:
            x = x - out[-1].astype(jnp.float32)
    return jnp.concatenate(out, axis=1)


def minus(a, b):
    if b is None:
        return a
    return -b if a is None else a - b


def near_far(a, b, c, d):
    near, far = 27.0 * minus(a, b), minus(c, d)
    return near if c is None and d is None else near - far


class Grid:
    def __init__(self, origin=None, before=None, after=None):
        self.origin, self.before, self.after = origin, before, after
        self.sub = lax.broadcasted_iota(jnp.int32, (SUB, LANES), 0)
        self.lane = lax.broadcasted_iota(jnp.int32, (SUB, LANES), 1)
        self.first = self.lane % GROUP < EDGE
        self.left = self.lane < HALF
        self.group = self.lane // GROUP
        self.zero = jnp.zeros((SUB, LANES), jnp.float32)
        depth = [self.sub + SUB * t for t in range(TILES)] + [self.sub + SUB * (self.group % TILES)]
        self.depth = [d.astype(jnp.float32) for d in depth]

    def beside(self, window):
        return jnp.where(self.first, window, rolled(window, HALF, 1))

    def edge(self, beside, t):
        return None if t == WINDOW else rolled(beside, LANES - EDGE - GROUP * t, 1)

    def along(self, x, offset, edge):
        if edge is not None:
            lane = self.lane
            keep = {-1: lane == LANES - 1, -2: lane >= LANES - 2, 1: lane == 0, 2: lane <= 1}[offset]
            x = jnp.where(keep, edge, x)
        return rolled(x, -offset, 1)

    def down(self, field, y, t, offset):
        if t < WINDOW:
            x = field(y, t, self.origin + offset)
            if t == 0 and offset < 0:
                return jnp.where(self.sub >= -offset, x, 0.0)
            if t == TILES - 1 and offset > 0:
                return jnp.where(self.sub < SUB - offset, x, 0.0)
            return x
        x, at = field(y, t), self.lane % HALF
        if offset < 0:
            beyond, far = jnp.where(at >= GROUP, rolled(x, GROUP, 1), 0.0), self.sub >= SUB + offset
        else:
            beyond, far = jnp.where(at < HALF - GROUP, rolled(x, -GROUP, 1), 0.0), self.sub < offset
        return rolled(jnp.where(far, beyond, x), -offset, 0)

    def fz(self, field, y, t):
        down = lambda offset: self.down(field, y, t, offset)
        return near_far(down(1), field(y, t), down(2), down(-1))

    def bz(self, field, y, t):
        down = lambda offset: self.down(field, y, t, offset)
        return near_far(field(y, t), down(-1), down(1), down(-2))

    def along_rows(self, matrix, rows):
        main = split(jnp.concatenate([f(y, t) for f, y in rows for t in range(TILES)], axis=0), 2)
        sides = [f(y, WINDOW) for f, y in rows]
        side = split(jnp.concatenate(sides + sides[: len(sides) % 2], axis=0), 2)
        main = jnp.dot(main, matrix[:, :LANES], preferred_element_type=jnp.float32)
        side = jnp.dot(side, matrix[...], preferred_element_type=jnp.float32)
        out = []
        for i in range(len(rows)):
            part = side[i * SUB : (i + 1) * SUB, :]
            parts = [part[:, t * LANES : (t + 1) * LANES] for t in range(SPAN)]
            tiles = [
                main[(i * TILES + t) * SUB : (i * TILES + t + 1) * SUB, :] + parts[1 + t] for t in range(TILES)
            ]
            out.append(tiles + parts[:1])
        return out

    def fy(self, field, y, t):
        return near_far(field(y + 1, t), field(y, t), field(y + 2, t), field(y - 1, t))

    def by(self, field, y, t):
        return near_far(field(y, t), field(y - 1, t), field(y + 1, t), field(y - 2, t))

    def windows(self, own, from_left, from_right):
        return jnp.where(
            self.left, jnp.where(self.first, from_left, own), jnp.where(self.first, own, from_right)
        )

    def every_group(self, x):
        for shift in (GROUP, 2 * GROUP):
            x = x + jnp.where(self.lane % HALF >= shift, rolled(x, shift, 1), rolled(x, shift - HALF, 1))
        return x

    def across(self, x, offset, beside):
        end = 0 if offset < 0 else ROWS - 1
        return jnp.where(self.sub == end, beside, rolled(x, -offset, 0))


def inside(field):
    return lambda y, t, *start: field(y, t, *start) if 0 <= y < ROWS else None


def fields_of(main, windows):
    def field(f):
        def read(y, t, *start):
            return tile(windows, f * ROWS + y) if t == WINDOW else tile(main, (f * ROWS + y) * TILES + t, *start)

        return read

    return field


def pack(grid, groups, to_right, out):
    for index, (a, b, c, d) in enumerate(groups):
        if to_right:
            one, two = jnp.where(grid.first, a, rolled(b, EDGE, 1)), jnp.where(grid.first, c, rolled(d, EDGE, 1))
        else:
            one, two = jnp.where(grid.first, rolled(b, -EDGE, 1), a), jnp.where(grid.first, rolled(d, -EDGE, 1), c)
        store(out, index, jnp.where(grid.left, one, two))


def edge_groups(own, own_flat):
    groups = [
        [tile(own, h * ROWS + y) for y in (q, q + 1) for h in (f, f + 1)]
        for f in range(0, FIELDS, 2)
        for q in range(0, ROWS, 2)
    ]
    flat = [tile(own_flat, k) for k in range(6)]
    return groups + [flat[:4], flat[4:] * 2]


def unpack(grid, items, odd, even_in, odd_in, index):
    x, y = tile(even_in, index), tile(odd_in, index)
    before, after = jnp.where(odd, x, y), jnp.where(odd, y, x)
    befores = [before, rolled(before, -EDGE, 1), rolled(before, HALF, 1), rolled(before, HALF - EDGE, 1)]
    afters = [rolled(after, HALF, 1), rolled(after, HALF + EDGE, 1), after, rolled(after, EDGE, 1)]
    return [grid.windows(*three) for three in zip(items, befores, afters)]


def difference_matrix(out, weights, offsets):
    shape = (LANES, LANES)
    k, n = [lax.broadcasted_iota(jnp.int32, shape, axis) for axis in range(2)]

    def weight(apart):
        total = jnp.zeros(shape, jnp.float32)
        for w, offset in zip(weights, offsets):
            total = jnp.where(apart == offset, w, total)
        return total

    inner, left = k % GROUP, k < HALF
    column = jnp.where(left, inner - EDGE, LANES - EDGE + inner)
    outside = (left & (inner < EDGE)) | (jnp.logical_not(left) & (inner >= EDGE))
    beside = jnp.where(outside, weight(n - column), 0.0)
    parts = [weight(n - k)]
    parts += [jnp.where(k % HALF // GROUP == t, beside, 0.0) for t in range(TILES)]
    for p, x in enumerate(parts):
        for half in range(2):
            out[half * LANES : (half + 1) * LANES, p * LANES : (p + 1) * LANES] = x.astype(jnp.bfloat16)


def picker(t):
    k, n = [lax.broadcasted_iota(jnp.int32, (LANES, LANES), axis) for axis in range(2)]
    column = (n % GROUP - EDGE) % LANES
    one = jnp.where((n % HALF // GROUP == t) & (k == column), 1.0, 0.0).astype(jnp.bfloat16)
    return jnp.concatenate([one] * 2, axis=0)


def edges_kernel(flags, *refs):
    hbm, refs = refs[:8], refs[8:]
    (before, after, main, flat, own, own_flat, even_way, odd_way, early_even, early_odd), refs = refs[:10], refs[10:]
    fields, picked, low, high, ocean, deep, floor, wet, sem = refs
    sent = []

    def copy(source, target):
        sent.append(pltpu.make_async_copy(source, target, sem.at[len(sent)]))
        sent[-1].start()
        return sent[-1]

    whole = [copy(x, fields.at[f]) for f, x in enumerate([hbm[0].at[f] for f in range(9)] + list(hbm[1:4]))]
    rest = [copy(hbm[4 + k], x) for k, x in enumerate((ocean, deep, floor, wet))]
    for rows, out in ((BUOY_LOW, low), (BUOY_HIGH, high)):
        for k, (f, y) in enumerate(rows):
            rest.append(copy(hbm[f - SHEAR + 2].at[:, y, :], out.at[k * TILES * SUB : (k + 1) * TILES * SUB, :]))
    turned = []
    for y in range(ROWS):
        turned.append(copy(hbm[0].at[:, :, y, :], main.at[:LAME, y]))
        turned += [copy(hbm[1 + k].at[:, y, :], main.at[LAME + k, y]) for k in range(3)]
    difference_matrix(before, (27.0, -27.0, -1.0, 1.0), (0, 1, -1, 2))
    difference_matrix(after, (27.0, -27.0, -1.0, 1.0), (-1, 0, -2, 1))
    pickers = [picker(t) for t in range(TILES)]
    grid = Grid()
    for one in whole:
        one.wait()
    size = SUB * ROWS
    for half in range(2):
        mine = range(half * FIELDS // 2, (half + 1) * FIELDS // 2)
        total = None
        for t in range(TILES):
            x = [fields[f, t * SUB : (t + 1) * SUB].reshape(size, LANES) for f in mine]
            part = jnp.dot(split(jnp.concatenate(x, axis=0), 2), pickers[t], preferred_element_type=jnp.float32)
            total = part if total is None else total + part
        picked[mine[0] * size : (mine[-1] + 1) * size, :] = total
        for f in mine:
            for y in range(ROWS):
                store(own, f * ROWS + y, picked[pl.ds(f * size + y, SUB, stride=ROWS), :])
    for one in rest:
        one.wait()
    planes = [ocean[k] for k in range(3)] + [deep[...]]
    planes += [floor[...].astype(jnp.float32), wet[...].astype(jnp.float32)]
    for k, x in enumerate(planes):
        store(flat, k, x)
        out = grid.zero
        for g in range(LANES // GROUP):
            out = jnp.where(grid.group == g, rolled(x, EDGE + GROUP * g, 1), out)
        store(own_flat, k, out)

    @pl.when((flags[0] & 1) == 1)
    def _():
        pack(grid, edge_groups(own, own_flat), True, odd_way)
        pack(grid, edge_groups(own, own_flat), False, even_way)

    @pl.when((flags[0] & 1) == 0)
    def _():
        pack(grid, edge_groups(own, own_flat), False, odd_way)
        pack(grid, edge_groups(own, own_flat), True, even_way)

    odd = (flags[1] & 1) == 1
    for index in range(2 * TILES):
        a, b = tile(low, index), tile(high, index)
        store(early_even, index, jnp.where(odd, a, b))
        store(early_odd, index, jnp.where(odd, b, a))
    for one in turned:
        one.wait()


def speeds(grid, stress, speed, buoy, todo, put):
    sxx, syy, szz, sxy, sxz, syz = stress
    forth = [(VX, y) for c, y in todo if c == VX]
    back = [(c, y) for c, y in todo if c != VX]
    change = dict(zip(forth, grid.along_rows(grid.after, [(sxx, y) for _, y in forth])))
    change.update(zip(back, grid.along_rows(grid.before, [(sxy if c == VY else sxz, y) for c, y in back])))
    for y in range(ROWS):
        parts = [c for c in (VX, VY, VZ) if (c, y) in todo]
        if not parts:
            continue
        for t in range(SPAN):
            rate = RATE * buoy(y, t)
            for c in parts:
                a = change[c, y][t]
                if c == VX:
                    a = a + grid.by(sxy, y, t) + grid.bz(sxz, y, t)
                elif c == VY:
                    a = a + grid.fy(syy, y, t) + grid.bz(syz, y, t)
                else:
                    a = a + grid.by(syz, y, t) + grid.fz(szz, y, t)
                put(c, y, t, speed(c)(y, t) + rate * a)


def stresses(grid, rows, tiles, speed, stress, lame, shear, put, done=lambda t: None):
    vx, vy, vz = [speed(c) for c in (VX, VY, VZ)]
    back = grid.along_rows(grid.before, [(vx, y) for y in rows])
    forth = grid.along_rows(grid.after, [(v, y) for v in (vy, vz) for y in rows])
    for t in range(tiles):
        for i, y in enumerate(rows):
            strain_x = back[i][t]
            strain_y = grid.by(vy, y, t)
            strain_z = grid.bz(vz, y, t)
            mu = RATE * shear(y, t)
            spread = (RATE * lame(y, t)) * (strain_x + strain_y + strain_z)
            two = mu + mu
            put(SXX, y, t, stress(SXX)(y, t) + (spread + two * strain_x))
            put(SYY, y, t, stress(SYY)(y, t) + (spread + two * strain_y))
            put(SZZ, y, t, stress(SZZ)(y, t) + (spread + two * strain_z))
            put(SXY, y, t, stress(SXY)(y, t) + mu * (grid.fy(vx, y, t) + forth[i][t]))
            put(SXZ, y, t, stress(SXZ)(y, t) + mu * (grid.fz(vx, y, t) + forth[len(rows) + i][t]))
            put(SYZ, y, t, stress(SYZ)(y, t) + mu * (grid.fz(vy, y, t) + grid.fy(vz, y, t)))
        done(t)


def flat_edge(grid, at, k):
    return grid.edge(grid.beside(at(1)), 0) if k == 0 else None


def partial_level(grid, flat, put):
    for k in range(2):
        x, y = flat(FLUX_X, k), flat(FLUX_Y, k)
        edge = flat_edge(grid, lambda q: flat(FLUX_X, q), k)
        spread = 0.5 * (grid.along(x, 1, edge) - grid.along(x, -1, edge))
        spread = spread + 0.5 * (grid.across(y, 1, 0.0) - grid.across(y, -1, 0.0))
        put(k, flat(LEVEL, k) - OCEAN_RATE * (flat(WET, k) * spread))


def cells(rows, tiles):
    return [(f, y, t) for f, y in rows for t in tiles]


class Message:
    def __init__(self, tiles):
        self.at = {which: i for i, which in enumerate(tiles)}
        self.base = len(tiles) * SUB
        self.size = self.base + 2 * SUB


ALL, INSIDE = range(SPAN), range(TILES)
SIDES = (WINDOW,)
EARLY = [{which: i for i, which in enumerate(cells(rows, INSIDE))} for rows in (BUOY_HIGH, BUOY_LOW)]
FIRST = [
    Message(cells(rows, ALL) + cells(buoy, SIDES))
    for rows, buoy in ((SPEED_HIGH + STRESS_HIGH, BUOY_HIGH), (SPEED_LOW + STRESS_LOW, BUOY_LOW))
]
LATER = [
    Message(cells(speed, INSIDE) + cells(rest, ALL))
    for speed, rest in ((SPEED_HIGH, STRESS_HIGH), (SPEED_LOW, STRESS_LOW))
]


def message_tiles(kind):
    return max(m.size for m in kind) // SUB


def send(kind, odd, field, line, even_way, odd_way):
    high, low = kind

    def fill(message, edge, out):
        for (f, y, t), at in message.at.items():
            store(out, at, field(f)(y, t))
        at = message.base
        for which in LINES:
            for k in range(2):
                out[at : at + 1, :] = line(which, k, edge)
                at += 1
        out[at : at + 6, :] = jnp.zeros((6, LANES), jnp.float32)
        tail = out.shape[0]
        if message.size < tail:
            out[message.size : tail, :] = jnp.zeros((tail - message.size, LANES), jnp.float32)

    @pl.when(odd)
    def _():
        fill(high, ROWS - 1, odd_way)
        fill(low, 0, even_way)

    @pl.when(jnp.logical_not(odd))
    def _():
        fill(high, ROWS - 1, even_way)
        fill(low, 0, odd_way)


class Received:
    def __init__(self, message, odd, if_odd, if_even):
        self.message, self.odd, self.if_odd, self.if_even = message, odd, if_odd, if_even

    def __call__(self, f, y, t):
        at = self.message.at[f, y, t]
        return jnp.where(self.odd, tile(self.if_odd, at), tile(self.if_even, at))

    def line(self, which, k):
        at = self.message.base + 2 * LINES.index(which) + k
        return jnp.where(self.odd, row(self.if_odd, at), row(self.if_even, at))


def received(kind, odd, even_in, odd_in):
    return Received(kind[0], odd, even_in, odd_in), Received(kind[1], odd, odd_in, even_in)


def early(odd, even_in, odd_in, later):
    def reader(at, if_odd, if_even, rest):
        def read(f, y, t):
            if (f, y, t) not in at:
                return rest(f, y, t)
            return jnp.where(odd, tile(if_odd, at[f, y, t]), tile(if_even, at[f, y, t]))

        return read

    return reader(EARLY[0], even_in, odd_in, later[0]), reader(EARLY[1], odd_in, even_in, later[1])


AROUND = ROWS + 4


def finish(grid, tiles, partial, stress, buoy, lo, hi, lo_buoy, hi_buoy, speed):
    sxy, syy, syz = [stress(f) for f in (SXY, SYY, SYZ)]

    def put(c, y, t, value):
        store(speed, (c * AROUND + y + 2) * SPAN + t, value)

    for t in range(SPAN):
        for c, f in ((VX, SXY), (VZ, SYZ)):
            two, one = lo(f, 6, t), lo(f, 7, t)
            rate = [RATE * buoy(y, t) for y in (0, 1, 7)]
            put(c, 0, t, partial(c, 0, t) + rate[0] * (two - 27.0 * one))
            put(c, 1, t, partial(c, 1, t) + rate[1] * one)
            put(c, 7, t, partial(c, 7, t) - rate[2] * hi(f, 0, t))
        h8, h9 = hi(SYY, 0, t), hi(SYY, 1, t)
        put(VY, 0, t, partial(VY, 0, t) + (RATE * buoy(0, t)) * lo(SYY, 7, t))
        put(VY, 6, t, partial(VY, 6, t) - (RATE * buoy(6, t)) * h8)
        put(VY, 7, t, partial(VY, 7, t) + (RATE * buoy(7, t)) * (27.0 * h8 - h9))
    for t in range(tiles):
        b2, b1 = RATE * lo_buoy(BUOY, 6, t), RATE * lo_buoy(BUOY, 7, t)
        b8, b9 = RATE * hi_buoy(BUOY, 0, t), RATE * hi_buoy(BUOY, 1, t)
        put(VX, -1, t, lo(VX, 7, t) - b1 * sxy(0, t))
        put(VY, -2, t, lo(VY, 6, t) - b2 * syy(0, t))
        put(VY, -1, t, lo(VY, 7, t) + b1 * (27.0 * syy(0, t) - syy(1, t)))
        put(VZ, -1, t, lo(VZ, 7, t) - b1 * syz(0, t))
        put(VX, 8, t, hi(VX, 0, t) + b8 * (sxy(6, t) - 27.0 * sxy(7, t)))
        put(VX, 9, t, hi(VX, 1, t) + b9 * sxy(7, t))
        put(VY, 8, t, hi(VY, 0, t) + b8 * syy(7, t))
        put(VZ, 8, t, hi(VZ, 0, t) + b8 * (syz(6, t) - 27.0 * syz(7, t)))
        put(VZ, 9, t, hi(VZ, 1, t) + b9 * syz(7, t))


def seafloor(grid, vz, y, floors, out, index):
    total = None
    for t in range(TILES):
        part = jnp.where(floors[0] == grid.depth[t], vz(y, t), 0.0)
        total = part if total is None else total + part
    out[index : index + 1, :] = jnp.sum(total, axis=0, keepdims=True)
    if len(floors) > 1:
        part = jnp.where(floors[1] == grid.depth[WINDOW], vz(y, WINDOW), 0.0)
        out[2 * SUB + index : 2 * SUB + index + 1, :] = jnp.sum(part, axis=0, keepdims=True)


def sea(grid, speed, level, now, fixed, line, lo, hi, sums, new, last):
    vz = speed(VZ)
    for y in range(ROWS):
        seafloor(grid, vz, y, [line(FLOOR, k, y) for k in range(2)], sums, y)
    ends = 1 if last else 2
    for y, side, at in ((-1, lo, ROWS), (ROWS, hi, ROWS + 1)):
        seafloor(grid, vz, y, [side.line(FLOOR, k) for k in range(ends)], sums, at)
    floors, beyond = [tile(sums, 0), grid.every_group(tile(sums, 2))], [tile(sums, 1), None]
    if not last:
        beyond[1] = grid.every_group(tile(sums, 3))
    sub = grid.sub
    levels, lows, highs = [], [], []
    for k in range(2):
        near = jnp.where(sub == 0, lo.line(FLUX_Y, k), jnp.where(sub == ROWS - 1, -hi.line(FLUX_Y, k), 0.0))
        levels.append(level(k) + fixed(WET, k) * (UPLIFT * floors[k] + (0.5 * OCEAN_RATE) * near))
        new(LEVEL, k, levels[k])
        if k < ends:
            for side, at, y, sign, out in ((lo, 0, 0, -1.0, lows), (hi, 1, ROWS - 1, 1.0, highs)):
                mine = (sign * 0.5 * OCEAN_RATE) * line(FLUX_Y, k, y)
                rest = UPLIFT * beyond[k][at : at + 1, :] + mine
                out.append(side.line(None, k) + side.line(WET, k) * rest)
    for k in range(ends):
        wet, deep = fixed(WET, k), fixed(DEPTH, k)
        edge = flat_edge(grid, lambda q: levels[q], k)
        slope_x = 0.5 * (grid.along(levels[k], 1, edge) - grid.along(levels[k], -1, edge))
        slope_y = 0.5 * (grid.across(levels[k], 1, highs[k]) - grid.across(levels[k], -1, lows[k]))
        for which, slope in ((FLUX_X, slope_x), (FLUX_Y, slope_y)):
            x = now(which, k)
            edge = flat_edge(grid, lambda q: now(which, q), k)
            laplace = grid.along(x, 1, edge) + grid.along(x, -1, edge) - 4.0 * x
            laplace = laplace + grid.across(x, 1, hi.line(which, k)) + grid.across(x, -1, lo.line(which, k))
            new(which, k, wet * (x - OCEAN_RATE * deep * slope + VISCOUS * laplace))
    return levels


def press(grid, levels, fixed, line, pressure):
    for k in range(2):
        store(pressure, k, LOADING * fixed(WET, k) * levels[k])

    def load(y, t):
        k = 1 if t == WINDOW else 0
        return jnp.where(line(FLOOR, k, y) == grid.depth[t], row(pressure, k * ROWS + y), 0.0)

    return load


def edge_index(c, y):
    return OPEN.index((c, y)) * SPAN


def block_index(c, y):
    return (c * ROWS + y) * SPAN


def start_kernel(
    flags, before, after, main, flat, own, own_flat, even_in, odd_in, early_even, early_odd,
    windows, flat_windows, partial, level, even_way, odd_way,
):
    grid = Grid(flags[2], before, after)
    odd = (flags[0] & 1) == 1
    for f in range(0, FIELDS, 2):
        for q in range(0, ROWS, 2):
            places = [h * ROWS + y for y in (q, q + 1) for h in (f, f + 1)]
            items = [tile(own, p) for p in places]
            for p, x in zip(places, unpack(grid, items, odd, even_in, odd_in, (f * ROWS // 2 + q) // 2)):
                store(windows, p, x)
    items = [tile(own_flat, k) for k in range(6)]
    base = FIELDS * ROWS // 4
    for k, x in enumerate(unpack(grid, items[:4], odd, even_in, odd_in, base)):
        store(flat_windows, k, x)
    for k, x in enumerate(unpack(grid, items[4:] * 2, odd, even_in, odd_in, base + 1)[:2]):
        store(flat_windows, 4 + k, x)

    field = fields_of(main, windows)
    speeds(
        grid, [inside(field(f)) for f in range(SXX, SYZ + 1)], field, field(BUOY), OPEN,
        lambda c, y, t, value: store(partial, edge_index(c, y) + t, value),
    )
    flats = (flat, flat_windows)
    partial_level(grid, lambda f, k: tile(flats[k], f), lambda k, value: store(level, k, value))

    def rows_of(f):
        return (lambda y, t: tile(partial, edge_index(f, y) + t)) if f < 3 else field(f)

    def line(which, k, y):
        return row(level, k * ROWS + y) if which is None else row(flats[k], which * ROWS + y)

    send(FIRST, (flags[1] & 1) == 1, rows_of, line, even_way, odd_way)


def start_rest_kernel(flags, before, after, main, windows, speed_out, stress_out):
    grid = Grid(flags[2], before, after)
    field = fields_of(main, windows)
    speeds(
        grid, [inside(field(f)) for f in range(SXX, SYZ + 1)], field, field(BUOY), CLOSED,
        lambda c, y, t, value: store(speed_out, block_index(c, y) + t, value),
    )
    stresses(
        grid, INNER, SPAN, block_reader(speed_out, VX), field,
        field(LAME), field(SHEAR),
        lambda f, y, t, value: store(stress_out, block_index(f - SXX, y) + t, value),
    )


def block_reader(ref, least):
    return lambda f: lambda y, t, *start: tile(ref, block_index(f - least, y) + t, *start)


def speed_reader(around, block):
    def speed(c):
        def read(y, t, *start):
            if (c, y) in CLOSED:
                return tile(block, block_index(c, y) + t, *start)
            return tile(around, (c * AROUND + y + 2) * SPAN + t, *start)

        return read

    return speed


def middle_kernel(
    flags, before, after, main, windows, flat, flat_windows, partial, level, speed_in, stress_in,
    early_even, early_odd, even_in, odd_in,
    speed_out, stress_out, ocean, partial_out, level_out, even_way, odd_way,
    sums, pressure,
):
    grid = Grid(flags[2], before, after)
    odd = (flags[1] & 1) == 1
    lo, hi = received(FIRST, odd, even_in, odd_in)
    field = fields_of(main, windows)
    finish(
        grid, SPAN, lambda c, y, t: tile(partial, edge_index(c, y) + t), field, field(BUOY), lo, hi, *early(odd, early_even, early_odd, (lo, hi)),
        speed_out,
    )
    speed = speed_reader(speed_out, speed_in)
    flats = (flat, flat_windows)
    fixed = lambda f, k: tile(flats[k], f)
    line = lambda f, k, y: row(flats[k], f * ROWS + y)

    def new(f, k, value):
        store(ocean, 3 * k + f, value)

    levels = sea(grid, speed, lambda k: tile(level, k), fixed, fixed, line, lo, hi, sums, new, False)
    load = press(grid, levels, fixed, line, pressure)

    def put(f, y, t, value):
        store(stress_out, block_index(f - SXX, y) + t, value - load(y, t) if f == SZZ else value)

    stresses(grid, OUTER, SPAN, speed, field, field(LAME), field(SHEAR), put)
    for f in range(SXX, SYZ + 1):
        for y in INNER:
            for t in range(SPAN):
                put(f, y, t, tile(stress_in, block_index(f - SXX, y) + t))
    stress = block_reader(stress_out, SXX)
    speeds(
        grid, [inside(stress(f)) for f in range(SXX, SYZ + 1)], speed, field(BUOY), OPEN,
        lambda c, y, t, value: store(partial_out, edge_index(c, y) + t, value),
    )
    moving = lambda f, k: tile(flats[k], f) if f >= DEPTH else tile(ocean, 3 * k + f)
    partial_level(grid, moving, lambda k, value: store(level_out, k, value))

    def rows_of(f):
        return (lambda y, t: tile(partial_out, edge_index(f, y) + t)) if f < 3 else stress(f)

    def line_out(which, k, y):
        if which is None:
            return row(level_out, k * ROWS + y)
        return line(which, k, y) if which >= DEPTH else row(ocean, (3 * k + which) * ROWS + y)

    send(LATER, odd, rows_of, line_out, even_way, odd_way)


def middle_rest_kernel(flags, before, after, main, windows, around, speed_in, stress_in, speed_out, stress_out):
    grid = Grid(flags[2], before, after)
    field = fields_of(main, windows)
    stress = block_reader(stress_in, SXX)
    speeds(
        grid, [inside(stress(f)) for f in range(SXX, SYZ + 1)], speed_reader(around, speed_in), field(BUOY), CLOSED,
        lambda c, y, t, value: store(speed_out, block_index(c, y) + t, value),
    )
    stresses(
        grid, INNER, TILES, block_reader(speed_out, VX), stress,
        field(LAME), field(SHEAR),
        lambda f, y, t, value: store(stress_out, block_index(f - SXX, y) + t, value),
    )


def last_kernel(
    flags, before, after, main, windows, flat, flat_windows, stress_in, ocean_in, partial, level, speed_in, inner_in,
    early_even, early_odd, even_in, odd_in,
    wave_hbm, ocean_out,
    sums, pressure, around, wave, sem,
):
    grid = Grid(flags[2], before, after)
    odd = (flags[1] & 1) == 1
    lo, hi = received(LATER, odd, even_in, odd_in)
    lo_buoy, hi_buoy = early(odd, early_even, early_odd, (lo, hi))
    field = fields_of(main, windows)
    stress = block_reader(stress_in, SXX)
    finish(
        grid, TILES, lambda c, y, t: tile(partial, edge_index(c, y) + t), stress, field(BUOY),
        lo, hi, lo_buoy, hi_buoy, around,
    )
    speed = speed_reader(around, speed_in)
    sent = []

    def copy(source, target):
        sent.append(pltpu.make_async_copy(source, target, sem.at[len(sent)]))
        sent[-1].start()

    def copy_row(ref, index, f, y):
        copy(ref.at[index * SUB : (index + TILES) * SUB, :], wave_hbm.at[f, :, y, :])

    for c, y in CLOSED:
        copy_row(speed_in, block_index(c, y), c, y)
    for c, y in OPEN:
        copy_row(around, (c * AROUND + y + 2) * SPAN, c, y)
    flats = (flat, flat_windows)
    fixed = lambda f, k: tile(flats[k], f)

    def line(f, k, y):
        return row(flats[k], f * ROWS + y) if f >= DEPTH else row(ocean_in, (3 * k + f) * ROWS + y)

    def new(f, k, value):
        if k == 0:
            store(ocean_out, f, value)

    levels = sea(
        grid, speed, lambda k: tile(level, k), lambda f, k: tile(ocean_in, 3 * k + f), fixed, line, lo, hi, sums, new, True
    )
    load = press(grid, levels, fixed, line, pressure)

    def put(f, y, t, value):
        size = TILES * SUB * ROWS
        if f == SZZ:
            value = value - load(y, t)
        wave[pl.ds((f - SXX) * size + t * SUB * ROWS + y, SUB, stride=ROWS), :] = value

    for f in range(SXX, SYZ + 1):
        for y in INNER:
            for t in range(TILES):
                put(f, y, t, tile(inner_in, block_index(f - SXX, y) + t))
    def done(t):
        for f in range(SXX, SYZ + 1):
            at = ((f - SXX) * TILES + t) * SUB * ROWS
            target = wave_hbm.at[f, t * SUB : (t + 1) * SUB].reshape(SUB * ROWS, LANES)
            copy(wave.at[at : at + SUB * ROWS, :], target)

    stresses(grid, OUTER, TILES, speed, stress, field(LAME), field(SHEAR), put, done)
    for one in sent:
        one.wait()


IN_VMEM = pl.BlockSpec(memory_space=pltpu.VMEM)
IN_SMEM = pl.BlockSpec(memory_space=pltpu.SMEM)
IN_HBM = pl.BlockSpec(memory_space=pltpu.HBM)


def call(kernel, tiles, scratch, *arguments, flags=None, place=IN_VMEM, out_places=None, work=1):
    specs = place if isinstance(place, list) else [place] * len(arguments)
    if flags is not None:
        arguments, specs = (flags, *arguments), [IN_SMEM] + specs
    moved = sum(x.size for x in arguments) + sum(n for n in tiles if isinstance(n, int)) * SUB * LANES
    return pl.pallas_call(
        kernel,
        out_shape=[n if hasattr(n, "dtype") else jax.ShapeDtypeStruct((n * SUB, LANES), jnp.float32) for n in tiles],
        in_specs=specs,
        out_specs=out_places or [IN_VMEM] * len(tiles),
        scratch_shapes=scratch,
        cost_estimate=pl.CostEstimate(flops=work * 1000000, bytes_accessed=4 * moved, transcendentals=0),
        compiler_params=pltpu.CompilerParams(vmem_limit_bytes=24 * 1024 * 1024),
    )(*arguments)


def planes(n):
    return pltpu.VMEM((n * SUB, LANES), jnp.float32)


def swap(x, axis, start):
    pairs = [(i, i + 1) for i in range(start, lax.axis_size(axis) - 1, 2)]
    return lax.ppermute(x, axis, pairs + [(j, i) for i, j in pairs])


def local(*arguments):
    ocean_state = arguments[4]
    inputs = [pltpu.with_memory_space_constraint(x, pltpu.HBM) for x in arguments]
    flags = jnp.stack([lax.axis_index("gx"), lax.axis_index("gy"), 0])
    matrix = jax.ShapeDtypeStruct((2 * LANES, SPAN * LANES), jnp.bfloat16)
    cells4 = jax.ShapeDtypeStruct((FIELDS, ROWS, TILES * SUB, LANES), jnp.float32)

    edge = FIELDS * ROWS // 4 + 2
    before, after, main, flat, own, own_flat, even_way, odd_way, early_even, early_odd = call(
        edges_kernel, [matrix, matrix, cells4, 6, FIELDS * ROWS, 6, edge, edge, 2 * TILES, 2 * TILES],
        [pltpu.VMEM((FIELDS, *arguments[1].shape), jnp.float32), planes(FIELDS * SUB), planes(2 * TILES), planes(2 * TILES)]
        + [pltpu.VMEM(x.shape, x.dtype) for x in inputs[4:]] + [pltpu.SemaphoreType.DMA((FIELDS + 8 + 4 * ROWS,))],
        *inputs, flags=flags, place=IN_HBM,
    )
    x_in = swap(even_way, "gx", 0), swap(odd_way, "gx", 1)
    early_in = swap(early_even, "gy", 0), swap(early_odd, "gy", 1)
    main = main.reshape(-1, LANES)
    first, later = [message_tiles(kind) for kind in (FIRST, LATER)]
    edges, block = len(OPEN) * SPAN, ROWS * SPAN
    windows, flat_windows, partial, level, even_way, odd_way = call(
        start_kernel, [FIELDS * ROWS, 6, edges, 2, first, first], [],
        before, after, main, flat, own, own_flat, *x_in, *early_in, flags=flags,
    )
    y_in = swap(even_way, "gy", 0), swap(odd_way, "gy", 1)
    speed, inner = call(start_rest_kernel, [3 * block, 6 * block], [], before, after, main, windows, flags=flags, work=4)
    around, stress, ocean, partial, level, even_way, odd_way = call(
        middle_kernel, [3 * AROUND * SPAN, 6 * block, 6, edges, 2, later, later], [planes(4), planes(2)],
        before, after, main, windows, flat, flat_windows, partial, level, speed, inner, *early_in, *y_in, flags=flags,
    )
    y_in = swap(even_way, "gy", 0), swap(odd_way, "gy", 1)
    speed, inner = call(
        middle_rest_kernel, [3 * block, 6 * block], [], before, after, main, windows, around, speed, stress, flags=flags, work=4
    )
    copies = len(CLOSED) + len(OPEN) + 6 * TILES
    wave_out, ocean_out = call(
        last_kernel, [jax.ShapeDtypeStruct(arguments[0].shape, jnp.float32), 3],
        [
            planes(4), planes(2), planes(3 * AROUND * SPAN), planes(6 * ROWS * TILES),
            pltpu.SemaphoreType.DMA((copies,)),
        ],
        before, after, main, windows, flat, flat_windows, stress, ocean, partial, level, speed, inner, *early_in, *y_in,
        flags=flags, out_places=[IN_HBM, IN_VMEM],
    )
    return wave_out, ocean_out.reshape(ocean_state.shape)


def solution(mesh):
    in_specs = (
        P(None, None, "gy", "gx"),
        P(None, "gy", "gx"),
        P(None, "gy", "gx"),
        P(None, "gy", "gx"),
        P(None, "gy", "gx"),
        P("gy", "gx"),
        P("gy", "gx"),
        P("gy", "gx"),
    )
    out_specs = (P(None, None, "gy", "gx"), P(None, "gy", "gx"))
    return jax.shard_map(local, mesh=mesh, in_specs=in_specs, out_specs=out_specs, check_vma=False)
```

```python
import jax
import jax.numpy as jnp
from jax import lax
from jax.experimental import pallas as pl
from jax.experimental.pallas import tpu as pltpu
from jax.sharding import PartitionSpec as P

RATE = 0.3 / 24.0
OCEAN_RATE = 0.3
UPLIFT = 0.5
LOADING = 0.5
VISCOUS = 0.1

ROWS = 8
SUB = 8
LANES = 128
EDGE = 8
GROUP = 2 * EDGE
TILES = 4
HALF = TILES * GROUP
SPAN = TILES + 1
WINDOW = TILES

LEVEL, FLUX_X, FLUX_Y, DEPTH, FLOOR, WET = range(6)
VX, VY, VZ, SXX, SYY, SZZ, SXY, SXZ, SYZ, LAME, SHEAR, BUOY = range(12)
FIELDS = 12

OPEN = ((VX, 0), (VX, 1), (VX, 7), (VY, 0), (VY, 6), (VY, 7), (VZ, 0), (VZ, 1), (VZ, 7))
CLOSED = tuple((c, y) for y in range(ROWS) for c in (VX, VY, VZ) if (c, y) not in OPEN)
INNER = (3, 4)
OUTER = tuple(y for y in range(ROWS) if y not in INNER)

SPEED_HIGH = ((VX, 7), (VY, 6), (VY, 7), (VZ, 7))
SPEED_LOW = ((VX, 0), (VX, 1), (VY, 0), (VZ, 0), (VZ, 1))
STRESS_HIGH = ((SXY, 6), (SXY, 7), (SYY, 7), (SYZ, 6), (SYZ, 7))
STRESS_LOW = ((SXY, 0), (SYY, 0), (SYY, 1), (SYZ, 0))
BUOY_HIGH = ((BUOY, 6), (BUOY, 7))
BUOY_LOW = ((BUOY, 0), (BUOY, 1))
LINES = (None, WET, FLOOR, FLUX_X, FLUX_Y)


def rolled(x, shift, axis):
    shift %= x.shape[axis]
    return x if shift == 0 else pltpu.roll(x, shift, axis)


def tile(ref, index, start=None):
    if start is None:
        return ref[index * SUB : (index + 1) * SUB, :]
    return ref[pl.ds(start + index * SUB, SUB), :]


def row(ref, index):
    return ref[index : index + 1, :]


def store(ref, index, value):
    ref[index * SUB : (index + 1) * SUB, :] = value


def split(x, parts):
    out = []
    for part in range(parts):
        out.append(x.astype(jnp.bfloat16))
        if part + 1 < parts:
            x = x - out[-1].astype(jnp.float32)
    return jnp.concatenate(out, axis=1)


def minus(a, b):
    if b is None:
        return a
    return -b if a is None else a - b


def near_far(a, b, c, d):
    near, far = 27.0 * minus(a, b), minus(c, d)
    return near if c is None and d is None else near - far


class Grid:
    def __init__(self, origin=None, before=None, after=None):
        self.origin, self.before, self.after = origin, before, after
        self.sub = lax.broadcasted_iota(jnp.int32, (SUB, LANES), 0)
        self.lane = lax.broadcasted_iota(jnp.int32, (SUB, LANES), 1)
        self.first = self.lane % GROUP < EDGE
        self.left = self.lane < HALF
        self.group = self.lane // GROUP
        self.zero = jnp.zeros((SUB, LANES), jnp.float32)
        depth = [self.sub + SUB * t for t in range(TILES)] + [self.sub + SUB * (self.group % TILES)]
        self.depth = [d.astype(jnp.float32) for d in depth]

    def beside(self, window):
        return jnp.where(self.first, window, rolled(window, HALF, 1))

    def edge(self, beside, t):
        return None if t == WINDOW else rolled(beside, LANES - EDGE - GROUP * t, 1)

    def along(self, x, offset, edge):
        if edge is not None:
            lane = self.lane
            keep = {-1: lane == LANES - 1, -2: lane >= LANES - 2, 1: lane == 0, 2: lane <= 1}[offset]
            x = jnp.where(keep, edge, x)
        return rolled(x, -offset, 1)

    def down(self, field, y, t, offset):
        if t < WINDOW:
            x = field(y, t, self.origin + offset)
            if t == 0 and offset < 0:
                return jnp.where(self.sub >= -offset, x, 0.0)
            if t == TILES - 1 and offset > 0:
                return jnp.where(self.sub < SUB - offset, x, 0.0)
            return x
        x, at = field(y, t), self.lane % HALF
        if offset < 0:
            beyond, far = jnp.where(at >= GROUP, rolled(x, GROUP, 1), 0.0), self.sub >= SUB + offset
        else:
            beyond, far = jnp.where(at < HALF - GROUP, rolled(x, -GROUP, 1), 0.0), self.sub < offset
        return rolled(jnp.where(far, beyond, x), -offset, 0)

    def fz(self, field, y, t):
        down = lambda offset: self.down(field, y, t, offset)
        return near_far(down(1), field(y, t), down(2), down(-1))

    def bz(self, field, y, t):
        down = lambda offset: self.down(field, y, t, offset)
        return near_far(field(y, t), down(-1), down(1), down(-2))

    def along_rows(self, matrix, rows):
        main = split(jnp.concatenate([f(y, t) for f, y in rows for t in range(TILES)], axis=0), 2)
        sides = [f(y, WINDOW) for f, y in rows]
        side = split(jnp.concatenate(sides + sides[: len(sides) % 2], axis=0), 2)
        main = jnp.dot(main, matrix[:, :LANES], preferred_element_type=jnp.float32)
        side = jnp.dot(side, matrix[...], preferred_element_type=jnp.float32)
        out = []
        for i in range(len(rows)):
            part = side[i * SUB : (i + 1) * SUB, :]
            parts = [part[:, t * LANES : (t + 1) * LANES] for t in range(SPAN)]
            tiles = [
                main[(i * TILES + t) * SUB : (i * TILES + t + 1) * SUB, :] + parts[1 + t] for t in range(TILES)
            ]
            out.append(tiles + parts[:1])
        return out

    def fy(self, field, y, t):
        return near_far(field(y + 1, t), field(y, t), field(y + 2, t), field(y - 1, t))

    def by(self, field, y, t):
        return near_far(field(y, t), field(y - 1, t), field(y + 1, t), field(y - 2, t))

    def windows(self, own, from_left, from_right):
        return jnp.where(
            self.left, jnp.where(self.first, from_left, own), jnp.where(self.first, own, from_right)
        )

    def every_group(self, x):
        for shift in (GROUP, 2 * GROUP):
            x = x + jnp.where(self.lane % HALF >= shift, rolled(x, shift, 1), rolled(x, shift - HALF, 1))
        return x

    def across(self, x, offset, beside):
        end = 0 if offset < 0 else ROWS - 1
        return jnp.where(self.sub == end, beside, rolled(x, -offset, 0))


def inside(field):
    return lambda y, t, *start: field(y, t, *start) if 0 <= y < ROWS else None


def fields_of(main, windows):
    def field(f):
        def read(y, t, *start):
            return tile(windows, f * ROWS + y) if t == WINDOW else tile(main, (f * ROWS + y) * TILES + t, *start)

        return read

    return field


def pack(grid, groups, to_right, out):
    for index, (a, b, c, d) in enumerate(groups):
        if to_right:
            one, two = jnp.where(grid.first, a, rolled(b, EDGE, 1)), jnp.where(grid.first, c, rolled(d, EDGE, 1))
        else:
            one, two = jnp.where(grid.first, rolled(b, -EDGE, 1), a), jnp.where(grid.first, rolled(d, -EDGE, 1), c)
        store(out, index, jnp.where(grid.left, one, two))


def edge_groups(own, own_flat):
    groups = [
        [tile(own, h * ROWS + y) for y in (q, q + 1) for h in (f, f + 1)]
        for f in range(0, FIELDS, 2)
        for q in range(0, ROWS, 2)
    ]
    flat = [tile(own_flat, k) for k in range(6)]
    return groups + [flat[:4], flat[4:] * 2]


def unpack(grid, items, odd, even_in, odd_in, index):
    x, y = tile(even_in, index), tile(odd_in, index)
    before, after = jnp.where(odd, x, y), jnp.where(odd, y, x)
    befores = [before, rolled(before, -EDGE, 1), rolled(before, HALF, 1), rolled(before, HALF - EDGE, 1)]
    afters = [rolled(after, HALF, 1), rolled(after, HALF + EDGE, 1), after, rolled(after, EDGE, 1)]
    return [grid.windows(*three) for three in zip(items, befores, afters)]


def difference_matrix(out, weights, offsets):
    shape = (LANES, LANES)
    k, n = [lax.broadcasted_iota(jnp.int32, shape, axis) for axis in range(2)]

    def weight(apart):
        total = jnp.zeros(shape, jnp.float32)
        for w, offset in zip(weights, offsets):
            total = jnp.where(apart == offset, w, total)
        return total

    inner, left = k % GROUP, k < HALF
    column = jnp.where(left, inner - EDGE, LANES - EDGE + inner)
    outside = (left & (inner < EDGE)) | (jnp.logical_not(left) & (inner >= EDGE))
    beside = jnp.where(outside, weight(n - column), 0.0)
    parts = [weight(n - k)]
    parts += [jnp.where(k % HALF // GROUP == t, beside, 0.0) for t in range(TILES)]
    for p, x in enumerate(parts):
        for half in range(2):
            out[half * LANES : (half + 1) * LANES, p * LANES : (p + 1) * LANES] = x.astype(jnp.bfloat16)


def picker(t):
    k, n = [lax.broadcasted_iota(jnp.int32, (LANES, LANES), axis) for axis in range(2)]
    column = (n % GROUP - EDGE) % LANES
    one = jnp.where((n % HALF // GROUP == t) & (k == column), 1.0, 0.0).astype(jnp.bfloat16)
    return jnp.concatenate([one] * 2, axis=0)


def edges_kernel(flags, *refs):
    hbm, refs = refs[:8], refs[8:]
    (before, after, main, flat, own, own_flat, even_way, odd_way, early_even, early_odd), refs = refs[:10], refs[10:]
    ocean, deep, floor, wet, sem = refs
    sent = []

    def copy(source, target):
        sent.append(pltpu.make_async_copy(source, target, sem.at[len(sent)]))
        sent[-1].start()
        return sent[-1]

    ready = [[], []]
    cut = FIELDS // 2
    for y in range(ROWS):
        ready[0].append(copy(hbm[0].at[:cut, :, y, :], main.at[:cut, y]))
    for y in range(ROWS):
        ready[1].append(copy(hbm[0].at[cut:, :, y, :], main.at[cut:LAME, y]))
        ready[1] += [copy(hbm[1 + k].at[:, y, :], main.at[LAME + k, y]) for k in range(3)]
    rest = [copy(hbm[4 + k], x) for k, x in enumerate((ocean, deep, floor, wet))]
    difference_matrix(before, (27.0, -27.0, -1.0, 1.0), (0, 1, -1, 2))
    difference_matrix(after, (27.0, -27.0, -1.0, 1.0), (-1, 0, -2, 1))
    pickers = [picker(t) for t in range(TILES)]
    grid = Grid()
    size = SUB * ROWS
    for half in range(2):
        for one in ready[half]:
            one.wait()
        mine = range(half * cut, (half + 1) * cut)
        total = None
        for t in range(TILES):
            x = [main[f, y, t * SUB : (t + 1) * SUB, :] for f in mine for y in range(ROWS)]
            part = jnp.dot(split(jnp.concatenate(x, axis=0), 2), pickers[t], preferred_element_type=jnp.float32)
            total = part if total is None else total + part
        own[mine[0] * size : (mine[-1] + 1) * size, :] = total
    for one in rest:
        one.wait()
    planes = [ocean[k] for k in range(3)] + [deep[...]]
    planes += [floor[...].astype(jnp.float32), wet[...].astype(jnp.float32)]
    for k, x in enumerate(planes):
        store(flat, k, x)
        out = grid.zero
        for g in range(LANES // GROUP):
            out = jnp.where(grid.group == g, rolled(x, EDGE + GROUP * g, 1), out)
        store(own_flat, k, out)

    @pl.when((flags[0] & 1) == 1)
    def _():
        pack(grid, edge_groups(own, own_flat), True, odd_way)
        pack(grid, edge_groups(own, own_flat), False, even_way)

    @pl.when((flags[0] & 1) == 0)
    def _():
        pack(grid, edge_groups(own, own_flat), False, odd_way)
        pack(grid, edge_groups(own, own_flat), True, even_way)

    odd = (flags[1] & 1) == 1
    for k, ((_, below), (_, above)) in enumerate(zip(BUOY_LOW, BUOY_HIGH)):
        for t in range(TILES):
            a, b = [main[BUOY, y, t * SUB : (t + 1) * SUB, :] for y in (below, above)]
            store(early_even, k * TILES + t, jnp.where(odd, a, b))
            store(early_odd, k * TILES + t, jnp.where(odd, b, a))


def speeds(grid, stress, speed, buoy, todo, put):
    sxx, syy, szz, sxy, sxz, syz = stress
    forth = [(VX, y) for c, y in todo if c == VX]
    back = [(c, y) for c, y in todo if c != VX]
    change = dict(zip(forth, grid.along_rows(grid.after, [(sxx, y) for _, y in forth])))
    change.update(zip(back, grid.along_rows(grid.before, [(sxy if c == VY else sxz, y) for c, y in back])))
    for y in range(ROWS):
        parts = [c for c in (VX, VY, VZ) if (c, y) in todo]
        if not parts:
            continue
        for t in range(SPAN):
            rate = RATE * buoy(y, t)
            for c in parts:
                a = change[c, y][t]
                if c == VX:
                    a = a + grid.by(sxy, y, t) + grid.bz(sxz, y, t)
                elif c == VY:
                    a = a + grid.fy(syy, y, t) + grid.bz(syz, y, t)
                else:
                    a = a + grid.by(syz, y, t) + grid.fz(szz, y, t)
                put(c, y, t, speed(c)(y, t) + rate * a)


def stresses(grid, rows, tiles, speed, stress, lame, shear, put, done=lambda y: None):
    vx, vy, vz = [speed(c) for c in (VX, VY, VZ)]
    back = grid.along_rows(grid.before, [(vx, y) for y in rows])
    forth = grid.along_rows(grid.after, [(v, y) for v in (vy, vz) for y in rows])
    for i, y in enumerate(rows):
        for t in range(tiles):
            strain_x = back[i][t]
            strain_y = grid.by(vy, y, t)
            strain_z = grid.bz(vz, y, t)
            mu = RATE * shear(y, t)
            spread = (RATE * lame(y, t)) * (strain_x + strain_y + strain_z)
            two = mu + mu
            put(SXX, y, t, stress(SXX)(y, t) + (spread + two * strain_x))
            put(SYY, y, t, stress(SYY)(y, t) + (spread + two * strain_y))
            put(SZZ, y, t, stress(SZZ)(y, t) + (spread + two * strain_z))
            put(SXY, y, t, stress(SXY)(y, t) + mu * (grid.fy(vx, y, t) + forth[i][t]))
            put(SXZ, y, t, stress(SXZ)(y, t) + mu * (grid.fz(vx, y, t) + forth[len(rows) + i][t]))
            put(SYZ, y, t, stress(SYZ)(y, t) + mu * (grid.fz(vy, y, t) + grid.fy(vz, y, t)))
        done(y)


def flat_edge(grid, at, k):
    return grid.edge(grid.beside(at(1)), 0) if k == 0 else None


def partial_level(grid, flat, put):
    for k in range(2):
        x, y = flat(FLUX_X, k), flat(FLUX_Y, k)
        edge = flat_edge(grid, lambda q: flat(FLUX_X, q), k)
        spread = 0.5 * (grid.along(x, 1, edge) - grid.along(x, -1, edge))
        spread = spread + 0.5 * (grid.across(y, 1, 0.0) - grid.across(y, -1, 0.0))
        put(k, flat(LEVEL, k) - OCEAN_RATE * (flat(WET, k) * spread))


def cells(rows, tiles):
    return [(f, y, t) for f, y in rows for t in tiles]


class Message:
    def __init__(self, tiles):
        self.at = {which: i for i, which in enumerate(tiles)}
        self.base = len(tiles) * SUB
        self.size = self.base + 2 * SUB


ALL, INSIDE = range(SPAN), range(TILES)
SIDES = (WINDOW,)
EARLY = [{which: i for i, which in enumerate(cells(rows, INSIDE))} for rows in (BUOY_HIGH, BUOY_LOW)]
FIRST = [
    Message(cells(rows, ALL) + cells(buoy, SIDES))
    for rows, buoy in ((SPEED_HIGH + STRESS_HIGH, BUOY_HIGH), (SPEED_LOW + STRESS_LOW, BUOY_LOW))
]
LATER = [
    Message(cells(speed, INSIDE) + cells(rest, ALL))
    for speed, rest in ((SPEED_HIGH, STRESS_HIGH), (SPEED_LOW, STRESS_LOW))
]


def message_tiles(kind):
    return max(m.size for m in kind) // SUB


def send(kind, odd, field, line, even_way, odd_way):
    high, low = kind

    def fill(message, edge, out):
        for (f, y, t), at in message.at.items():
            store(out, at, field(f)(y, t))
        at = message.base
        for which in LINES:
            for k in range(2):
                out[at : at + 1, :] = line(which, k, edge)
                at += 1
        out[at : at + 6, :] = jnp.zeros((6, LANES), jnp.float32)
        tail = out.shape[0]
        if message.size < tail:
            out[message.size : tail, :] = jnp.zeros((tail - message.size, LANES), jnp.float32)

    @pl.when(odd)
    def _():
        fill(high, ROWS - 1, odd_way)
        fill(low, 0, even_way)

    @pl.when(jnp.logical_not(odd))
    def _():
        fill(high, ROWS - 1, even_way)
        fill(low, 0, odd_way)


class Received:
    def __init__(self, message, odd, if_odd, if_even):
        self.message, self.odd, self.if_odd, self.if_even = message, odd, if_odd, if_even

    def __call__(self, f, y, t):
        at = self.message.at[f, y, t]
        return jnp.where(self.odd, tile(self.if_odd, at), tile(self.if_even, at))

    def line(self, which, k):
        at = self.message.base + 2 * LINES.index(which) + k
        return jnp.where(self.odd, row(self.if_odd, at), row(self.if_even, at))


def received(kind, odd, even_in, odd_in):
    return Received(kind[0], odd, even_in, odd_in), Received(kind[1], odd, odd_in, even_in)


def early(odd, even_in, odd_in, later):
    def reader(at, if_odd, if_even, rest):
        def read(f, y, t):
            if (f, y, t) not in at:
                return rest(f, y, t)
            return jnp.where(odd, tile(if_odd, at[f, y, t]), tile(if_even, at[f, y, t]))

        return read

    return reader(EARLY[0], even_in, odd_in, later[0]), reader(EARLY[1], odd_in, even_in, later[1])


AROUND = ROWS + 4


def finish(grid, tiles, partial, stress, buoy, lo, hi, lo_buoy, hi_buoy, speed):
    sxy, syy, syz = [stress(f) for f in (SXY, SYY, SYZ)]

    def put(c, y, t, value):
        store(speed, (c * AROUND + y + 2) * SPAN + t, value)

    for t in range(SPAN):
        for c, f in ((VX, SXY), (VZ, SYZ)):
            two, one = lo(f, 6, t), lo(f, 7, t)
            rate = [RATE * buoy(y, t) for y in (0, 1, 7)]
            put(c, 0, t, partial(c, 0, t) + rate[0] * (two - 27.0 * one))
            put(c, 1, t, partial(c, 1, t) + rate[1] * one)
            put(c, 7, t, partial(c, 7, t) - rate[2] * hi(f, 0, t))
        h8, h9 = hi(SYY, 0, t), hi(SYY, 1, t)
        put(VY, 0, t, partial(VY, 0, t) + (RATE * buoy(0, t)) * lo(SYY, 7, t))
        put(VY, 6, t, partial(VY, 6, t) - (RATE * buoy(6, t)) * h8)
        put(VY, 7, t, partial(VY, 7, t) + (RATE * buoy(7, t)) * (27.0 * h8 - h9))
    for t in range(tiles):
        b2, b1 = RATE * lo_buoy(BUOY, 6, t), RATE * lo_buoy(BUOY, 7, t)
        b8, b9 = RATE * hi_buoy(BUOY, 0, t), RATE * hi_buoy(BUOY, 1, t)
        put(VX, -1, t, lo(VX, 7, t) - b1 * sxy(0, t))
        put(VY, -2, t, lo(VY, 6, t) - b2 * syy(0, t))
        put(VY, -1, t, lo(VY, 7, t) + b1 * (27.0 * syy(0, t) - syy(1, t)))
        put(VZ, -1, t, lo(VZ, 7, t) - b1 * syz(0, t))
        put(VX, 8, t, hi(VX, 0, t) + b8 * (sxy(6, t) - 27.0 * sxy(7, t)))
        put(VX, 9, t, hi(VX, 1, t) + b9 * sxy(7, t))
        put(VY, 8, t, hi(VY, 0, t) + b8 * syy(7, t))
        put(VZ, 8, t, hi(VZ, 0, t) + b8 * (syz(6, t) - 27.0 * syz(7, t)))
        put(VZ, 9, t, hi(VZ, 1, t) + b9 * syz(7, t))


def seafloor(grid, vz, y, floors, out, index):
    total = None
    for t in range(TILES):
        part = jnp.where(floors[0] == grid.depth[t], vz(y, t), 0.0)
        total = part if total is None else total + part
    out[index : index + 1, :] = jnp.sum(total, axis=0, keepdims=True)
    if len(floors) > 1:
        part = jnp.where(floors[1] == grid.depth[WINDOW], vz(y, WINDOW), 0.0)
        out[2 * SUB + index : 2 * SUB + index + 1, :] = jnp.sum(part, axis=0, keepdims=True)


def sea(grid, speed, level, now, fixed, line, lo, hi, sums, new, last):
    vz = speed(VZ)
    for y in range(ROWS):
        seafloor(grid, vz, y, [line(FLOOR, k, y) for k in range(2)], sums, y)
    ends = 1 if last else 2
    for y, side, at in ((-1, lo, ROWS), (ROWS, hi, ROWS + 1)):
        seafloor(grid, vz, y, [side.line(FLOOR, k) for k in range(ends)], sums, at)
    floors, beyond = [tile(sums, 0), grid.every_group(tile(sums, 2))], [tile(sums, 1), None]
    if not last:
        beyond[1] = grid.every_group(tile(sums, 3))
    sub = grid.sub
    levels, lows, highs = [], [], []
    for k in range(2):
        near = jnp.where(sub == 0, lo.line(FLUX_Y, k), jnp.where(sub == ROWS - 1, -hi.line(FLUX_Y, k), 0.0))
        levels.append(level(k) + fixed(WET, k) * (UPLIFT * floors[k] + (0.5 * OCEAN_RATE) * near))
        new(LEVEL, k, levels[k])
        if k < ends:
            for side, at, y, sign, out in ((lo, 0, 0, -1.0, lows), (hi, 1, ROWS - 1, 1.0, highs)):
                mine = (sign * 0.5 * OCEAN_RATE) * line(FLUX_Y, k, y)
                rest = UPLIFT * beyond[k][at : at + 1, :] + mine
                out.append(side.line(None, k) + side.line(WET, k) * rest)
    for k in range(ends):
        wet, deep = fixed(WET, k), fixed(DEPTH, k)
        edge = flat_edge(grid, lambda q: levels[q], k)
        slope_x = 0.5 * (grid.along(levels[k], 1, edge) - grid.along(levels[k], -1, edge))
        slope_y = 0.5 * (grid.across(levels[k], 1, highs[k]) - grid.across(levels[k], -1, lows[k]))
        for which, slope in ((FLUX_X, slope_x), (FLUX_Y, slope_y)):
            x = now(which, k)
            edge = flat_edge(grid, lambda q: now(which, q), k)
            laplace = grid.along(x, 1, edge) + grid.along(x, -1, edge) - 4.0 * x
            laplace = laplace + grid.across(x, 1, hi.line(which, k)) + grid.across(x, -1, lo.line(which, k))
            new(which, k, wet * (x - OCEAN_RATE * deep * slope + VISCOUS * laplace))
    return levels


def press(grid, levels, fixed, line, pressure):
    for k in range(2):
        store(pressure, k, LOADING * fixed(WET, k) * levels[k])

    def load(y, t):
        k = 1 if t == WINDOW else 0
        return jnp.where(line(FLOOR, k, y) == grid.depth[t], row(pressure, k * ROWS + y), 0.0)

    return load


def edge_index(c, y):
    return OPEN.index((c, y)) * SPAN


def block_index(c, y):
    return (c * ROWS + y) * SPAN


def start_kernel(
    flags, before, after, main, flat, own, own_flat, even_in, odd_in, early_even, early_odd,
    windows, flat_windows, partial, level, even_way, odd_way,
):
    grid = Grid(flags[2], before, after)
    odd = (flags[0] & 1) == 1
    for f in range(0, FIELDS, 2):
        for q in range(0, ROWS, 2):
            places = [h * ROWS + y for y in (q, q + 1) for h in (f, f + 1)]
            items = [tile(own, p) for p in places]
            for p, x in zip(places, unpack(grid, items, odd, even_in, odd_in, (f * ROWS // 2 + q) // 2)):
                store(windows, p, x)
    items = [tile(own_flat, k) for k in range(6)]
    base = FIELDS * ROWS // 4
    for k, x in enumerate(unpack(grid, items[:4], odd, even_in, odd_in, base)):
        store(flat_windows, k, x)
    for k, x in enumerate(unpack(grid, items[4:] * 2, odd, even_in, odd_in, base + 1)[:2]):
        store(flat_windows, 4 + k, x)

    field = fields_of(main, windows)
    speeds(
        grid, [inside(field(f)) for f in range(SXX, SYZ + 1)], field, field(BUOY), OPEN,
        lambda c, y, t, value: store(partial, edge_index(c, y) + t, value),
    )
    flats = (flat, flat_windows)
    partial_level(grid, lambda f, k: tile(flats[k], f), lambda k, value: store(level, k, value))

    def rows_of(f):
        return (lambda y, t: tile(partial, edge_index(f, y) + t)) if f < 3 else field(f)

    def line(which, k, y):
        return row(level, k * ROWS + y) if which is None else row(flats[k], which * ROWS + y)

    send(FIRST, (flags[1] & 1) == 1, rows_of, line, even_way, odd_way)


def start_rest_kernel(flags, before, after, main, windows, speed_out, stress_out):
    grid = Grid(flags[2], before, after)
    field = fields_of(main, windows)
    speeds(
        grid, [inside(field(f)) for f in range(SXX, SYZ + 1)], field, field(BUOY), CLOSED,
        lambda c, y, t, value: store(speed_out, block_index(c, y) + t, value),
    )
    stresses(
        grid, INNER, SPAN, block_reader(speed_out, VX), field,
        field(LAME), field(SHEAR),
        lambda f, y, t, value: store(stress_out, block_index(f - SXX, y) + t, value),
    )


def block_reader(ref, least):
    return lambda f: lambda y, t, *start: tile(ref, block_index(f - least, y) + t, *start)


def speed_reader(around, block):
    def speed(c):
        def read(y, t, *start):
            if (c, y) in CLOSED:
                return tile(block, block_index(c, y) + t, *start)
            return tile(around, (c * AROUND + y + 2) * SPAN + t, *start)

        return read

    return speed


def middle_kernel(
    flags, before, after, main, windows, flat, flat_windows, partial, level, speed_in, stress_in,
    early_even, early_odd, even_in, odd_in,
    speed_out, stress_out, ocean, partial_out, level_out, even_way, odd_way,
    sums, pressure,
):
    grid = Grid(flags[2], before, after)
    odd = (flags[1] & 1) == 1
    lo, hi = received(FIRST, odd, even_in, odd_in)
    field = fields_of(main, windows)
    finish(
        grid, SPAN, lambda c, y, t: tile(partial, edge_index(c, y) + t), field, field(BUOY), lo, hi, *early(odd, early_even, early_odd, (lo, hi)),
        speed_out,
    )
    speed = speed_reader(speed_out, speed_in)
    flats = (flat, flat_windows)
    fixed = lambda f, k: tile(flats[k], f)
    line = lambda f, k, y: row(flats[k], f * ROWS + y)

    def new(f, k, value):
        store(ocean, 3 * k + f, value)

    levels = sea(grid, speed, lambda k: tile(level, k), fixed, fixed, line, lo, hi, sums, new, False)
    load = press(grid, levels, fixed, line, pressure)

    def put(f, y, t, value):
        store(stress_out, block_index(f - SXX, y) + t, value - load(y, t) if f == SZZ else value)

    stresses(grid, OUTER, SPAN, speed, field, field(LAME), field(SHEAR), put)
    for f in range(SXX, SYZ + 1):
        for y in INNER:
            for t in range(SPAN):
                put(f, y, t, tile(stress_in, block_index(f - SXX, y) + t))
    stress = block_reader(stress_out, SXX)
    speeds(
        grid, [inside(stress(f)) for f in range(SXX, SYZ + 1)], speed, field(BUOY), OPEN,
        lambda c, y, t, value: store(partial_out, edge_index(c, y) + t, value),
    )
    moving = lambda f, k: tile(flats[k], f) if f >= DEPTH else tile(ocean, 3 * k + f)
    partial_level(grid, moving, lambda k, value: store(level_out, k, value))

    def rows_of(f):
        return (lambda y, t: tile(partial_out, edge_index(f, y) + t)) if f < 3 else stress(f)

    def line_out(which, k, y):
        if which is None:
            return row(level_out, k * ROWS + y)
        return line(which, k, y) if which >= DEPTH else row(ocean, (3 * k + which) * ROWS + y)

    send(LATER, odd, rows_of, line_out, even_way, odd_way)


def copy_rows(ref, index, hbm, f, y, sem):
    return pltpu.make_async_copy(ref.at[index * SUB : (index + TILES) * SUB, :], hbm.at[f, :, y, :], sem)


BY_ROWS = (SXX, SYY)
BY_FIELD = (SZZ, SXY, SXZ, SYZ)


def middle_rest_kernel(flags, before, after, main, windows, around, speed_in, stress_in, speed_out, stress_out, wave_hbm, sem):
    grid = Grid(flags[2], before, after)
    field = fields_of(main, windows)
    stress = block_reader(stress_in, SXX)
    speeds(
        grid, [inside(stress(f)) for f in range(SXX, SYZ + 1)], speed_reader(around, speed_in), field(BUOY), CLOSED,
        lambda c, y, t, value: store(speed_out, block_index(c, y) + t, value),
    )
    sent = [copy_rows(speed_out, block_index(c, y), wave_hbm, c, y, sem.at[i]) for i, (c, y) in enumerate(CLOSED)]
    for one in sent:
        one.start()
    stresses(
        grid, INNER, TILES, block_reader(speed_out, VX), stress,
        field(LAME), field(SHEAR),
        lambda f, y, t, value: store(stress_out, block_index(f - SXX, y) + t, value),
    )
    for f in BY_ROWS:
        for y in INNER:
            sent.append(copy_rows(stress_out, block_index(f - SXX, y), wave_hbm, f, y, sem.at[len(sent)]))
            sent[-1].start()
    for one in sent:
        one.wait()


def last_kernel(
    flags, before, after, main, windows, flat, flat_windows, stress_in, ocean_in, partial, level, speed_in, inner_in,
    early_even, early_odd, even_in, odd_in, wave_in,
    wave_hbm, ocean_out,
    sums, pressure, around, turned, wave, sem,
):
    grid = Grid(flags[2], before, after)
    odd = (flags[1] & 1) == 1
    lo, hi = received(LATER, odd, even_in, odd_in)
    lo_buoy, hi_buoy = early(odd, early_even, early_odd, (lo, hi))
    field = fields_of(main, windows)
    stress = block_reader(stress_in, SXX)
    finish(
        grid, TILES, lambda c, y, t: tile(partial, edge_index(c, y) + t), stress, field(BUOY),
        lo, hi, lo_buoy, hi_buoy, around,
    )
    speed = speed_reader(around, speed_in)
    sent = []

    def copy(source, target):
        sent.append(pltpu.make_async_copy(source, target, sem.at[len(sent)]))
        sent[-1].start()

    for c, y in OPEN:
        sent.append(copy_rows(around, (c * AROUND + y + 2) * SPAN, wave_hbm, c, y, sem.at[len(sent)]))
        sent[-1].start()
    flats = (flat, flat_windows)
    fixed = lambda f, k: tile(flats[k], f)

    def line(f, k, y):
        return row(flats[k], f * ROWS + y) if f >= DEPTH else row(ocean_in, (3 * k + f) * ROWS + y)

    def new(f, k, value):
        if k == 0:
            store(ocean_out, f, value)

    levels = sea(
        grid, speed, lambda k: tile(level, k), lambda f, k: tile(ocean_in, 3 * k + f), fixed, line, lo, hi, sums, new, True
    )
    load = press(grid, levels, fixed, line, pressure)

    size = TILES * SUB * ROWS

    def put(f, y, t, value):
        if f in BY_ROWS:
            turned[f - SXX, y, t * SUB : (t + 1) * SUB, :] = value
            return
        if f == SZZ:
            value = value - load(y, t)
        wave[pl.ds(BY_FIELD.index(f) * size + t * SUB * ROWS + y, SUB, stride=ROWS), :] = value

    def done(y):
        copy(turned.at[:, y], wave_hbm.at[SXX : SYY + 1, :, y, :])

    stresses(grid, OUTER, TILES, speed, stress, field(LAME), field(SHEAR), put, done)
    for f in BY_FIELD:
        for y in INNER:
            for t in range(TILES):
                put(f, y, t, tile(inner_in, block_index(f - SXX, y) + t))
    copy(wave, wave_hbm.at[SZZ : SYZ + 1].reshape(len(BY_FIELD) * size, LANES))
    for one in sent:
        one.wait()


IN_VMEM = pl.BlockSpec(memory_space=pltpu.VMEM)
IN_SMEM = pl.BlockSpec(memory_space=pltpu.SMEM)
IN_HBM = pl.BlockSpec(memory_space=pltpu.HBM)


def call(kernel, tiles, scratch, *arguments, flags=None, place=IN_VMEM, out_places=None, work=1, aliases={}):
    specs = place if isinstance(place, list) else [place] * len(arguments)
    if flags is not None:
        arguments, specs = (flags, *arguments), [IN_SMEM] + specs
    moved = sum(x.size for x in arguments) + sum(n for n in tiles if isinstance(n, int)) * SUB * LANES
    return pl.pallas_call(
        kernel,
        out_shape=[n if hasattr(n, "dtype") else jax.ShapeDtypeStruct((n * SUB, LANES), jnp.float32) for n in tiles],
        in_specs=specs,
        out_specs=out_places or [IN_VMEM] * len(tiles),
        scratch_shapes=scratch,
        input_output_aliases=aliases,
        cost_estimate=pl.CostEstimate(flops=work * 1000000, bytes_accessed=4 * moved, transcendentals=0),
        compiler_params=pltpu.CompilerParams(vmem_limit_bytes=24 * 1024 * 1024),
    )(*arguments)


def planes(n):
    return pltpu.VMEM((n * SUB, LANES), jnp.float32)


def swap(x, axis, start):
    pairs = [(i, i + 1) for i in range(start, lax.axis_size(axis) - 1, 2)]
    return lax.ppermute(x, axis, pairs + [(j, i) for i, j in pairs])


def local(*arguments):
    ocean_state = arguments[4]
    inputs = [pltpu.with_memory_space_constraint(x, pltpu.HBM) for x in arguments]
    flags = jnp.stack([lax.axis_index("gx"), lax.axis_index("gy"), 0])
    matrix = jax.ShapeDtypeStruct((2 * LANES, SPAN * LANES), jnp.bfloat16)
    cells4 = jax.ShapeDtypeStruct((FIELDS, ROWS, TILES * SUB, LANES), jnp.float32)

    edge = FIELDS * ROWS // 4 + 2
    before, after, main, flat, own, own_flat, even_way, odd_way, early_even, early_odd = call(
        edges_kernel, [matrix, matrix, cells4, 6, FIELDS * ROWS, 6, edge, edge, 2 * TILES, 2 * TILES],
        [pltpu.VMEM(x.shape, x.dtype) for x in inputs[4:]] + [pltpu.SemaphoreType.DMA((4 + 5 * ROWS,))],
        *inputs, flags=flags, place=IN_HBM,
    )
    x_in = swap(even_way, "gx", 0), swap(odd_way, "gx", 1)
    early_in = swap(early_even, "gy", 0), swap(early_odd, "gy", 1)
    main = main.reshape(-1, LANES)
    first, later = [message_tiles(kind) for kind in (FIRST, LATER)]
    edges, block = len(OPEN) * SPAN, ROWS * SPAN
    windows, flat_windows, partial, level, even_way, odd_way = call(
        start_kernel, [FIELDS * ROWS, 6, edges, 2, first, first], [],
        before, after, main, flat, own, own_flat, *x_in, *early_in, flags=flags,
    )
    y_in = swap(even_way, "gy", 0), swap(odd_way, "gy", 1)
    speed, inner = call(start_rest_kernel, [3 * block, 6 * block], [], before, after, main, windows, flags=flags, work=4)
    around, stress, ocean, partial, level, even_way, odd_way = call(
        middle_kernel, [3 * AROUND * SPAN, 6 * block, 6, edges, 2, later, later], [planes(4), planes(2)],
        before, after, main, windows, flat, flat_windows, partial, level, speed, inner, *early_in, *y_in, flags=flags,
    )
    y_in = swap(even_way, "gy", 0), swap(odd_way, "gy", 1)
    wave = jax.ShapeDtypeStruct(arguments[0].shape, jnp.float32)
    speed, inner, wave_part = call(
        middle_rest_kernel, [3 * block, 6 * block, wave],
        [pltpu.SemaphoreType.DMA((len(CLOSED) + len(BY_ROWS) * len(INNER),))],
        before, after, main, windows, around, speed, stress, flags=flags, out_places=[IN_VMEM, IN_VMEM, IN_HBM], work=4,
    )
    operands = (
        before, after, main, windows, flat, flat_windows, stress, ocean, partial, level, speed, inner, *early_in, *y_in, wave_part
    )
    wave_out, ocean_out = call(
        last_kernel, [wave, 3],
        [
            planes(4), planes(2), planes(3 * AROUND * SPAN),
            pltpu.VMEM((len(BY_ROWS), *cells4.shape[1:]), jnp.float32), planes(len(BY_FIELD) * ROWS * TILES),
            pltpu.SemaphoreType.DMA((len(OPEN) + len(OUTER) + 1,)),
        ],
        *operands, flags=flags, place=[IN_VMEM] * (len(operands) - 1) + [IN_HBM], out_places=[IN_HBM, IN_VMEM],
        aliases={len(operands): 0},
    )
    return wave_out, ocean_out.reshape(ocean_state.shape)


def solution(mesh):
    in_specs = (
        P(None, None, "gy", "gx"),
        P(None, "gy", "gx"),
        P(None, "gy", "gx"),
        P(None, "gy", "gx"),
        P(None, "gy", "gx"),
        P("gy", "gx"),
        P("gy", "gx"),
        P("gy", "gx"),
    )
    out_specs = (P(None, None, "gy", "gx"), P(None, "gy", "gx"))
    return jax.shard_map(local, mesh=mesh, in_specs=in_specs, out_specs=out_specs, check_vma=False)
```

```python
import jax
import jax.numpy as jnp
from jax import lax
from jax.experimental import pallas as pl
from jax.experimental.pallas import tpu as pltpu
from jax.sharding import PartitionSpec as P

RATE = 0.3 / 24.0
OCEAN_RATE = 0.3
UPLIFT = 0.5
LOADING = 0.5
VISCOUS = 0.1

ROWS = 8
SUB = 8
LANES = 128
EDGE = 8
GROUP = 2 * EDGE
TILES = 4
HALF = TILES * GROUP
SPAN = TILES + 1
WINDOW = TILES

LEVEL, FLUX_X, FLUX_Y, DEPTH, FLOOR, WET = range(6)
VX, VY, VZ, SXX, SYY, SZZ, SXY, SXZ, SYZ, LAME, SHEAR, BUOY = range(12)
FIELDS = 12

OPEN = ((VX, 0), (VX, 1), (VX, 7), (VY, 0), (VY, 6), (VY, 7), (VZ, 0), (VZ, 1), (VZ, 7))
CLOSED = tuple((c, y) for y in range(ROWS) for c in (VX, VY, VZ) if (c, y) not in OPEN)
INNER = (3, 4)
OUTER = tuple(y for y in range(ROWS) if y not in INNER)

SPEED_HIGH = ((VX, 7), (VY, 6), (VY, 7), (VZ, 7))
SPEED_LOW = ((VX, 0), (VX, 1), (VY, 0), (VZ, 0), (VZ, 1))
STRESS_HIGH = ((SXY, 6), (SXY, 7), (SYY, 7), (SYZ, 6), (SYZ, 7))
STRESS_LOW = ((SXY, 0), (SYY, 0), (SYY, 1), (SYZ, 0))
BUOY_HIGH = ((BUOY, 6), (BUOY, 7))
BUOY_LOW = ((BUOY, 0), (BUOY, 1))
LINES = (None, WET, FLOOR, FLUX_X, FLUX_Y)


def rolled(x, shift, axis):
    shift %= x.shape[axis]
    return x if shift == 0 else pltpu.roll(x, shift, axis)


def tile(ref, index, start=None):
    if start is None:
        return ref[index * SUB : (index + 1) * SUB, :]
    return ref[pl.ds(start + index * SUB, SUB), :]


def row(ref, index):
    return ref[index : index + 1, :]


def store(ref, index, value):
    ref[index * SUB : (index + 1) * SUB, :] = value


def split(x, parts):
    out = []
    for part in range(parts):
        out.append(x.astype(jnp.bfloat16))
        if part + 1 < parts:
            x = x - out[-1].astype(jnp.float32)
    return jnp.concatenate(out, axis=1)


def minus(a, b):
    if b is None:
        return a
    return -b if a is None else a - b


def near_far(a, b, c, d):
    near, far = 27.0 * minus(a, b), minus(c, d)
    return near if c is None and d is None else near - far


class Grid:
    def __init__(self, origin=None, before=None, after=None):
        self.origin, self.before, self.after = origin, before, after
        self.sub = lax.broadcasted_iota(jnp.int32, (SUB, LANES), 0)
        self.lane = lax.broadcasted_iota(jnp.int32, (SUB, LANES), 1)
        self.first = self.lane % GROUP < EDGE
        self.left = self.lane < HALF
        self.group = self.lane // GROUP
        self.zero = jnp.zeros((SUB, LANES), jnp.float32)
        depth = [self.sub + SUB * t for t in range(TILES)] + [self.sub + SUB * (self.group % TILES)]
        self.depth = [d.astype(jnp.float32) for d in depth]

    def beside(self, window):
        return jnp.where(self.first, window, rolled(window, HALF, 1))

    def edge(self, beside, t):
        return None if t == WINDOW else rolled(beside, LANES - EDGE - GROUP * t, 1)

    def along(self, x, offset, edge):
        if edge is not None:
            lane = self.lane
            keep = {-1: lane == LANES - 1, -2: lane >= LANES - 2, 1: lane == 0, 2: lane <= 1}[offset]
            x = jnp.where(keep, edge, x)
        return rolled(x, -offset, 1)

    def down(self, field, y, t, offset):
        if t < WINDOW:
            x = field(y, t, self.origin + offset)
            if t == 0 and offset < 0:
                return jnp.where(self.sub >= -offset, x, 0.0)
            if t == TILES - 1 and offset > 0:
                return jnp.where(self.sub < SUB - offset, x, 0.0)
            return x
        x, at = field(y, t), self.lane % HALF
        if offset < 0:
            beyond, far = jnp.where(at >= GROUP, rolled(x, GROUP, 1), 0.0), self.sub >= SUB + offset
        else:
            beyond, far = jnp.where(at < HALF - GROUP, rolled(x, -GROUP, 1), 0.0), self.sub < offset
        return rolled(jnp.where(far, beyond, x), -offset, 0)

    def fz(self, field, y, t):
        down = lambda offset: self.down(field, y, t, offset)
        return near_far(down(1), field(y, t), down(2), down(-1))

    def bz(self, field, y, t):
        down = lambda offset: self.down(field, y, t, offset)
        return near_far(field(y, t), down(-1), down(1), down(-2))

    def along_rows(self, matrix, rows):
        main = split(jnp.concatenate([f(y, t) for f, y in rows for t in range(TILES)], axis=0), 2)
        sides = [f(y, WINDOW) for f, y in rows]
        side = split(jnp.concatenate(sides + sides[: len(sides) % 2], axis=0), 2)
        main = jnp.dot(main, matrix[:, :LANES], preferred_element_type=jnp.float32)
        side = jnp.dot(side, matrix[...], preferred_element_type=jnp.float32)
        out = []
        for i in range(len(rows)):
            part = side[i * SUB : (i + 1) * SUB, :]
            parts = [part[:, t * LANES : (t + 1) * LANES] for t in range(SPAN)]
            tiles = [
                main[(i * TILES + t) * SUB : (i * TILES + t + 1) * SUB, :] + parts[1 + t] for t in range(TILES)
            ]
            out.append(tiles + parts[:1])
        return out

    def fy(self, field, y, t):
        return near_far(field(y + 1, t), field(y, t), field(y + 2, t), field(y - 1, t))

    def by(self, field, y, t):
        return near_far(field(y, t), field(y - 1, t), field(y + 1, t), field(y - 2, t))

    def windows(self, own, from_left, from_right):
        return jnp.where(
            self.left, jnp.where(self.first, from_left, own), jnp.where(self.first, own, from_right)
        )

    def every_group(self, x):
        for shift in (GROUP, 2 * GROUP):
            x = x + jnp.where(self.lane % HALF >= shift, rolled(x, shift, 1), rolled(x, shift - HALF, 1))
        return x

    def across(self, x, offset, beside):
        end = 0 if offset < 0 else ROWS - 1
        return jnp.where(self.sub == end, beside, rolled(x, -offset, 0))


def inside(field):
    return lambda y, t, *start: field(y, t, *start) if 0 <= y < ROWS else None


def fields_of(main, windows):
    def field(f):
        def read(y, t, *start):
            return tile(windows, f * ROWS + y) if t == WINDOW else tile(main, (f * ROWS + y) * TILES + t, *start)

        return read

    return field


def pack(grid, own, other, flat, other_flat, to_right, out):
    for index, (near, far) in enumerate(zip(edge_groups(own, flat), edge_groups(other, other_flat))):
        a, b, c, d = near[0], far[1], near[2], far[3]
        if not to_right:
            a, b, c, d = b, a, d, c
        store(out, index, jnp.where(grid.left, jnp.where(grid.first, a, b), jnp.where(grid.first, c, d)))


def edge_groups(own, own_flat):
    groups = [
        [tile(own, h * ROWS + y) for y in (q, q + 1) for h in (f, f + 1)]
        for f in range(0, FIELDS, 2)
        for q in range(0, ROWS, 2)
    ]
    flat = [tile(own_flat, k) for k in range(6)]
    return groups + [flat[:4], flat[4:] * 2]


def unpack(grid, items, odd, even_in, odd_in, index):
    x, y = tile(even_in, index), tile(odd_in, index)
    before, after = jnp.where(odd, x, y), jnp.where(odd, y, x)
    befores = [before, rolled(before, -EDGE, 1), rolled(before, HALF, 1), rolled(before, HALF - EDGE, 1)]
    afters = [rolled(after, HALF, 1), rolled(after, HALF + EDGE, 1), after, rolled(after, EDGE, 1)]
    return [grid.windows(*three) for three in zip(items, befores, afters)]


def difference_matrix(out, weights, offsets):
    shape = (LANES, LANES)
    k, n = [lax.broadcasted_iota(jnp.int32, shape, axis) for axis in range(2)]

    def weight(apart):
        total = jnp.zeros(shape, jnp.float32)
        for w, offset in zip(weights, offsets):
            total = jnp.where(apart == offset, w, total)
        return total

    inner, left = k % GROUP, k < HALF
    column = jnp.where(left, inner - EDGE, LANES - EDGE + inner)
    outside = (left & (inner < EDGE)) | (jnp.logical_not(left) & (inner >= EDGE))
    beside = jnp.where(outside, weight(n - column), 0.0)
    parts = [weight(n - k)]
    parts += [jnp.where(k % HALF // GROUP == t, beside, 0.0) for t in range(TILES)]
    for p, x in enumerate(parts):
        for half in range(2):
            out[half * LANES : (half + 1) * LANES, p * LANES : (p + 1) * LANES] = x.astype(jnp.bfloat16)


def picker(t):
    k, n = [lax.broadcasted_iota(jnp.int32, (LANES, LANES), axis) for axis in range(2)]
    inner, mine = n % GROUP, n % HALF // GROUP == t
    both = []
    for swapped in (False, True):
        last = inner >= EDGE if swapped else inner < EDGE
        column = jnp.where(last, LANES - EDGE, 0) + inner % EDGE
        both.append(jnp.where(mine & (k == column), 1.0, 0.0).astype(jnp.bfloat16))
    return jnp.concatenate([jnp.concatenate(both, axis=1)] * 2, axis=0)


def edges_kernel(flags, *refs):
    hbm, refs = refs[:8], refs[8:]
    (before, after, main, flat, own, own_flat, even_way, odd_way, early_even, early_odd), refs = refs[:10], refs[10:]
    other, other_flat, ocean, deep, floor, wet, sem = refs
    sent = []

    def copy(source, target):
        sent.append(pltpu.make_async_copy(source, target, sem.at[len(sent)]))
        sent[-1].start()
        return sent[-1]

    ready = [[], []]
    cut = FIELDS // 2
    for y in range(ROWS):
        ready[0].append(copy(hbm[0].at[:cut, :, y, :], main.at[:cut, y]))
    for y in range(ROWS):
        ready[1].append(copy(hbm[0].at[cut:, :, y, :], main.at[cut:LAME, y]))
        ready[1] += [copy(hbm[1 + k].at[:, y, :], main.at[LAME + k, y]) for k in range(3)]
    rest = [copy(hbm[4 + k], x) for k, x in enumerate((ocean, deep, floor, wet))]
    difference_matrix(before, (27.0, -27.0, -1.0, 1.0), (0, 1, -1, 2))
    difference_matrix(after, (27.0, -27.0, -1.0, 1.0), (-1, 0, -2, 1))
    pickers = [picker(t) for t in range(TILES)]
    for one in rest:
        one.wait()
    planes = [ocean[k] for k in range(3)] + [deep[...]]
    planes += [floor[...].astype(jnp.float32), wet[...].astype(jnp.float32)]
    for k, x in enumerate(planes):
        store(flat, k, x)
    size = SUB * ROWS
    for half in range(2):
        for one in ready[half]:
            one.wait()
        mine = range(half * cut, (half + 1) * cut)
        total = None
        for t in range(TILES):
            x = [main[f, y, t * SUB : (t + 1) * SUB, :] for f in mine for y in range(ROWS)]
            x = x if half else x + planes
            part = jnp.dot(split(jnp.concatenate(x, axis=0), 2), pickers[t], preferred_element_type=jnp.float32)
            total = part if total is None else total + part
        for ref, ref_flat, x in ((own, own_flat, total[:, :LANES]), (other, other_flat, total[:, LANES:])):
            ref[mine[0] * size : (mine[-1] + 1) * size, :] = x[: cut * size, :]
            if not half:
                ref_flat[...] = x[cut * size :, :]
    grid = Grid()
    edges = own, other, own_flat, other_flat

    @pl.when((flags[0] & 1) == 1)
    def _():
        pack(grid, *edges, True, odd_way)
        pack(grid, *edges, False, even_way)

    @pl.when((flags[0] & 1) == 0)
    def _():
        pack(grid, *edges, False, odd_way)
        pack(grid, *edges, True, even_way)

    odd = (flags[1] & 1) == 1
    for k, ((_, below), (_, above)) in enumerate(zip(BUOY_LOW, BUOY_HIGH)):
        for t in range(TILES):
            a, b = [main[BUOY, y, t * SUB : (t + 1) * SUB, :] for y in (below, above)]
            store(early_even, k * TILES + t, jnp.where(odd, a, b))
            store(early_odd, k * TILES + t, jnp.where(odd, b, a))


def speeds(grid, stress, speed, buoy, todo, put):
    sxx, syy, szz, sxy, sxz, syz = stress
    forth = [(VX, y) for c, y in todo if c == VX]
    back = [(c, y) for c, y in todo if c != VX]
    change = dict(zip(forth, grid.along_rows(grid.after, [(sxx, y) for _, y in forth])))
    change.update(zip(back, grid.along_rows(grid.before, [(sxy if c == VY else sxz, y) for c, y in back])))
    for y in range(ROWS):
        parts = [c for c in (VX, VY, VZ) if (c, y) in todo]
        if not parts:
            continue
        for t in range(SPAN):
            rate = RATE * buoy(y, t)
            for c in parts:
                a = change[c, y][t]
                if c == VX:
                    a = a + grid.by(sxy, y, t) + grid.bz(sxz, y, t)
                elif c == VY:
                    a = a + grid.fy(syy, y, t) + grid.bz(syz, y, t)
                else:
                    a = a + grid.by(syz, y, t) + grid.fz(szz, y, t)
                put(c, y, t, speed(c)(y, t) + rate * a)


def stresses(grid, rows, tiles, speed, stress, lame, shear, put, done=lambda y: None):
    vx, vy, vz = [speed(c) for c in (VX, VY, VZ)]
    back = grid.along_rows(grid.before, [(vx, y) for y in rows])
    forth = grid.along_rows(grid.after, [(v, y) for v in (vy, vz) for y in rows])
    for i, y in enumerate(rows):
        for t in range(tiles):
            strain_x = back[i][t]
            strain_y = grid.by(vy, y, t)
            strain_z = grid.bz(vz, y, t)
            mu = RATE * shear(y, t)
            spread = (RATE * lame(y, t)) * (strain_x + strain_y + strain_z)
            two = mu + mu
            put(SXX, y, t, stress(SXX)(y, t) + (spread + two * strain_x))
            put(SYY, y, t, stress(SYY)(y, t) + (spread + two * strain_y))
            put(SZZ, y, t, stress(SZZ)(y, t) + (spread + two * strain_z))
            put(SXY, y, t, stress(SXY)(y, t) + mu * (grid.fy(vx, y, t) + forth[i][t]))
            put(SXZ, y, t, stress(SXZ)(y, t) + mu * (grid.fz(vx, y, t) + forth[len(rows) + i][t]))
            put(SYZ, y, t, stress(SYZ)(y, t) + mu * (grid.fz(vy, y, t) + grid.fy(vz, y, t)))
        done(y)


def flat_edge(grid, at, k):
    return grid.edge(grid.beside(at(1)), 0) if k == 0 else None


def partial_level(grid, flat, put):
    for k in range(2):
        x, y = flat(FLUX_X, k), flat(FLUX_Y, k)
        edge = flat_edge(grid, lambda q: flat(FLUX_X, q), k)
        spread = 0.5 * (grid.along(x, 1, edge) - grid.along(x, -1, edge))
        spread = spread + 0.5 * (grid.across(y, 1, 0.0) - grid.across(y, -1, 0.0))
        put(k, flat(LEVEL, k) - OCEAN_RATE * (flat(WET, k) * spread))


def cells(rows, tiles):
    return [(f, y, t) for f, y in rows for t in tiles]


class Message:
    def __init__(self, tiles):
        self.at = {which: i for i, which in enumerate(tiles)}
        self.base = len(tiles) * SUB
        self.size = self.base + 2 * SUB


ALL, INSIDE = range(SPAN), range(TILES)
SIDES = (WINDOW,)
EARLY = [{which: i for i, which in enumerate(cells(rows, INSIDE))} for rows in (BUOY_HIGH, BUOY_LOW)]
FIRST = [
    Message(cells(rows, ALL) + cells(buoy, SIDES))
    for rows, buoy in ((SPEED_HIGH + STRESS_HIGH, BUOY_HIGH), (SPEED_LOW + STRESS_LOW, BUOY_LOW))
]
LATER = [
    Message(cells(speed, INSIDE) + cells(rest, ALL))
    for speed, rest in ((SPEED_HIGH, STRESS_HIGH), (SPEED_LOW, STRESS_LOW))
]


def message_tiles(kind):
    return max(m.size for m in kind) // SUB


def send(kind, odd, field, line, even_way, odd_way):
    high, low = kind

    def fill(message, edge, out):
        for (f, y, t), at in message.at.items():
            store(out, at, field(f)(y, t))
        at = message.base
        for which in LINES:
            for k in range(2):
                out[at : at + 1, :] = line(which, k, edge)
                at += 1
        out[at : at + 6, :] = jnp.zeros((6, LANES), jnp.float32)
        tail = out.shape[0]
        if message.size < tail:
            out[message.size : tail, :] = jnp.zeros((tail - message.size, LANES), jnp.float32)

    @pl.when(odd)
    def _():
        fill(high, ROWS - 1, odd_way)
        fill(low, 0, even_way)

    @pl.when(jnp.logical_not(odd))
    def _():
        fill(high, ROWS - 1, even_way)
        fill(low, 0, odd_way)


class Received:
    def __init__(self, message, odd, if_odd, if_even):
        self.message, self.odd, self.if_odd, self.if_even = message, odd, if_odd, if_even

    def __call__(self, f, y, t):
        at = self.message.at[f, y, t]
        return jnp.where(self.odd, tile(self.if_odd, at), tile(self.if_even, at))

    def line(self, which, k):
        at = self.message.base + 2 * LINES.index(which) + k
        return jnp.where(self.odd, row(self.if_odd, at), row(self.if_even, at))


def received(kind, odd, even_in, odd_in):
    return Received(kind[0], odd, even_in, odd_in), Received(kind[1], odd, odd_in, even_in)


def early(odd, even_in, odd_in, later):
    def reader(at, if_odd, if_even, rest):
        def read(f, y, t):
            if (f, y, t) not in at:
                return rest(f, y, t)
            return jnp.where(odd, tile(if_odd, at[f, y, t]), tile(if_even, at[f, y, t]))

        return read

    return reader(EARLY[0], even_in, odd_in, later[0]), reader(EARLY[1], odd_in, even_in, later[1])


AROUND = ROWS + 4


def finish(grid, tiles, partial, stress, buoy, lo, hi, lo_buoy, hi_buoy, speed):
    sxy, syy, syz = [stress(f) for f in (SXY, SYY, SYZ)]

    def put(c, y, t, value):
        store(speed, (c * AROUND + y + 2) * SPAN + t, value)

    for t in range(SPAN):
        for c, f in ((VX, SXY), (VZ, SYZ)):
            two, one = lo(f, 6, t), lo(f, 7, t)
            rate = [RATE * buoy(y, t) for y in (0, 1, 7)]
            put(c, 0, t, partial(c, 0, t) + rate[0] * (two - 27.0 * one))
            put(c, 1, t, partial(c, 1, t) + rate[1] * one)
            put(c, 7, t, partial(c, 7, t) - rate[2] * hi(f, 0, t))
        h8, h9 = hi(SYY, 0, t), hi(SYY, 1, t)
        put(VY, 0, t, partial(VY, 0, t) + (RATE * buoy(0, t)) * lo(SYY, 7, t))
        put(VY, 6, t, partial(VY, 6, t) - (RATE * buoy(6, t)) * h8)
        put(VY, 7, t, partial(VY, 7, t) + (RATE * buoy(7, t)) * (27.0 * h8 - h9))
    for t in range(tiles):
        b2, b1 = RATE * lo_buoy(BUOY, 6, t), RATE * lo_buoy(BUOY, 7, t)
        b8, b9 = RATE * hi_buoy(BUOY, 0, t), RATE * hi_buoy(BUOY, 1, t)
        put(VX, -1, t, lo(VX, 7, t) - b1 * sxy(0, t))
        put(VY, -2, t, lo(VY, 6, t) - b2 * syy(0, t))
        put(VY, -1, t, lo(VY, 7, t) + b1 * (27.0 * syy(0, t) - syy(1, t)))
        put(VZ, -1, t, lo(VZ, 7, t) - b1 * syz(0, t))
        put(VX, 8, t, hi(VX, 0, t) + b8 * (sxy(6, t) - 27.0 * sxy(7, t)))
        put(VX, 9, t, hi(VX, 1, t) + b9 * sxy(7, t))
        put(VY, 8, t, hi(VY, 0, t) + b8 * syy(7, t))
        put(VZ, 8, t, hi(VZ, 0, t) + b8 * (syz(6, t) - 27.0 * syz(7, t)))
        put(VZ, 9, t, hi(VZ, 1, t) + b9 * syz(7, t))


def seafloor(grid, vz, y, floors, out, index):
    total = None
    for t in range(TILES):
        part = jnp.where(floors[0] == grid.depth[t], vz(y, t), 0.0)
        total = part if total is None else total + part
    out[index : index + 1, :] = jnp.sum(total, axis=0, keepdims=True)
    if len(floors) > 1:
        part = jnp.where(floors[1] == grid.depth[WINDOW], vz(y, WINDOW), 0.0)
        out[2 * SUB + index : 2 * SUB + index + 1, :] = jnp.sum(part, axis=0, keepdims=True)


def sea(grid, speed, level, now, fixed, line, lo, hi, sums, new, last):
    vz = speed(VZ)
    for y in range(ROWS):
        seafloor(grid, vz, y, [line(FLOOR, k, y) for k in range(2)], sums, y)
    ends = 1 if last else 2
    for y, side, at in ((-1, lo, ROWS), (ROWS, hi, ROWS + 1)):
        seafloor(grid, vz, y, [side.line(FLOOR, k) for k in range(ends)], sums, at)
    floors, beyond = [tile(sums, 0), grid.every_group(tile(sums, 2))], [tile(sums, 1), None]
    if not last:
        beyond[1] = grid.every_group(tile(sums, 3))
    sub = grid.sub
    levels, lows, highs = [], [], []
    for k in range(2):
        near = jnp.where(sub == 0, lo.line(FLUX_Y, k), jnp.where(sub == ROWS - 1, -hi.line(FLUX_Y, k), 0.0))
        levels.append(level(k) + fixed(WET, k) * (UPLIFT * floors[k] + (0.5 * OCEAN_RATE) * near))
        new(LEVEL, k, levels[k])
        if k < ends:
            for side, at, y, sign, out in ((lo, 0, 0, -1.0, lows), (hi, 1, ROWS - 1, 1.0, highs)):
                mine = (sign * 0.5 * OCEAN_RATE) * line(FLUX_Y, k, y)
                rest = UPLIFT * beyond[k][at : at + 1, :] + mine
                out.append(side.line(None, k) + side.line(WET, k) * rest)
    for k in range(ends):
        wet, deep = fixed(WET, k), fixed(DEPTH, k)
        edge = flat_edge(grid, lambda q: levels[q], k)
        slope_x = 0.5 * (grid.along(levels[k], 1, edge) - grid.along(levels[k], -1, edge))
        slope_y = 0.5 * (grid.across(levels[k], 1, highs[k]) - grid.across(levels[k], -1, lows[k]))
        for which, slope in ((FLUX_X, slope_x), (FLUX_Y, slope_y)):
            x = now(which, k)
            edge = flat_edge(grid, lambda q: now(which, q), k)
            laplace = grid.along(x, 1, edge) + grid.along(x, -1, edge) - 4.0 * x
            laplace = laplace + grid.across(x, 1, hi.line(which, k)) + grid.across(x, -1, lo.line(which, k))
            new(which, k, wet * (x - OCEAN_RATE * deep * slope + VISCOUS * laplace))
    return levels


def press(grid, levels, fixed, line, pressure):
    for k in range(2):
        store(pressure, k, LOADING * fixed(WET, k) * levels[k])

    def load(y, t):
        k = 1 if t == WINDOW else 0
        return jnp.where(line(FLOOR, k, y) == grid.depth[t], row(pressure, k * ROWS + y), 0.0)

    return load


def edge_index(c, y):
    return OPEN.index((c, y)) * SPAN


def block_index(c, y):
    return (c * ROWS + y) * SPAN


def start_kernel(
    flags, before, after, main, flat, own, own_flat, even_in, odd_in, early_odd, early_even,
    windows, flat_windows, partial, level, even_way, odd_way,
):
    grid = Grid(flags[2], before, after)
    odd = (flags[0] & 1) == 1
    for f in range(0, FIELDS, 2):
        for q in range(0, ROWS, 2):
            places = [h * ROWS + y for y in (q, q + 1) for h in (f, f + 1)]
            items = [tile(own, p) for p in places]
            for p, x in zip(places, unpack(grid, items, odd, even_in, odd_in, (f * ROWS // 2 + q) // 2)):
                store(windows, p, x)
    items = [tile(own_flat, k) for k in range(6)]
    base = FIELDS * ROWS // 4
    for k, x in enumerate(unpack(grid, items[:4], odd, even_in, odd_in, base)):
        store(flat_windows, k, x)
    for k, x in enumerate(unpack(grid, items[4:] * 2, odd, even_in, odd_in, base + 1)[:2]):
        store(flat_windows, 4 + k, x)

    field = fields_of(main, windows)
    speeds(
        grid, [inside(field(f)) for f in range(SXX, SYZ + 1)], field, field(BUOY), OPEN,
        lambda c, y, t, value: store(partial, edge_index(c, y) + t, value),
    )
    flats = (flat, flat_windows)
    partial_level(grid, lambda f, k: tile(flats[k], f), lambda k, value: store(level, k, value))

    def rows_of(f):
        return (lambda y, t: tile(partial, edge_index(f, y) + t)) if f < 3 else field(f)

    def line(which, k, y):
        return row(level, k * ROWS + y) if which is None else row(flats[k], which * ROWS + y)

    send(FIRST, (flags[1] & 1) == 1, rows_of, line, even_way, odd_way)


def start_rest_kernel(flags, before, after, main, windows, speed_out, stress_out):
    grid = Grid(flags[2], before, after)
    field = fields_of(main, windows)
    speeds(
        grid, [inside(field(f)) for f in range(SXX, SYZ + 1)], field, field(BUOY), CLOSED,
        lambda c, y, t, value: store(speed_out, block_index(c, y) + t, value),
    )
    stresses(
        grid, INNER, SPAN, block_reader(speed_out, VX), field,
        field(LAME), field(SHEAR),
        lambda f, y, t, value: store(stress_out, block_index(f - SXX, y) + t, value),
    )


def block_reader(ref, least):
    return lambda f: lambda y, t, *start: tile(ref, block_index(f - least, y) + t, *start)


def speed_reader(around, block):
    def speed(c):
        def read(y, t, *start):
            if (c, y) in CLOSED:
                return tile(block, block_index(c, y) + t, *start)
            return tile(around, (c * AROUND + y + 2) * SPAN + t, *start)

        return read

    return speed


def middle_kernel(
    flags, before, after, main, windows, flat, flat_windows, partial, level, speed_in, stress_in,
    early_even, early_odd, even_in, odd_in,
    speed_out, stress_out, ocean, partial_out, level_out, even_way, odd_way,
    sums, pressure,
):
    grid = Grid(flags[2], before, after)
    odd = (flags[1] & 1) == 1
    lo, hi = received(FIRST, odd, even_in, odd_in)
    field = fields_of(main, windows)
    finish(
        grid, SPAN, lambda c, y, t: tile(partial, edge_index(c, y) + t), field, field(BUOY), lo, hi, *early(odd, early_even, early_odd, (lo, hi)),
        speed_out,
    )
    speed = speed_reader(speed_out, speed_in)
    flats = (flat, flat_windows)
    fixed = lambda f, k: tile(flats[k], f)
    line = lambda f, k, y: row(flats[k], f * ROWS + y)

    def new(f, k, value):
        store(ocean, 3 * k + f, value)

    levels = sea(grid, speed, lambda k: tile(level, k), fixed, fixed, line, lo, hi, sums, new, False)
    load = press(grid, levels, fixed, line, pressure)

    def put(f, y, t, value):
        store(stress_out, block_index(f - SXX, y) + t, value - load(y, t) if f == SZZ else value)

    stresses(grid, OUTER, SPAN, speed, field, field(LAME), field(SHEAR), put)
    for f in range(SXX, SYZ + 1):
        for y in INNER:
            for t in range(SPAN):
                put(f, y, t, tile(stress_in, block_index(f - SXX, y) + t))
    stress = block_reader(stress_out, SXX)
    speeds(
        grid, [inside(stress(f)) for f in range(SXX, SYZ + 1)], speed, field(BUOY), OPEN,
        lambda c, y, t, value: store(partial_out, edge_index(c, y) + t, value),
    )
    moving = lambda f, k: tile(flats[k], f) if f >= DEPTH else tile(ocean, 3 * k + f)
    partial_level(grid, moving, lambda k, value: store(level_out, k, value))

    def rows_of(f):
        return (lambda y, t: tile(partial_out, edge_index(f, y) + t)) if f < 3 else stress(f)

    def line_out(which, k, y):
        if which is None:
            return row(level_out, k * ROWS + y)
        return line(which, k, y) if which >= DEPTH else row(ocean, (3 * k + which) * ROWS + y)

    send(LATER, odd, rows_of, line_out, even_way, odd_way)


def copy_rows(ref, index, hbm, f, y, sem):
    return pltpu.make_async_copy(ref.at[index * SUB : (index + TILES) * SUB, :], hbm.at[f, :, y, :], sem)


BY_ROWS = (SXX, SYY)
BY_FIELD = (SZZ, SXY, SXZ, SYZ)


def middle_rest_kernel(flags, before, after, main, windows, around, speed_in, stress_in, speed_out, stress_out, wave_hbm, sem):
    grid = Grid(flags[2], before, after)
    field = fields_of(main, windows)
    stress = block_reader(stress_in, SXX)
    speeds(
        grid, [inside(stress(f)) for f in range(SXX, SYZ + 1)], speed_reader(around, speed_in), field(BUOY), CLOSED,
        lambda c, y, t, value: store(speed_out, block_index(c, y) + t, value),
    )
    sent = [copy_rows(speed_out, block_index(c, y), wave_hbm, c, y, sem.at[i]) for i, (c, y) in enumerate(CLOSED)]
    for one in sent:
        one.start()
    stresses(
        grid, INNER, TILES, block_reader(speed_out, VX), stress,
        field(LAME), field(SHEAR),
        lambda f, y, t, value: store(stress_out, block_index(f - SXX, y) + t, value),
    )
    for f in BY_ROWS:
        for y in INNER:
            sent.append(copy_rows(stress_out, block_index(f - SXX, y), wave_hbm, f, y, sem.at[len(sent)]))
            sent[-1].start()
    for one in sent:
        one.wait()


def last_kernel(
    flags, before, after, main, windows, flat, flat_windows, stress_in, ocean_in, partial, level, speed_in, inner_in,
    early_even, early_odd, even_in, odd_in, wave_in,
    wave_hbm, ocean_out,
    sums, pressure, around, turned, wave, sem,
):
    grid = Grid(flags[2], before, after)
    odd = (flags[1] & 1) == 1
    lo, hi = received(LATER, odd, even_in, odd_in)
    lo_buoy, hi_buoy = early(odd, early_even, early_odd, (lo, hi))
    field = fields_of(main, windows)
    stress = block_reader(stress_in, SXX)
    finish(
        grid, TILES, lambda c, y, t: tile(partial, edge_index(c, y) + t), stress, field(BUOY),
        lo, hi, lo_buoy, hi_buoy, around,
    )
    speed = speed_reader(around, speed_in)
    sent = []

    def copy(source, target):
        sent.append(pltpu.make_async_copy(source, target, sem.at[len(sent)]))
        sent[-1].start()

    for c, y in OPEN:
        sent.append(copy_rows(around, (c * AROUND + y + 2) * SPAN, wave_hbm, c, y, sem.at[len(sent)]))
        sent[-1].start()
    flats = (flat, flat_windows)
    fixed = lambda f, k: tile(flats[k], f)

    def line(f, k, y):
        return row(flats[k], f * ROWS + y) if f >= DEPTH else row(ocean_in, (3 * k + f) * ROWS + y)

    def new(f, k, value):
        if k == 0:
            store(ocean_out, f, value)

    levels = sea(
        grid, speed, lambda k: tile(level, k), lambda f, k: tile(ocean_in, 3 * k + f), fixed, line, lo, hi, sums, new, True
    )
    load = press(grid, levels, fixed, line, pressure)

    size = TILES * SUB * ROWS

    def put(f, y, t, value):
        if f in BY_ROWS:
            turned[f - SXX, y, t * SUB : (t + 1) * SUB, :] = value
            return
        if f == SZZ:
            value = value - load(y, t)
        wave[pl.ds(BY_FIELD.index(f) * size + t * SUB * ROWS + y, SUB, stride=ROWS), :] = value

    def done(y):
        copy(turned.at[:, y], wave_hbm.at[SXX : SYY + 1, :, y, :])

    stresses(grid, OUTER, TILES, speed, stress, field(LAME), field(SHEAR), put, done)
    for f in BY_FIELD:
        for y in INNER:
            for t in range(TILES):
                put(f, y, t, tile(inner_in, block_index(f - SXX, y) + t))
    copy(wave, wave_hbm.at[SZZ : SYZ + 1].reshape(len(BY_FIELD) * size, LANES))
    for one in sent:
        one.wait()


IN_VMEM = pl.BlockSpec(memory_space=pltpu.VMEM)
IN_SMEM = pl.BlockSpec(memory_space=pltpu.SMEM)
IN_HBM = pl.BlockSpec(memory_space=pltpu.HBM)


def call(kernel, tiles, scratch, *arguments, flags=None, place=IN_VMEM, out_places=None, work=1, aliases={}):
    specs = place if isinstance(place, list) else [place] * len(arguments)
    if flags is not None:
        arguments, specs = (flags, *arguments), [IN_SMEM] + specs
    moved = sum(x.size for x in arguments) + sum(n for n in tiles if isinstance(n, int)) * SUB * LANES
    return pl.pallas_call(
        kernel,
        out_shape=[n if hasattr(n, "dtype") else jax.ShapeDtypeStruct((n * SUB, LANES), jnp.float32) for n in tiles],
        in_specs=specs,
        out_specs=out_places or [IN_VMEM] * len(tiles),
        scratch_shapes=scratch,
        input_output_aliases=aliases,
        cost_estimate=pl.CostEstimate(flops=work * 1000000, bytes_accessed=4 * moved, transcendentals=0),
        compiler_params=pltpu.CompilerParams(vmem_limit_bytes=24 * 1024 * 1024),
    )(*arguments)


def planes(n):
    return pltpu.VMEM((n * SUB, LANES), jnp.float32)


def swap(x, axis, start):
    pairs = [(i, i + 1) for i in range(start, lax.axis_size(axis) - 1, 2)]
    return lax.ppermute(x, axis, pairs + [(j, i) for i, j in pairs])


def local(*arguments):
    ocean_state = arguments[4]
    inputs = [pltpu.with_memory_space_constraint(x, pltpu.HBM) for x in arguments]
    flags = jnp.stack([lax.axis_index("gx"), lax.axis_index("gy"), 0])
    matrix = jax.ShapeDtypeStruct((2 * LANES, SPAN * LANES), jnp.bfloat16)
    cells4 = jax.ShapeDtypeStruct((FIELDS, ROWS, TILES * SUB, LANES), jnp.float32)

    edge = FIELDS * ROWS // 4 + 2
    before, after, main, flat, own, own_flat, even_way, odd_way, early_even, early_odd = call(
        edges_kernel, [matrix, matrix, cells4, 6, FIELDS * ROWS, 6, edge, edge, 2 * TILES, 2 * TILES],
        [planes(FIELDS * ROWS), planes(6)] + [pltpu.VMEM(x.shape, x.dtype) for x in inputs[4:]]
        + [pltpu.SemaphoreType.DMA((4 + 5 * ROWS,))],
        *inputs, flags=flags, place=IN_HBM,
    )
    x_in = swap(even_way, "gx", 0), swap(odd_way, "gx", 1)
    early_in = swap(early_even, "gy", 0), swap(early_odd, "gy", 1)
    main = main.reshape(-1, LANES)
    first, later = [message_tiles(kind) for kind in (FIRST, LATER)]
    edges, block = len(OPEN) * SPAN, ROWS * SPAN
    windows, flat_windows, partial, level, even_way, odd_way = call(
        start_kernel, [FIELDS * ROWS, 6, edges, 2, first, first], [],
        before, after, main, flat, own, own_flat, *x_in, *early_in[::-1], flags=flags,
    )
    y_in = swap(even_way, "gy", 0), swap(odd_way, "gy", 1)
    speed, inner = call(start_rest_kernel, [3 * block, 6 * block], [], before, after, main, windows, flags=flags, work=4)
    around, stress, ocean, partial, level, even_way, odd_way = call(
        middle_kernel, [3 * AROUND * SPAN, 6 * block, 6, edges, 2, later, later], [planes(4), planes(2)],
        before, after, main, windows, flat, flat_windows, partial, level, speed, inner, *early_in, *y_in, flags=flags,
    )
    y_in = swap(even_way, "gy", 0), swap(odd_way, "gy", 1)
    wave = jax.ShapeDtypeStruct(arguments[0].shape, jnp.float32)
    speed, inner, wave_part = call(
        middle_rest_kernel, [3 * block, 6 * block, wave],
        [pltpu.SemaphoreType.DMA((len(CLOSED) + len(BY_ROWS) * len(INNER),))],
        before, after, main, windows, around, speed, stress, flags=flags, out_places=[IN_VMEM, IN_VMEM, IN_HBM], work=4,
    )
    operands = (
        before, after, main, windows, flat, flat_windows, stress, ocean, partial, level, speed, inner, *early_in, *y_in, wave_part
    )
    wave_out, ocean_out = call(
        last_kernel, [wave, 3],
        [
            planes(4), planes(2), planes(3 * AROUND * SPAN),
            pltpu.VMEM((len(BY_ROWS), *cells4.shape[1:]), jnp.float32), planes(len(BY_FIELD) * ROWS * TILES),
            pltpu.SemaphoreType.DMA((len(OPEN) + len(OUTER) + 1,)),
        ],
        *operands, flags=flags, place=[IN_VMEM] * (len(operands) - 1) + [IN_HBM], out_places=[IN_HBM, IN_VMEM],
        aliases={len(operands): 0},
    )
    return wave_out, ocean_out.reshape(ocean_state.shape)


def solution(mesh):
    in_specs = (
        P(None, None, "gy", "gx"),
        P(None, "gy", "gx"),
        P(None, "gy", "gx"),
        P(None, "gy", "gx"),
        P(None, "gy", "gx"),
        P("gy", "gx"),
        P("gy", "gx"),
        P("gy", "gx"),
    )
    out_specs = (P(None, None, "gy", "gx"), P(None, "gy", "gx"))
    return jax.shard_map(local, mesh=mesh, in_specs=in_specs, out_specs=out_specs, check_vma=False)
```

```python
import jax
import jax.numpy as jnp
from jax import lax
from jax.experimental import pallas as pl
from jax.experimental.pallas import tpu as pltpu
from jax.sharding import PartitionSpec as P

RATE = 0.3 / 24.0
OCEAN_RATE = 0.3
UPLIFT = 0.5
LOADING = 0.5
VISCOUS = 0.1

ROWS = 8
SUB = 8
LANES = 128
EDGE = 8
GROUP = 2 * EDGE
TILES = 4
HALF = TILES * GROUP
SPAN = TILES + 1
WINDOW = TILES

LEVEL, FLUX_X, FLUX_Y, DEPTH, FLOOR, WET = range(6)
VX, VY, VZ, SXX, SYY, SZZ, SXY, SXZ, SYZ, LAME, SHEAR, BUOY = range(12)
FIELDS = 12

OPEN = ((VX, 0), (VX, 1), (VX, 7), (VY, 0), (VY, 6), (VY, 7), (VZ, 0), (VZ, 1), (VZ, 7))
CLOSED = tuple((c, y) for y in range(ROWS) for c in (VX, VY, VZ) if (c, y) not in OPEN)
INNER = (3, 4)
OUTER = tuple(y for y in range(ROWS) if y not in INNER)

SPEED_HIGH = ((VX, 7), (VY, 6), (VY, 7), (VZ, 7))
SPEED_LOW = ((VX, 0), (VX, 1), (VY, 0), (VZ, 0), (VZ, 1))
STRESS_HIGH = ((SXY, 6), (SXY, 7), (SYY, 7), (SYZ, 6), (SYZ, 7))
STRESS_LOW = ((SXY, 0), (SYY, 0), (SYY, 1), (SYZ, 0))
BUOY_HIGH = ((BUOY, 6), (BUOY, 7))
BUOY_LOW = ((BUOY, 0), (BUOY, 1))
LINES = (None, WET, FLOOR, FLUX_X, FLUX_Y)


def rest(x, size):
    return x & (size - 1)


def count(x, size):
    return x >> (size.bit_length() - 1)


def rolled(x, shift, axis):
    shift %= x.shape[axis]
    return x if shift == 0 else pltpu.roll(x, shift, axis)


def tile(ref, index, start=None):
    if start is None:
        return ref[index * SUB : (index + 1) * SUB, :]
    return ref[pl.ds(start + index * SUB, SUB), :]


def row(ref, index):
    return ref[index : index + 1, :]


def store(ref, index, value):
    ref[index * SUB : (index + 1) * SUB, :] = value


def split(x, parts):
    out = []
    for part in range(parts):
        out.append(x.astype(jnp.bfloat16))
        if part + 1 < parts:
            x = x - out[-1].astype(jnp.float32)
    return jnp.concatenate(out, axis=1)


def minus(a, b):
    if b is None:
        return a
    return -b if a is None else a - b


def near_far(a, b, c, d):
    near, far = 27.0 * minus(a, b), minus(c, d)
    return near if c is None and d is None else near - far


class Grid:
    def __init__(self, origin=None, before=None, after=None):
        self.origin, self.before, self.after = origin, before, after
        self.sub = lax.broadcasted_iota(jnp.int32, (SUB, LANES), 0)
        self.lane = lax.broadcasted_iota(jnp.int32, (SUB, LANES), 1)
        self.first = rest(self.lane, GROUP) < EDGE
        self.left = self.lane < HALF
        self.group = count(self.lane, GROUP)
        self.zero = jnp.zeros((SUB, LANES), jnp.float32)
        depth = [self.sub + SUB * t for t in range(TILES)] + [self.sub + SUB * rest(self.group, TILES)]
        self.depth = [d.astype(jnp.float32) for d in depth]

    def beside(self, window):
        return jnp.where(self.first, window, rolled(window, HALF, 1))

    def edge(self, beside, t):
        return None if t == WINDOW else rolled(beside, LANES - EDGE - GROUP * t, 1)

    def along(self, x, offset, edge):
        if edge is not None:
            lane = self.lane
            keep = {-1: lane == LANES - 1, -2: lane >= LANES - 2, 1: lane == 0, 2: lane <= 1}[offset]
            x = jnp.where(keep, edge, x)
        return rolled(x, -offset, 1)

    def down(self, field, y, t, offset):
        if t < WINDOW:
            x = field(y, t, self.origin + offset)
            if t == 0 and offset < 0:
                return jnp.where(self.sub >= -offset, x, 0.0)
            if t == TILES - 1 and offset > 0:
                return jnp.where(self.sub < SUB - offset, x, 0.0)
            return x
        x, at = field(y, t), rest(self.lane, HALF)
        if offset < 0:
            beyond, far = jnp.where(at >= GROUP, rolled(x, GROUP, 1), 0.0), self.sub >= SUB + offset
        else:
            beyond, far = jnp.where(at < HALF - GROUP, rolled(x, -GROUP, 1), 0.0), self.sub < offset
        return rolled(jnp.where(far, beyond, x), -offset, 0)

    def fz(self, field, y, t):
        down = lambda offset: self.down(field, y, t, offset)
        return near_far(down(1), field(y, t), down(2), down(-1))

    def bz(self, field, y, t):
        down = lambda offset: self.down(field, y, t, offset)
        return near_far(field(y, t), down(-1), down(1), down(-2))

    def along_rows(self, matrix, rows):
        main = split(jnp.concatenate([f(y, t) for f, y in rows for t in range(TILES)], axis=0), 2)
        sides = [f(y, WINDOW) for f, y in rows]
        side = split(jnp.concatenate(sides + sides[: len(sides) % 2], axis=0), 2)
        main = jnp.dot(main, matrix[:, :LANES], preferred_element_type=jnp.float32)
        side = jnp.dot(side, matrix[...], preferred_element_type=jnp.float32)
        out = []
        for i in range(len(rows)):
            part = side[i * SUB : (i + 1) * SUB, :]
            parts = [part[:, t * LANES : (t + 1) * LANES] for t in range(SPAN)]
            tiles = [
                main[(i * TILES + t) * SUB : (i * TILES + t + 1) * SUB, :] + parts[1 + t] for t in range(TILES)
            ]
            out.append(tiles + parts[:1])
        return out

    def fy(self, field, y, t):
        return near_far(field(y + 1, t), field(y, t), field(y + 2, t), field(y - 1, t))

    def by(self, field, y, t):
        return near_far(field(y, t), field(y - 1, t), field(y + 1, t), field(y - 2, t))

    def windows(self, own, from_left, from_right):
        return jnp.where(
            self.left, jnp.where(self.first, from_left, own), jnp.where(self.first, own, from_right)
        )

    def every_group(self, x):
        for shift in (GROUP, 2 * GROUP):
            x = x + jnp.where(rest(self.lane, HALF) >= shift, rolled(x, shift, 1), rolled(x, shift - HALF, 1))
        return x

    def across(self, x, offset, beside):
        end = 0 if offset < 0 else ROWS - 1
        return jnp.where(self.sub == end, beside, rolled(x, -offset, 0))


def inside(field):
    return lambda y, t, *start: field(y, t, *start) if 0 <= y < ROWS else None


def fields_of(main, windows):
    def field(f):
        def read(y, t, *start):
            return tile(windows, f * ROWS + y) if t == WINDOW else tile(main, (f * ROWS + y) * TILES + t, *start)

        return read

    return field


def pack(grid, own, other, flat, other_flat, to_right, out):
    for index, (near, far) in enumerate(zip(edge_groups(own, flat), edge_groups(other, other_flat))):
        a, b, c, d = near[0], far[1], near[2], far[3]
        if not to_right:
            a, b, c, d = b, a, d, c
        store(out, index, jnp.where(grid.left, jnp.where(grid.first, a, b), jnp.where(grid.first, c, d)))


def edge_groups(own, own_flat):
    groups = [
        [tile(own, h * ROWS + y) for y in (q, q + 1) for h in (f, f + 1)]
        for f in range(0, FIELDS, 2)
        for q in range(0, ROWS, 2)
    ]
    flat = [tile(own_flat, k) for k in range(6)]
    return groups + [flat[:4], flat[4:] * 2]


def unpack(grid, items, odd, even_in, odd_in, index):
    x, y = tile(even_in, index), tile(odd_in, index)
    before, after = jnp.where(odd, x, y), jnp.where(odd, y, x)
    befores = [before, rolled(before, -EDGE, 1), rolled(before, HALF, 1), rolled(before, HALF - EDGE, 1)]
    afters = [rolled(after, HALF, 1), rolled(after, HALF + EDGE, 1), after, rolled(after, EDGE, 1)]
    return [grid.windows(*three) for three in zip(items, befores, afters)]


def difference_matrix(out, weights, offsets):
    shape = (LANES, LANES)
    k, n = [lax.broadcasted_iota(jnp.int32, shape, axis) for axis in range(2)]

    def weight(apart):
        total = jnp.zeros(shape, jnp.float32)
        for w, offset in zip(weights, offsets):
            total = jnp.where(apart == offset, w, total)
        return total

    inner, left = rest(k, GROUP), k < HALF
    column = jnp.where(left, inner - EDGE, LANES - EDGE + inner)
    outside = (left & (inner < EDGE)) | (jnp.logical_not(left) & (inner >= EDGE))
    beside = jnp.where(outside, weight(n - column), 0.0)
    parts = [weight(n - k)]
    parts += [jnp.where(count(rest(k, HALF), GROUP) == t, beside, 0.0) for t in range(TILES)]
    for p, x in enumerate(parts):
        for half in range(2):
            out[half * LANES : (half + 1) * LANES, p * LANES : (p + 1) * LANES] = x.astype(jnp.bfloat16)


def picker(t):
    k, n = [lax.broadcasted_iota(jnp.int32, (LANES, LANES), axis) for axis in range(2)]
    inner, mine = rest(n, GROUP), count(rest(n, HALF), GROUP) == t
    both = []
    for swapped in (False, True):
        last = inner >= EDGE if swapped else inner < EDGE
        column = jnp.where(last, LANES - EDGE, 0) + rest(inner, EDGE)
        both.append(jnp.where(mine & (k == column), 1.0, 0.0).astype(jnp.bfloat16))
    return jnp.concatenate([jnp.concatenate(both, axis=1)] * 2, axis=0)


def edges_kernel(flags, *refs):
    hbm, refs = refs[:8], refs[8:]
    (before, after, main, flat, own, own_flat, even_way, odd_way, early_even, early_odd), refs = refs[:10], refs[10:]
    other, other_flat, ocean, deep, floor, wet, sem = refs
    sent = []

    def copy(source, target):
        sent.append(pltpu.make_async_copy(source, target, sem.at[len(sent)]))
        sent[-1].start()
        return sent[-1]

    ready = [[], []]
    cut = FIELDS // 2
    for y in range(ROWS):
        ready[0].append(copy(hbm[0].at[:cut, :, y, :], main.at[:cut, y]))
    for y in range(ROWS):
        ready[1].append(copy(hbm[0].at[cut:, :, y, :], main.at[cut:LAME, y]))
        ready[1] += [copy(hbm[1 + k].at[:, y, :], main.at[LAME + k, y]) for k in range(3)]
    flats = [copy(hbm[4 + k], x) for k, x in enumerate((ocean, deep, floor, wet))]
    difference_matrix(before, (27.0, -27.0, -1.0, 1.0), (0, 1, -1, 2))
    difference_matrix(after, (27.0, -27.0, -1.0, 1.0), (-1, 0, -2, 1))
    pickers = [picker(t) for t in range(TILES)]
    for one in flats:
        one.wait()
    planes = [ocean[k] for k in range(3)] + [deep[...]]
    planes += [floor[...].astype(jnp.float32), wet[...].astype(jnp.float32)]
    for k, x in enumerate(planes):
        store(flat, k, x)
    size = SUB * ROWS
    for half in range(2):
        for one in ready[half]:
            one.wait()
        mine = range(half * cut, (half + 1) * cut)
        total = None
        for t in range(TILES):
            x = [main[f, y, t * SUB : (t + 1) * SUB, :] for f in mine for y in range(ROWS)]
            x = x if half else x + planes
            part = jnp.dot(split(jnp.concatenate(x, axis=0), 2), pickers[t], preferred_element_type=jnp.float32)
            total = part if total is None else total + part
        for ref, ref_flat, x in ((own, own_flat, total[:, :LANES]), (other, other_flat, total[:, LANES:])):
            ref[mine[0] * size : (mine[-1] + 1) * size, :] = x[: cut * size, :]
            if not half:
                ref_flat[...] = x[cut * size :, :]
    grid = Grid()
    edges = own, other, own_flat, other_flat

    @pl.when((flags[0] & 1) == 1)
    def _():
        pack(grid, *edges, True, odd_way)
        pack(grid, *edges, False, even_way)

    @pl.when((flags[0] & 1) == 0)
    def _():
        pack(grid, *edges, False, odd_way)
        pack(grid, *edges, True, even_way)

    odd = (flags[1] & 1) == 1
    for k, ((_, below), (_, above)) in enumerate(zip(BUOY_LOW, BUOY_HIGH)):
        for t in range(TILES):
            a, b = [main[BUOY, y, t * SUB : (t + 1) * SUB, :] for y in (below, above)]
            store(early_even, k * TILES + t, jnp.where(odd, a, b))
            store(early_odd, k * TILES + t, jnp.where(odd, b, a))


def speeds(grid, stress, speed, buoy, todo, put):
    sxx, syy, szz, sxy, sxz, syz = stress
    forth = [(VX, y) for c, y in todo if c == VX]
    back = [(c, y) for c, y in todo if c != VX]
    change = dict(zip(forth, grid.along_rows(grid.after, [(sxx, y) for _, y in forth])))
    change.update(zip(back, grid.along_rows(grid.before, [(sxy if c == VY else sxz, y) for c, y in back])))
    for y in range(ROWS):
        parts = [c for c in (VX, VY, VZ) if (c, y) in todo]
        if not parts:
            continue
        for t in range(SPAN):
            rate = RATE * buoy(y, t)
            for c in parts:
                a = change[c, y][t]
                if c == VX:
                    a = a + grid.by(sxy, y, t) + grid.bz(sxz, y, t)
                elif c == VY:
                    a = a + grid.fy(syy, y, t) + grid.bz(syz, y, t)
                else:
                    a = a + grid.by(syz, y, t) + grid.fz(szz, y, t)
                put(c, y, t, speed(c)(y, t) + rate * a)


def stresses(grid, rows, tiles, speed, stress, lame, shear, put, done=lambda y: None):
    vx, vy, vz = [speed(c) for c in (VX, VY, VZ)]
    back = grid.along_rows(grid.before, [(vx, y) for y in rows])
    forth = grid.along_rows(grid.after, [(v, y) for v in (vy, vz) for y in rows])
    for i, y in enumerate(rows):
        for t in range(tiles):
            strain_x = back[i][t]
            strain_y = grid.by(vy, y, t)
            strain_z = grid.bz(vz, y, t)
            mu = RATE * shear(y, t)
            spread = (RATE * lame(y, t)) * (strain_x + strain_y + strain_z)
            two = mu + mu
            put(SXX, y, t, stress(SXX)(y, t) + (spread + two * strain_x))
            put(SYY, y, t, stress(SYY)(y, t) + (spread + two * strain_y))
            put(SZZ, y, t, stress(SZZ)(y, t) + (spread + two * strain_z))
            put(SXY, y, t, stress(SXY)(y, t) + mu * (grid.fy(vx, y, t) + forth[i][t]))
            put(SXZ, y, t, stress(SXZ)(y, t) + mu * (grid.fz(vx, y, t) + forth[len(rows) + i][t]))
            put(SYZ, y, t, stress(SYZ)(y, t) + mu * (grid.fz(vy, y, t) + grid.fy(vz, y, t)))
        done(y)


def flat_edge(grid, at, k):
    return grid.edge(grid.beside(at(1)), 0) if k == 0 else None


def partial_level(grid, flat, put):
    for k in range(2):
        x, y = flat(FLUX_X, k), flat(FLUX_Y, k)
        edge = flat_edge(grid, lambda q: flat(FLUX_X, q), k)
        spread = 0.5 * (grid.along(x, 1, edge) - grid.along(x, -1, edge))
        spread = spread + 0.5 * (grid.across(y, 1, 0.0) - grid.across(y, -1, 0.0))
        put(k, flat(LEVEL, k) - OCEAN_RATE * (flat(WET, k) * spread))


def cells(rows, tiles):
    return [(f, y, t) for f, y in rows for t in tiles]


class Message:
    def __init__(self, tiles):
        self.at = {which: i for i, which in enumerate(tiles)}
        self.base = len(tiles) * SUB
        self.size = self.base + 2 * SUB


ALL, INSIDE = range(SPAN), range(TILES)
SIDES = (WINDOW,)
EARLY = [{which: i for i, which in enumerate(cells(rows, INSIDE))} for rows in (BUOY_HIGH, BUOY_LOW)]
FIRST = [
    Message(cells(rows, ALL) + cells(buoy, SIDES))
    for rows, buoy in ((SPEED_HIGH + STRESS_HIGH, BUOY_HIGH), (SPEED_LOW + STRESS_LOW, BUOY_LOW))
]
LATER = [
    Message(cells(speed, INSIDE) + cells(rest, ALL))
    for speed, rest in ((SPEED_HIGH, STRESS_HIGH), (SPEED_LOW, STRESS_LOW))
]


def message_tiles(kind):
    return max(m.size for m in kind) // SUB


def send(kind, odd, field, line, even_way, odd_way):
    high, low = kind

    def fill(message, edge, out):
        for (f, y, t), at in message.at.items():
            store(out, at, field(f)(y, t))
        at = message.base
        for which in LINES:
            for k in range(2):
                out[at : at + 1, :] = line(which, k, edge)
                at += 1
        out[at : at + 6, :] = jnp.zeros((6, LANES), jnp.float32)
        tail = out.shape[0]
        if message.size < tail:
            out[message.size : tail, :] = jnp.zeros((tail - message.size, LANES), jnp.float32)

    @pl.when(odd)
    def _():
        fill(high, ROWS - 1, odd_way)
        fill(low, 0, even_way)

    @pl.when(jnp.logical_not(odd))
    def _():
        fill(high, ROWS - 1, even_way)
        fill(low, 0, odd_way)


class Received:
    def __init__(self, message, odd, if_odd, if_even):
        self.message, self.odd, self.if_odd, self.if_even = message, odd, if_odd, if_even

    def __call__(self, f, y, t):
        at = self.message.at[f, y, t]
        return jnp.where(self.odd, tile(self.if_odd, at), tile(self.if_even, at))

    def line(self, which, k):
        at = self.message.base + 2 * LINES.index(which) + k
        return jnp.where(self.odd, row(self.if_odd, at), row(self.if_even, at))


def received(kind, odd, even_in, odd_in):
    return Received(kind[0], odd, even_in, odd_in), Received(kind[1], odd, odd_in, even_in)


def early(odd, even_in, odd_in, later):
    def reader(at, if_odd, if_even, rest):
        def read(f, y, t):
            if (f, y, t) not in at:
                return rest(f, y, t)
            return jnp.where(odd, tile(if_odd, at[f, y, t]), tile(if_even, at[f, y, t]))

        return read

    return reader(EARLY[0], even_in, odd_in, later[0]), reader(EARLY[1], odd_in, even_in, later[1])


AROUND = ROWS + 4


def finish(grid, tiles, partial, stress, buoy, lo, hi, lo_buoy, hi_buoy, speed):
    sxy, syy, syz = [stress(f) for f in (SXY, SYY, SYZ)]

    def put(c, y, t, value):
        store(speed, (c * AROUND + y + 2) * SPAN + t, value)

    for t in range(SPAN):
        for c, f in ((VX, SXY), (VZ, SYZ)):
            two, one = lo(f, 6, t), lo(f, 7, t)
            rate = [RATE * buoy(y, t) for y in (0, 1, 7)]
            put(c, 0, t, partial(c, 0, t) + rate[0] * (two - 27.0 * one))
            put(c, 1, t, partial(c, 1, t) + rate[1] * one)
            put(c, 7, t, partial(c, 7, t) - rate[2] * hi(f, 0, t))
        h8, h9 = hi(SYY, 0, t), hi(SYY, 1, t)
        put(VY, 0, t, partial(VY, 0, t) + (RATE * buoy(0, t)) * lo(SYY, 7, t))
        put(VY, 6, t, partial(VY, 6, t) - (RATE * buoy(6, t)) * h8)
        put(VY, 7, t, partial(VY, 7, t) + (RATE * buoy(7, t)) * (27.0 * h8 - h9))
    for t in range(tiles):
        b2, b1 = RATE * lo_buoy(BUOY, 6, t), RATE * lo_buoy(BUOY, 7, t)
        b8, b9 = RATE * hi_buoy(BUOY, 0, t), RATE * hi_buoy(BUOY, 1, t)
        put(VX, -1, t, lo(VX, 7, t) - b1 * sxy(0, t))
        put(VY, -2, t, lo(VY, 6, t) - b2 * syy(0, t))
        put(VY, -1, t, lo(VY, 7, t) + b1 * (27.0 * syy(0, t) - syy(1, t)))
        put(VZ, -1, t, lo(VZ, 7, t) - b1 * syz(0, t))
        put(VX, 8, t, hi(VX, 0, t) + b8 * (sxy(6, t) - 27.0 * sxy(7, t)))
        put(VX, 9, t, hi(VX, 1, t) + b9 * sxy(7, t))
        put(VY, 8, t, hi(VY, 0, t) + b8 * syy(7, t))
        put(VZ, 8, t, hi(VZ, 0, t) + b8 * (syz(6, t) - 27.0 * syz(7, t)))
        put(VZ, 9, t, hi(VZ, 1, t) + b9 * syz(7, t))


def seafloor(grid, vz, y, floors, out, index):
    total = None
    for t in range(TILES):
        part = jnp.where(floors[0] == grid.depth[t], vz(y, t), 0.0)
        total = part if total is None else total + part
    out[index : index + 1, :] = jnp.sum(total, axis=0, keepdims=True)
    if len(floors) > 1:
        part = jnp.where(floors[1] == grid.depth[WINDOW], vz(y, WINDOW), 0.0)
        out[2 * SUB + index : 2 * SUB + index + 1, :] = jnp.sum(part, axis=0, keepdims=True)


def sea(grid, speed, level, now, fixed, line, lo, hi, sums, new, last):
    vz = speed(VZ)
    for y in range(ROWS):
        seafloor(grid, vz, y, [line(FLOOR, k, y) for k in range(2)], sums, y)
    ends = 1 if last else 2
    for y, side, at in ((-1, lo, ROWS), (ROWS, hi, ROWS + 1)):
        seafloor(grid, vz, y, [side.line(FLOOR, k) for k in range(ends)], sums, at)
    floors, beyond = [tile(sums, 0), grid.every_group(tile(sums, 2))], [tile(sums, 1), None]
    if not last:
        beyond[1] = grid.every_group(tile(sums, 3))
    sub = grid.sub
    levels, lows, highs = [], [], []
    for k in range(2):
        near = jnp.where(sub == 0, lo.line(FLUX_Y, k), jnp.where(sub == ROWS - 1, -hi.line(FLUX_Y, k), 0.0))
        levels.append(level(k) + fixed(WET, k) * (UPLIFT * floors[k] + (0.5 * OCEAN_RATE) * near))
        new(LEVEL, k, levels[k])
        if k < ends:
            for side, at, y, sign, out in ((lo, 0, 0, -1.0, lows), (hi, 1, ROWS - 1, 1.0, highs)):
                mine = (sign * 0.5 * OCEAN_RATE) * line(FLUX_Y, k, y)
                rest = UPLIFT * beyond[k][at : at + 1, :] + mine
                out.append(side.line(None, k) + side.line(WET, k) * rest)
    for k in range(ends):
        wet, deep = fixed(WET, k), fixed(DEPTH, k)
        edge = flat_edge(grid, lambda q: levels[q], k)
        slope_x = 0.5 * (grid.along(levels[k], 1, edge) - grid.along(levels[k], -1, edge))
        slope_y = 0.5 * (grid.across(levels[k], 1, highs[k]) - grid.across(levels[k], -1, lows[k]))
        for which, slope in ((FLUX_X, slope_x), (FLUX_Y, slope_y)):
            x = now(which, k)
            edge = flat_edge(grid, lambda q: now(which, q), k)
            laplace = grid.along(x, 1, edge) + grid.along(x, -1, edge) - 4.0 * x
            laplace = laplace + grid.across(x, 1, hi.line(which, k)) + grid.across(x, -1, lo.line(which, k))
            new(which, k, wet * (x - OCEAN_RATE * deep * slope + VISCOUS * laplace))
    return levels


def press(grid, levels, fixed, line, pressure):
    for k in range(2):
        store(pressure, k, LOADING * fixed(WET, k) * levels[k])

    def load(y, t):
        k = 1 if t == WINDOW else 0
        return jnp.where(line(FLOOR, k, y) == grid.depth[t], row(pressure, k * ROWS + y), 0.0)

    return load


def edge_index(c, y):
    return OPEN.index((c, y)) * SPAN


def block_index(c, y):
    return (c * ROWS + y) * SPAN


def start_kernel(
    flags, before, after, main, flat, own, own_flat, even_in, odd_in, early_odd, early_even,
    windows, flat_windows, partial, level, even_way, odd_way,
):
    grid = Grid(flags[2], before, after)
    odd = (flags[0] & 1) == 1
    for f in range(0, FIELDS, 2):
        for q in range(0, ROWS, 2):
            places = [h * ROWS + y for y in (q, q + 1) for h in (f, f + 1)]
            items = [tile(own, p) for p in places]
            for p, x in zip(places, unpack(grid, items, odd, even_in, odd_in, (f * ROWS // 2 + q) // 2)):
                store(windows, p, x)
    items = [tile(own_flat, k) for k in range(6)]
    base = FIELDS * ROWS // 4
    for k, x in enumerate(unpack(grid, items[:4], odd, even_in, odd_in, base)):
        store(flat_windows, k, x)
    for k, x in enumerate(unpack(grid, items[4:] * 2, odd, even_in, odd_in, base + 1)[:2]):
        store(flat_windows, 4 + k, x)

    field = fields_of(main, windows)
    speeds(
        grid, [inside(field(f)) for f in range(SXX, SYZ + 1)], field, field(BUOY), OPEN,
        lambda c, y, t, value: store(partial, edge_index(c, y) + t, value),
    )
    flats = (flat, flat_windows)
    partial_level(grid, lambda f, k: tile(flats[k], f), lambda k, value: store(level, k, value))

    def rows_of(f):
        return (lambda y, t: tile(partial, edge_index(f, y) + t)) if f < 3 else field(f)

    def line(which, k, y):
        return row(level, k * ROWS + y) if which is None else row(flats[k], which * ROWS + y)

    send(FIRST, (flags[1] & 1) == 1, rows_of, line, even_way, odd_way)


def start_rest_kernel(flags, before, after, main, windows, speed_out, stress_out):
    grid = Grid(flags[2], before, after)
    field = fields_of(main, windows)
    speeds(
        grid, [inside(field(f)) for f in range(SXX, SYZ + 1)], field, field(BUOY), CLOSED,
        lambda c, y, t, value: store(speed_out, block_index(c, y) + t, value),
    )
    stresses(
        grid, INNER, SPAN, block_reader(speed_out, VX), field,
        field(LAME), field(SHEAR),
        lambda f, y, t, value: store(stress_out, block_index(f - SXX, y) + t, value),
    )


def block_reader(ref, least):
    return lambda f: lambda y, t, *start: tile(ref, block_index(f - least, y) + t, *start)


def speed_reader(around, block):
    def speed(c):
        def read(y, t, *start):
            if (c, y) in CLOSED:
                return tile(block, block_index(c, y) + t, *start)
            return tile(around, (c * AROUND + y + 2) * SPAN + t, *start)

        return read

    return speed


def middle_kernel(
    flags, before, after, main, windows, flat, flat_windows, partial, level, speed_in, stress_in,
    early_even, early_odd, even_in, odd_in,
    speed_out, stress_out, ocean, partial_out, level_out, even_way, odd_way,
    sums, pressure,
):
    grid = Grid(flags[2], before, after)
    odd = (flags[1] & 1) == 1
    lo, hi = received(FIRST, odd, even_in, odd_in)
    field = fields_of(main, windows)
    finish(
        grid, SPAN, lambda c, y, t: tile(partial, edge_index(c, y) + t), field, field(BUOY), lo, hi, *early(odd, early_even, early_odd, (lo, hi)),
        speed_out,
    )
    speed = speed_reader(speed_out, speed_in)
    flats = (flat, flat_windows)
    fixed = lambda f, k: tile(flats[k], f)
    line = lambda f, k, y: row(flats[k], f * ROWS + y)

    def new(f, k, value):
        store(ocean, 3 * k + f, value)

    levels = sea(grid, speed, lambda k: tile(level, k), fixed, fixed, line, lo, hi, sums, new, False)
    load = press(grid, levels, fixed, line, pressure)

    def put(f, y, t, value):
        store(stress_out, block_index(f - SXX, y) + t, value - load(y, t) if f == SZZ else value)

    stresses(grid, OUTER, SPAN, speed, field, field(LAME), field(SHEAR), put)
    for f in range(SXX, SYZ + 1):
        for y in INNER:
            for t in range(SPAN):
                put(f, y, t, tile(stress_in, block_index(f - SXX, y) + t))
    stress = block_reader(stress_out, SXX)
    speeds(
        grid, [inside(stress(f)) for f in range(SXX, SYZ + 1)], speed, field(BUOY), OPEN,
        lambda c, y, t, value: store(partial_out, edge_index(c, y) + t, value),
    )
    moving = lambda f, k: tile(flats[k], f) if f >= DEPTH else tile(ocean, 3 * k + f)
    partial_level(grid, moving, lambda k, value: store(level_out, k, value))

    def rows_of(f):
        return (lambda y, t: tile(partial_out, edge_index(f, y) + t)) if f < 3 else stress(f)

    def line_out(which, k, y):
        if which is None:
            return row(level_out, k * ROWS + y)
        return line(which, k, y) if which >= DEPTH else row(ocean, (3 * k + which) * ROWS + y)

    send(LATER, odd, rows_of, line_out, even_way, odd_way)


def copy_rows(ref, index, hbm, f, y, sem):
    return pltpu.make_async_copy(ref.at[index * SUB : (index + TILES) * SUB, :], hbm.at[f, :, y, :], sem)


BY_ROWS = (SXX, SYY)
BY_FIELD = (SZZ, SXY, SXZ, SYZ)


def middle_rest_kernel(flags, before, after, main, windows, around, speed_in, stress_in, speed_out, stress_out, wave_hbm, sem):
    grid = Grid(flags[2], before, after)
    field = fields_of(main, windows)
    stress = block_reader(stress_in, SXX)
    speeds(
        grid, [inside(stress(f)) for f in range(SXX, SYZ + 1)], speed_reader(around, speed_in), field(BUOY), CLOSED,
        lambda c, y, t, value: store(speed_out, block_index(c, y) + t, value),
    )
    sent = [copy_rows(speed_out, block_index(c, y), wave_hbm, c, y, sem.at[i]) for i, (c, y) in enumerate(CLOSED)]
    for one in sent:
        one.start()
    stresses(
        grid, INNER, TILES, block_reader(speed_out, VX), stress,
        field(LAME), field(SHEAR),
        lambda f, y, t, value: store(stress_out, block_index(f - SXX, y) + t, value),
    )
    for f in BY_ROWS:
        for y in INNER:
            sent.append(copy_rows(stress_out, block_index(f - SXX, y), wave_hbm, f, y, sem.at[len(sent)]))
            sent[-1].start()
    for one in sent:
        one.wait()


def last_kernel(
    flags, before, after, main, windows, flat, flat_windows, stress_in, ocean_in, partial, level, speed_in, inner_in,
    early_even, early_odd, even_in, odd_in, wave_in,
    wave_hbm, ocean_out,
    sums, pressure, around, turned, wave, sem,
):
    grid = Grid(flags[2], before, after)
    odd = (flags[1] & 1) == 1
    lo, hi = received(LATER, odd, even_in, odd_in)
    lo_buoy, hi_buoy = early(odd, early_even, early_odd, (lo, hi))
    field = fields_of(main, windows)
    stress = block_reader(stress_in, SXX)
    finish(
        grid, TILES, lambda c, y, t: tile(partial, edge_index(c, y) + t), stress, field(BUOY),
        lo, hi, lo_buoy, hi_buoy, around,
    )
    speed = speed_reader(around, speed_in)
    sent = []

    def copy(source, target):
        sent.append(pltpu.make_async_copy(source, target, sem.at[len(sent)]))
        sent[-1].start()

    for c, y in OPEN:
        sent.append(copy_rows(around, (c * AROUND + y + 2) * SPAN, wave_hbm, c, y, sem.at[len(sent)]))
        sent[-1].start()
    flats = (flat, flat_windows)
    fixed = lambda f, k: tile(flats[k], f)

    def line(f, k, y):
        return row(flats[k], f * ROWS + y) if f >= DEPTH else row(ocean_in, (3 * k + f) * ROWS + y)

    def new(f, k, value):
        if k == 0:
            store(ocean_out, f, value)

    levels = sea(
        grid, speed, lambda k: tile(level, k), lambda f, k: tile(ocean_in, 3 * k + f), fixed, line, lo, hi, sums, new, True
    )
    load = press(grid, levels, fixed, line, pressure)

    size = TILES * SUB * ROWS

    def put(f, y, t, value):
        if f in BY_ROWS:
            turned[f - SXX, y, t * SUB : (t + 1) * SUB, :] = value
            return
        if f == SZZ:
            value = value - load(y, t)
        wave[pl.ds(BY_FIELD.index(f) * size + t * SUB * ROWS + y, SUB, stride=ROWS), :] = value

    def done(y):
        copy(turned.at[:, y], wave_hbm.at[SXX : SYY + 1, :, y, :])

    stresses(grid, OUTER, TILES, speed, stress, field(LAME), field(SHEAR), put, done)
    for f in BY_FIELD:
        for y in INNER:
            for t in range(TILES):
                put(f, y, t, tile(inner_in, block_index(f - SXX, y) + t))
    copy(wave, wave_hbm.at[SZZ : SYZ + 1].reshape(len(BY_FIELD) * size, LANES))
    for one in sent:
        one.wait()


IN_VMEM = pl.BlockSpec(memory_space=pltpu.VMEM)
IN_SMEM = pl.BlockSpec(memory_space=pltpu.SMEM)
IN_HBM = pl.BlockSpec(memory_space=pltpu.HBM)


def call(kernel, tiles, scratch, *arguments, flags=None, place=IN_VMEM, out_places=None, work=1, aliases={}):
    specs = place if isinstance(place, list) else [place] * len(arguments)
    if flags is not None:
        arguments, specs = (flags, *arguments), [IN_SMEM] + specs
    moved = sum(x.size for x in arguments) + sum(n for n in tiles if isinstance(n, int)) * SUB * LANES
    return pl.pallas_call(
        kernel,
        out_shape=[n if hasattr(n, "dtype") else jax.ShapeDtypeStruct((n * SUB, LANES), jnp.float32) for n in tiles],
        in_specs=specs,
        out_specs=out_places or [IN_VMEM] * len(tiles),
        scratch_shapes=scratch,
        input_output_aliases=aliases,
        cost_estimate=pl.CostEstimate(flops=work * 1000000, bytes_accessed=4 * moved, transcendentals=0),
        compiler_params=pltpu.CompilerParams(vmem_limit_bytes=24 * 1024 * 1024),
    )(*arguments)


def planes(n):
    return pltpu.VMEM((n * SUB, LANES), jnp.float32)


def swap(x, axis, start):
    pairs = [(i, i + 1) for i in range(start, lax.axis_size(axis) - 1, 2)]
    return lax.ppermute(x, axis, pairs + [(j, i) for i, j in pairs])


def local(*arguments):
    ocean_state = arguments[4]
    inputs = [pltpu.with_memory_space_constraint(x, pltpu.HBM) for x in arguments]
    flags = jnp.stack([lax.axis_index("gx"), lax.axis_index("gy"), 0])
    matrix = jax.ShapeDtypeStruct((2 * LANES, SPAN * LANES), jnp.bfloat16)
    cells4 = jax.ShapeDtypeStruct((FIELDS, ROWS, TILES * SUB, LANES), jnp.float32)

    edge = FIELDS * ROWS // 4 + 2
    before, after, main, flat, own, own_flat, even_way, odd_way, early_even, early_odd = call(
        edges_kernel, [matrix, matrix, cells4, 6, FIELDS * ROWS, 6, edge, edge, 2 * TILES, 2 * TILES],
        [planes(FIELDS * ROWS), planes(6)] + [pltpu.VMEM(x.shape, x.dtype) for x in inputs[4:]]
        + [pltpu.SemaphoreType.DMA((4 + 5 * ROWS,))],
        *inputs, flags=flags, place=IN_HBM,
    )
    x_in = swap(even_way, "gx", 0), swap(odd_way, "gx", 1)
    early_in = swap(early_even, "gy", 0), swap(early_odd, "gy", 1)
    main = main.reshape(-1, LANES)
    first, later = [message_tiles(kind) for kind in (FIRST, LATER)]
    edges, block = len(OPEN) * SPAN, ROWS * SPAN
    windows, flat_windows, partial, level, even_way, odd_way = call(
        start_kernel, [FIELDS * ROWS, 6, edges, 2, first, first], [],
        before, after, main, flat, own, own_flat, *x_in, *early_in[::-1], flags=flags,
    )
    y_in = swap(even_way, "gy", 0), swap(odd_way, "gy", 1)
    speed, inner = call(start_rest_kernel, [3 * block, 6 * block], [], before, after, main, windows, flags=flags, work=4)
    around, stress, ocean, partial, level, even_way, odd_way = call(
        middle_kernel, [3 * AROUND * SPAN, 6 * block, 6, edges, 2, later, later], [planes(4), planes(2)],
        before, after, main, windows, flat, flat_windows, partial, level, speed, inner, *early_in, *y_in, flags=flags,
    )
    y_in = swap(even_way, "gy", 0), swap(odd_way, "gy", 1)
    wave = jax.ShapeDtypeStruct(arguments[0].shape, jnp.float32)
    speed, inner, wave_part = call(
        middle_rest_kernel, [3 * block, 6 * block, wave],
        [pltpu.SemaphoreType.DMA((len(CLOSED) + len(BY_ROWS) * len(INNER),))],
        before, after, main, windows, around, speed, stress, flags=flags, out_places=[IN_VMEM, IN_VMEM, IN_HBM], work=4,
    )
    operands = (
        before, after, main, windows, flat, flat_windows, stress, ocean, partial, level, speed, inner, *early_in, *y_in, wave_part
    )
    wave_out, ocean_out = call(
        last_kernel, [wave, 3],
        [
            planes(4), planes(2), planes(3 * AROUND * SPAN),
            pltpu.VMEM((len(BY_ROWS), *cells4.shape[1:]), jnp.float32), planes(len(BY_FIELD) * ROWS * TILES),
            pltpu.SemaphoreType.DMA((len(OPEN) + len(OUTER) + 1,)),
        ],
        *operands, flags=flags, place=[IN_VMEM] * (len(operands) - 1) + [IN_HBM], out_places=[IN_HBM, IN_VMEM],
        aliases={len(operands): 0},
    )
    return wave_out, ocean_out.reshape(ocean_state.shape)


def solution(mesh):
    in_specs = (
        P(None, None, "gy", "gx"),
        P(None, "gy", "gx"),
        P(None, "gy", "gx"),
        P(None, "gy", "gx"),
        P(None, "gy", "gx"),
        P("gy", "gx"),
        P("gy", "gx"),
        P("gy", "gx"),
    )
    out_specs = (P(None, None, "gy", "gx"), P(None, "gy", "gx"))
    return jax.shard_map(local, mesh=mesh, in_specs=in_specs, out_specs=out_specs, check_vma=False)
```

```python
import jax
import jax.numpy as jnp
from jax import lax
from jax.experimental import pallas as pl
from jax.experimental.pallas import tpu as pltpu
from jax.sharding import PartitionSpec as P

RATE = 0.3 / 24.0
OCEAN_RATE = 0.3
UPLIFT = 0.5
LOADING = 0.5
VISCOUS = 0.1

ROWS = 8
SUB = 8
LANES = 128
EDGE = 8
GROUP = 2 * EDGE
TILES = 4
HALF = TILES * GROUP
SPAN = TILES + 1
WINDOW = TILES

LEVEL, FLUX_X, FLUX_Y, DEPTH, FLOOR, WET = range(6)
VX, VY, VZ, SXX, SYY, SZZ, SXY, SXZ, SYZ, LAME, SHEAR, BUOY = range(12)
FIELDS = 12

OPEN = ((VX, 0), (VX, 1), (VX, 7), (VY, 0), (VY, 6), (VY, 7), (VZ, 0), (VZ, 1), (VZ, 7))
CLOSED = tuple((c, y) for y in range(ROWS) for c in (VX, VY, VZ) if (c, y) not in OPEN)
INNER = (3, 4)
OUTER = tuple(y for y in range(ROWS) if y not in INNER)

SPEED_HIGH = ((VX, 7), (VY, 6), (VY, 7), (VZ, 7))
SPEED_LOW = ((VX, 0), (VX, 1), (VY, 0), (VZ, 0), (VZ, 1))
STRESS_HIGH = ((SXY, 6), (SXY, 7), (SYY, 7), (SYZ, 6), (SYZ, 7))
STRESS_LOW = ((SXY, 0), (SYY, 0), (SYY, 1), (SYZ, 0))
BUOY_HIGH = ((BUOY, 6), (BUOY, 7))
BUOY_LOW = ((BUOY, 0), (BUOY, 1))
LINES = (None, WET, FLOOR, FLUX_X, FLUX_Y)


def rest(x, size):
    return x & (size - 1)


def count(x, size):
    return x >> (size.bit_length() - 1)


def rolled(x, shift, axis):
    shift %= x.shape[axis]
    return x if shift == 0 else pltpu.roll(x, shift, axis)


def tile(ref, index, start=None):
    if start is None:
        return ref[index * SUB : (index + 1) * SUB, :]
    return ref[pl.ds(start + index * SUB, SUB), :]


def row(ref, index):
    return ref[index : index + 1, :]


def store(ref, index, value):
    ref[index * SUB : (index + 1) * SUB, :] = value


def split(x, parts):
    out = []
    for part in range(parts):
        out.append(x.astype(jnp.bfloat16))
        if part + 1 < parts:
            x = x - out[-1].astype(jnp.float32)
    return jnp.concatenate(out, axis=1)


def minus(a, b):
    if b is None:
        return a
    return -b if a is None else a - b


def near_far(a, b, c, d):
    near, far = 27.0 * minus(a, b), minus(c, d)
    return near if c is None and d is None else near - far


class Grid:
    def __init__(self, origin=None, before=None, after=None):
        self.origin, self.before, self.after = origin, before, after
        self.sub = lax.broadcasted_iota(jnp.int32, (SUB, LANES), 0)
        self.lane = lax.broadcasted_iota(jnp.int32, (SUB, LANES), 1)
        self.first = rest(self.lane, GROUP) < EDGE
        self.left = self.lane < HALF
        self.group = count(self.lane, GROUP)
        self.zero = jnp.zeros((SUB, LANES), jnp.float32)
        depth = [self.sub + SUB * t for t in range(TILES)] + [self.sub + SUB * rest(self.group, TILES)]
        self.depth = [d.astype(jnp.float32) for d in depth]

    def beside(self, window):
        return jnp.where(self.first, window, rolled(window, HALF, 1))

    def edge(self, beside, t):
        return None if t == WINDOW else rolled(beside, LANES - EDGE - GROUP * t, 1)

    def along(self, x, offset, edge):
        if edge is not None:
            lane = self.lane
            keep = {-1: lane == LANES - 1, -2: lane >= LANES - 2, 1: lane == 0, 2: lane <= 1}[offset]
            x = jnp.where(keep, edge, x)
        return rolled(x, -offset, 1)

    def down(self, field, y, t, offset):
        if t < WINDOW:
            x = field(y, t, self.origin + offset)
            if t == 0 and offset < 0:
                return jnp.where(self.sub >= -offset, x, 0.0)
            if t == TILES - 1 and offset > 0:
                return jnp.where(self.sub < SUB - offset, x, 0.0)
            return x
        x, at = field(y, t), rest(self.lane, HALF)
        if offset < 0:
            beyond, far = jnp.where(at >= GROUP, rolled(x, GROUP, 1), 0.0), self.sub >= SUB + offset
        else:
            beyond, far = jnp.where(at < HALF - GROUP, rolled(x, -GROUP, 1), 0.0), self.sub < offset
        return rolled(jnp.where(far, beyond, x), -offset, 0)

    def fz(self, field, y, t):
        down = lambda offset: self.down(field, y, t, offset)
        return near_far(down(1), field(y, t), down(2), down(-1))

    def bz(self, field, y, t):
        down = lambda offset: self.down(field, y, t, offset)
        return near_far(field(y, t), down(-1), down(1), down(-2))

    def along_rows(self, matrix, rows):
        main = split(jnp.concatenate([f(y, t) for f, y in rows for t in range(TILES)], axis=0), 2)
        sides = [f(y, WINDOW) for f, y in rows]
        side = split(jnp.concatenate(sides + sides[: len(sides) % 2], axis=0), 2)
        main = jnp.dot(main, matrix[:, :LANES], preferred_element_type=jnp.float32)
        side = jnp.dot(side, matrix[...], preferred_element_type=jnp.float32)
        out = []
        for i in range(len(rows)):
            part = side[i * SUB : (i + 1) * SUB, :]
            parts = [part[:, t * LANES : (t + 1) * LANES] for t in range(SPAN)]
            tiles = [
                main[(i * TILES + t) * SUB : (i * TILES + t + 1) * SUB, :] + parts[1 + t] for t in range(TILES)
            ]
            out.append(tiles + parts[:1])
        return out

    def fy(self, field, y, t):
        return near_far(field(y + 1, t), field(y, t), field(y + 2, t), field(y - 1, t))

    def by(self, field, y, t):
        return near_far(field(y, t), field(y - 1, t), field(y + 1, t), field(y - 2, t))

    def windows(self, own, from_left, from_right):
        return jnp.where(
            self.left, jnp.where(self.first, from_left, own), jnp.where(self.first, own, from_right)
        )

    def every_group(self, x):
        for shift in (GROUP, 2 * GROUP):
            x = x + jnp.where(rest(self.lane, HALF) >= shift, rolled(x, shift, 1), rolled(x, shift - HALF, 1))
        return x

    def across(self, x, offset, beside):
        end = 0 if offset < 0 else ROWS - 1
        return jnp.where(self.sub == end, beside, rolled(x, -offset, 0))


def inside(field):
    return lambda y, t, *start: field(y, t, *start) if 0 <= y < ROWS else None


def fields_of(main, windows):
    def field(f):
        def read(y, t, *start):
            return tile(windows, f * ROWS + y) if t == WINDOW else tile(main, (f * ROWS + y) * TILES + t, *start)

        return read

    return field


def pack(grid, own, other, flat, other_flat, to_right, out):
    for index, (near, far) in enumerate(zip(edge_groups(own, flat), edge_groups(other, other_flat))):
        a, b, c, d = near[0], far[1], near[2], far[3]
        if not to_right:
            a, b, c, d = b, a, d, c
        store(out, index, jnp.where(grid.left, jnp.where(grid.first, a, b), jnp.where(grid.first, c, d)))


def edge_groups(own, own_flat):
    groups = [
        [tile(own, h * ROWS + y) for y in (q, q + 1) for h in (f, f + 1)]
        for f in range(0, FIELDS, 2)
        for q in range(0, ROWS, 2)
    ]
    flat = [tile(own_flat, k) for k in range(6)]
    return groups + [flat[:4], flat[4:] * 2]


def unpack(grid, items, odd, even_in, odd_in, index):
    x, y = tile(even_in, index), tile(odd_in, index)
    before, after = jnp.where(odd, x, y), jnp.where(odd, y, x)
    befores = [before, rolled(before, -EDGE, 1), rolled(before, HALF, 1), rolled(before, HALF - EDGE, 1)]
    afters = [rolled(after, HALF, 1), rolled(after, HALF + EDGE, 1), after, rolled(after, EDGE, 1)]
    return [grid.windows(*three) for three in zip(items, befores, afters)]


def difference_matrix(out, weights, offsets):
    shape = (LANES, LANES)
    k, n = [lax.broadcasted_iota(jnp.int32, shape, axis) for axis in range(2)]

    def weight(apart):
        total = jnp.zeros(shape, jnp.float32)
        for w, offset in zip(weights, offsets):
            total = jnp.where(apart == offset, w, total)
        return total

    inner, left = rest(k, GROUP), k < HALF
    column = jnp.where(left, inner - EDGE, LANES - EDGE + inner)
    outside = (left & (inner < EDGE)) | (jnp.logical_not(left) & (inner >= EDGE))
    beside = jnp.where(outside, weight(n - column), 0.0)
    parts = [weight(n - k)]
    parts += [jnp.where(count(rest(k, HALF), GROUP) == t, beside, 0.0) for t in range(TILES)]
    for p, x in enumerate(parts):
        for half in range(2):
            out[half * LANES : (half + 1) * LANES, p * LANES : (p + 1) * LANES] = x.astype(jnp.bfloat16)


def picker(t):
    k, n = [lax.broadcasted_iota(jnp.int32, (LANES, LANES), axis) for axis in range(2)]
    inner, mine = rest(n, GROUP), count(rest(n, HALF), GROUP) == t
    both = []
    for swapped in (False, True):
        last = inner >= EDGE if swapped else inner < EDGE
        column = jnp.where(last, LANES - EDGE, 0) + rest(inner, EDGE)
        both.append(jnp.where(mine & (k == column), 1.0, 0.0).astype(jnp.bfloat16))
    return jnp.concatenate([jnp.concatenate(both, axis=1)] * 2, axis=0)


def edges_kernel(flags, *refs):
    hbm, refs = refs[:8], refs[8:]
    (before, after, main, flat, own, own_flat, even_way, odd_way, early_even, early_odd), refs = refs[:10], refs[10:]
    other, other_flat, ocean, deep, floor, wet, sem = refs
    sent = []

    def copy(source, target):
        sent.append(pltpu.make_async_copy(source, target, sem.at[len(sent)]))
        sent[-1].start()
        return sent[-1]

    ready = [[], []]
    cut = FIELDS // 2
    for y in range(ROWS):
        ready[0].append(copy(hbm[0].at[:cut, :, y, :], main.at[:cut, y]))
    for y in range(ROWS):
        ready[1].append(copy(hbm[0].at[cut:, :, y, :], main.at[cut:LAME, y]))
        ready[1] += [copy(hbm[1 + k].at[:, y, :], main.at[LAME + k, y]) for k in range(3)]
    flats = [copy(hbm[4 + k], x) for k, x in enumerate((ocean, deep, floor, wet))]
    difference_matrix(before, (27.0, -27.0, -1.0, 1.0), (0, 1, -1, 2))
    difference_matrix(after, (27.0, -27.0, -1.0, 1.0), (-1, 0, -2, 1))
    pickers = [picker(t) for t in range(TILES)]
    for one in flats:
        one.wait()
    planes = [ocean[k] for k in range(3)] + [deep[...]]
    planes += [floor[...].astype(jnp.float32), wet[...].astype(jnp.float32)]
    for k, x in enumerate(planes):
        store(flat, k, x)
    size = SUB * ROWS
    for half in range(2):
        for one in ready[half]:
            one.wait()
        mine = range(half * cut, (half + 1) * cut)
        total = None
        for t in range(TILES):
            x = [main[f, y, t * SUB : (t + 1) * SUB, :] for f in mine for y in range(ROWS)]
            x = x if half else x + planes
            part = jnp.dot(split(jnp.concatenate(x, axis=0), 2), pickers[t], preferred_element_type=jnp.float32)
            total = part if total is None else total + part
        for ref, ref_flat, x in ((own, own_flat, total[:, :LANES]), (other, other_flat, total[:, LANES:])):
            ref[mine[0] * size : (mine[-1] + 1) * size, :] = x[: cut * size, :]
            if not half:
                ref_flat[...] = x[cut * size :, :]
    grid = Grid()
    edges = own, other, own_flat, other_flat

    @pl.when((flags[0] & 1) == 1)
    def _():
        pack(grid, *edges, True, odd_way)
        pack(grid, *edges, False, even_way)

    @pl.when((flags[0] & 1) == 0)
    def _():
        pack(grid, *edges, False, odd_way)
        pack(grid, *edges, True, even_way)

    odd = (flags[1] & 1) == 1
    for k, ((_, below), (_, above)) in enumerate(zip(BUOY_LOW, BUOY_HIGH)):
        for t in range(TILES):
            a, b = [main[BUOY, y, t * SUB : (t + 1) * SUB, :] for y in (below, above)]
            store(early_even, k * TILES + t, jnp.where(odd, a, b))
            store(early_odd, k * TILES + t, jnp.where(odd, b, a))


def speeds(grid, stress, speed, buoy, todo, put):
    sxx, syy, szz, sxy, sxz, syz = stress
    forth = [(VX, y) for c, y in todo if c == VX]
    back = [(c, y) for c, y in todo if c != VX]
    change = dict(zip(forth, grid.along_rows(grid.after, [(sxx, y) for _, y in forth])))
    change.update(zip(back, grid.along_rows(grid.before, [(sxy if c == VY else sxz, y) for c, y in back])))
    for y in range(ROWS):
        parts = [c for c in (VX, VY, VZ) if (c, y) in todo]
        if not parts:
            continue
        for t in range(SPAN):
            rate = RATE * buoy(y, t)
            for c in parts:
                a = change[c, y][t]
                if c == VX:
                    a = a + grid.by(sxy, y, t) + grid.bz(sxz, y, t)
                elif c == VY:
                    a = a + grid.fy(syy, y, t) + grid.bz(syz, y, t)
                else:
                    a = a + grid.by(syz, y, t) + grid.fz(szz, y, t)
                put(c, y, t, speed(c)(y, t) + rate * a)


def stresses(grid, rows, tiles, speed, stress, lame, shear, put, done=lambda y: None):
    vx, vy, vz = [speed(c) for c in (VX, VY, VZ)]
    back = grid.along_rows(grid.before, [(vx, y) for y in rows])
    forth = grid.along_rows(grid.after, [(v, y) for v in (vy, vz) for y in rows])
    for i, y in enumerate(rows):
        for t in range(tiles):
            strain_x = back[i][t]
            strain_y = grid.by(vy, y, t)
            strain_z = grid.bz(vz, y, t)
            mu = RATE * shear(y, t)
            spread = (RATE * lame(y, t)) * (strain_x + strain_y + strain_z)
            two = mu + mu
            put(SXX, y, t, stress(SXX)(y, t) + (spread + two * strain_x))
            put(SYY, y, t, stress(SYY)(y, t) + (spread + two * strain_y))
            put(SZZ, y, t, stress(SZZ)(y, t) + (spread + two * strain_z))
            put(SXY, y, t, stress(SXY)(y, t) + mu * (grid.fy(vx, y, t) + forth[i][t]))
            put(SXZ, y, t, stress(SXZ)(y, t) + mu * (grid.fz(vx, y, t) + forth[len(rows) + i][t]))
            put(SYZ, y, t, stress(SYZ)(y, t) + mu * (grid.fz(vy, y, t) + grid.fy(vz, y, t)))
        done(y)


def flat_edge(grid, at, k):
    return grid.edge(grid.beside(at(1)), 0) if k == 0 else None


def partial_level(grid, flat, put):
    for k in range(2):
        x, y = flat(FLUX_X, k), flat(FLUX_Y, k)
        edge = flat_edge(grid, lambda q: flat(FLUX_X, q), k)
        spread = 0.5 * (grid.along(x, 1, edge) - grid.along(x, -1, edge))
        spread = spread + 0.5 * (grid.across(y, 1, 0.0) - grid.across(y, -1, 0.0))
        put(k, flat(LEVEL, k) - OCEAN_RATE * (flat(WET, k) * spread))


def cells(rows, tiles):
    return [(f, y, t) for f, y in rows for t in tiles]


class Message:
    def __init__(self, tiles):
        self.at = {which: i for i, which in enumerate(tiles)}
        self.base = len(tiles) * SUB
        self.size = self.base + 2 * SUB


ALL, INSIDE = range(SPAN), range(TILES)
SIDES = (WINDOW,)
EARLY = [{which: i for i, which in enumerate(cells(rows, INSIDE))} for rows in (BUOY_HIGH, BUOY_LOW)]
FIRST = [
    Message(cells(rows, ALL) + cells(buoy, SIDES))
    for rows, buoy in ((SPEED_HIGH + STRESS_HIGH, BUOY_HIGH), (SPEED_LOW + STRESS_LOW, BUOY_LOW))
]
LATER = [
    Message(cells(speed, INSIDE) + cells(rest, ALL))
    for speed, rest in ((SPEED_HIGH, STRESS_HIGH), (SPEED_LOW, STRESS_LOW))
]


def message_tiles(kind):
    return max(m.size for m in kind) // SUB


def send(kind, odd, field, line, even_way, odd_way):
    high, low = kind

    def fill(message, edge, out):
        for (f, y, t), at in message.at.items():
            store(out, at, field(f)(y, t))
        at = message.base
        for which in LINES:
            for k in range(2):
                out[at : at + 1, :] = line(which, k, edge)
                at += 1
        out[at : at + 6, :] = jnp.zeros((6, LANES), jnp.float32)
        tail = out.shape[0]
        if message.size < tail:
            out[message.size : tail, :] = jnp.zeros((tail - message.size, LANES), jnp.float32)

    @pl.when(odd)
    def _():
        fill(high, ROWS - 1, odd_way)
        fill(low, 0, even_way)

    @pl.when(jnp.logical_not(odd))
    def _():
        fill(high, ROWS - 1, even_way)
        fill(low, 0, odd_way)


class Received:
    def __init__(self, message, odd, if_odd, if_even):
        self.message, self.odd, self.if_odd, self.if_even = message, odd, if_odd, if_even

    def __call__(self, f, y, t):
        at = self.message.at[f, y, t]
        return jnp.where(self.odd, tile(self.if_odd, at), tile(self.if_even, at))

    def line(self, which, k):
        at = self.message.base + 2 * LINES.index(which) + k
        return jnp.where(self.odd, row(self.if_odd, at), row(self.if_even, at))


def received(kind, odd, even_in, odd_in):
    return Received(kind[0], odd, even_in, odd_in), Received(kind[1], odd, odd_in, even_in)


def early(odd, even_in, odd_in, later):
    def reader(at, if_odd, if_even, rest):
        def read(f, y, t):
            if (f, y, t) not in at:
                return rest(f, y, t)
            return jnp.where(odd, tile(if_odd, at[f, y, t]), tile(if_even, at[f, y, t]))

        return read

    return reader(EARLY[0], even_in, odd_in, later[0]), reader(EARLY[1], odd_in, even_in, later[1])


AROUND = ROWS + 4


def finish(grid, tiles, partial, stress, buoy, lo, hi, lo_buoy, hi_buoy, speed):
    sxy, syy, syz = [stress(f) for f in (SXY, SYY, SYZ)]

    def put(c, y, t, value):
        store(speed, (c * AROUND + y + 2) * SPAN + t, value)

    for t in range(SPAN):
        for c, f in ((VX, SXY), (VZ, SYZ)):
            two, one = lo(f, 6, t), lo(f, 7, t)
            rate = [RATE * buoy(y, t) for y in (0, 1, 7)]
            put(c, 0, t, partial(c, 0, t) + rate[0] * (two - 27.0 * one))
            put(c, 1, t, partial(c, 1, t) + rate[1] * one)
            put(c, 7, t, partial(c, 7, t) - rate[2] * hi(f, 0, t))
        h8, h9 = hi(SYY, 0, t), hi(SYY, 1, t)
        put(VY, 0, t, partial(VY, 0, t) + (RATE * buoy(0, t)) * lo(SYY, 7, t))
        put(VY, 6, t, partial(VY, 6, t) - (RATE * buoy(6, t)) * h8)
        put(VY, 7, t, partial(VY, 7, t) + (RATE * buoy(7, t)) * (27.0 * h8 - h9))
    for t in range(tiles):
        b2, b1 = RATE * lo_buoy(BUOY, 6, t), RATE * lo_buoy(BUOY, 7, t)
        b8, b9 = RATE * hi_buoy(BUOY, 0, t), RATE * hi_buoy(BUOY, 1, t)
        put(VX, -1, t, lo(VX, 7, t) - b1 * sxy(0, t))
        put(VY, -2, t, lo(VY, 6, t) - b2 * syy(0, t))
        put(VY, -1, t, lo(VY, 7, t) + b1 * (27.0 * syy(0, t) - syy(1, t)))
        put(VZ, -1, t, lo(VZ, 7, t) - b1 * syz(0, t))
        put(VX, 8, t, hi(VX, 0, t) + b8 * (sxy(6, t) - 27.0 * sxy(7, t)))
        put(VX, 9, t, hi(VX, 1, t) + b9 * sxy(7, t))
        put(VY, 8, t, hi(VY, 0, t) + b8 * syy(7, t))
        put(VZ, 8, t, hi(VZ, 0, t) + b8 * (syz(6, t) - 27.0 * syz(7, t)))
        put(VZ, 9, t, hi(VZ, 1, t) + b9 * syz(7, t))


def seafloor(grid, vz, y, floors, out, index):
    total = None
    for t in range(TILES):
        part = jnp.where(floors[0] == grid.depth[t], vz(y, t), 0.0)
        total = part if total is None else total + part
    out[index : index + 1, :] = jnp.sum(total, axis=0, keepdims=True)
    if len(floors) > 1:
        part = jnp.where(floors[1] == grid.depth[WINDOW], vz(y, WINDOW), 0.0)
        out[2 * SUB + index : 2 * SUB + index + 1, :] = jnp.sum(part, axis=0, keepdims=True)


def sea(grid, speed, level, now, fixed, line, lo, hi, sums, new, last):
    vz = speed(VZ)
    for y in range(ROWS):
        seafloor(grid, vz, y, [line(FLOOR, k, y) for k in range(2)], sums, y)
    ends = 1 if last else 2
    for y, side, at in ((-1, lo, ROWS), (ROWS, hi, ROWS + 1)):
        seafloor(grid, vz, y, [side.line(FLOOR, k) for k in range(ends)], sums, at)
    floors, beyond = [tile(sums, 0), grid.every_group(tile(sums, 2))], [tile(sums, 1), None]
    if not last:
        beyond[1] = grid.every_group(tile(sums, 3))
    sub = grid.sub
    levels, lows, highs = [], [], []
    for k in range(2):
        near = jnp.where(sub == 0, lo.line(FLUX_Y, k), jnp.where(sub == ROWS - 1, -hi.line(FLUX_Y, k), 0.0))
        levels.append(level(k) + fixed(WET, k) * (UPLIFT * floors[k] + (0.5 * OCEAN_RATE) * near))
        new(LEVEL, k, levels[k])
        if k < ends:
            for side, at, y, sign, out in ((lo, 0, 0, -1.0, lows), (hi, 1, ROWS - 1, 1.0, highs)):
                mine = (sign * 0.5 * OCEAN_RATE) * line(FLUX_Y, k, y)
                rest = UPLIFT * beyond[k][at : at + 1, :] + mine
                out.append(side.line(None, k) + side.line(WET, k) * rest)
    for k in range(ends):
        wet, deep = fixed(WET, k), fixed(DEPTH, k)
        edge = flat_edge(grid, lambda q: levels[q], k)
        slope_x = 0.5 * (grid.along(levels[k], 1, edge) - grid.along(levels[k], -1, edge))
        slope_y = 0.5 * (grid.across(levels[k], 1, highs[k]) - grid.across(levels[k], -1, lows[k]))
        for which, slope in ((FLUX_X, slope_x), (FLUX_Y, slope_y)):
            x = now(which, k)
            edge = flat_edge(grid, lambda q: now(which, q), k)
            laplace = grid.along(x, 1, edge) + grid.along(x, -1, edge) - 4.0 * x
            laplace = laplace + grid.across(x, 1, hi.line(which, k)) + grid.across(x, -1, lo.line(which, k))
            new(which, k, wet * (x - OCEAN_RATE * deep * slope + VISCOUS * laplace))
    return levels


def press(grid, levels, fixed, line, pressure):
    for k in range(2):
        store(pressure, k, LOADING * fixed(WET, k) * levels[k])

    def load(y, t):
        k = 1 if t == WINDOW else 0
        return jnp.where(line(FLOOR, k, y) == grid.depth[t], row(pressure, k * ROWS + y), 0.0)

    return load


def edge_index(c, y):
    return OPEN.index((c, y)) * SPAN


def block_index(c, y):
    return (c * ROWS + y) * SPAN


def start_kernel(
    flags, before, after, main, flat, own, own_flat, even_in, odd_in, early_odd, early_even,
    windows, flat_windows, partial, level, even_way, odd_way,
):
    grid = Grid(flags[2], before, after)
    odd = (flags[0] & 1) == 1
    for f in range(0, FIELDS, 2):
        for q in range(0, ROWS, 2):
            places = [h * ROWS + y for y in (q, q + 1) for h in (f, f + 1)]
            items = [tile(own, p) for p in places]
            for p, x in zip(places, unpack(grid, items, odd, even_in, odd_in, (f * ROWS // 2 + q) // 2)):
                store(windows, p, x)
    items = [tile(own_flat, k) for k in range(6)]
    base = FIELDS * ROWS // 4
    for k, x in enumerate(unpack(grid, items[:4], odd, even_in, odd_in, base)):
        store(flat_windows, k, x)
    for k, x in enumerate(unpack(grid, items[4:] * 2, odd, even_in, odd_in, base + 1)[:2]):
        store(flat_windows, 4 + k, x)

    field = fields_of(main, windows)
    speeds(
        grid, [inside(field(f)) for f in range(SXX, SYZ + 1)], field, field(BUOY), OPEN,
        lambda c, y, t, value: store(partial, edge_index(c, y) + t, value),
    )
    flats = (flat, flat_windows)
    partial_level(grid, lambda f, k: tile(flats[k], f), lambda k, value: store(level, k, value))

    def rows_of(f):
        return (lambda y, t: tile(partial, edge_index(f, y) + t)) if f < 3 else field(f)

    def line(which, k, y):
        return row(level, k * ROWS + y) if which is None else row(flats[k], which * ROWS + y)

    send(FIRST, (flags[1] & 1) == 1, rows_of, line, even_way, odd_way)


def start_rest_kernel(flags, before, after, main, windows, speed_out, stress_out):
    grid = Grid(flags[2], before, after)
    field = fields_of(main, windows)
    speeds(
        grid, [inside(field(f)) for f in range(SXX, SYZ + 1)], field, field(BUOY), CLOSED,
        lambda c, y, t, value: store(speed_out, block_index(c, y) + t, value),
    )
    stresses(
        grid, INNER, SPAN, block_reader(speed_out, VX), field,
        field(LAME), field(SHEAR),
        lambda f, y, t, value: store(stress_out, block_index(f - SXX, y) + t, value),
    )


def block_reader(ref, least):
    return lambda f: lambda y, t, *start: tile(ref, block_index(f - least, y) + t, *start)


def speed_reader(around, block):
    def speed(c):
        def read(y, t, *start):
            if (c, y) in CLOSED:
                return tile(block, block_index(c, y) + t, *start)
            return tile(around, (c * AROUND + y + 2) * SPAN + t, *start)

        return read

    return speed


def middle_kernel(
    flags, before, after, main, windows, flat, flat_windows, partial, level, speed_in, stress_in,
    early_even, early_odd, odd_in, even_in,
    speed_out, stress_out, ocean, partial_out, level_out, even_way, odd_way,
    sums, pressure,
):
    grid = Grid(flags[2], before, after)
    odd = (flags[1] & 1) == 1
    lo, hi = received(FIRST, odd, even_in, odd_in)
    field = fields_of(main, windows)
    finish(
        grid, SPAN, lambda c, y, t: tile(partial, edge_index(c, y) + t), field, field(BUOY), lo, hi, *early(odd, early_even, early_odd, (lo, hi)),
        speed_out,
    )
    speed = speed_reader(speed_out, speed_in)
    flats = (flat, flat_windows)
    fixed = lambda f, k: tile(flats[k], f)
    line = lambda f, k, y: row(flats[k], f * ROWS + y)

    def new(f, k, value):
        store(ocean, 3 * k + f, value)

    levels = sea(grid, speed, lambda k: tile(level, k), fixed, fixed, line, lo, hi, sums, new, False)
    load = press(grid, levels, fixed, line, pressure)

    def put(f, y, t, value):
        store(stress_out, block_index(f - SXX, y) + t, value - load(y, t) if f == SZZ else value)

    stresses(grid, OUTER, SPAN, speed, field, field(LAME), field(SHEAR), put)
    for f in range(SXX, SYZ + 1):
        for y in INNER:
            for t in range(SPAN):
                put(f, y, t, tile(stress_in, block_index(f - SXX, y) + t))
    stress = block_reader(stress_out, SXX)
    speeds(
        grid, [inside(stress(f)) for f in range(SXX, SYZ + 1)], speed, field(BUOY), OPEN,
        lambda c, y, t, value: store(partial_out, edge_index(c, y) + t, value),
    )
    moving = lambda f, k: tile(flats[k], f) if f >= DEPTH else tile(ocean, 3 * k + f)
    partial_level(grid, moving, lambda k, value: store(level_out, k, value))

    def rows_of(f):
        return (lambda y, t: tile(partial_out, edge_index(f, y) + t)) if f < 3 else stress(f)

    def line_out(which, k, y):
        if which is None:
            return row(level_out, k * ROWS + y)
        return line(which, k, y) if which >= DEPTH else row(ocean, (3 * k + which) * ROWS + y)

    send(LATER, odd, rows_of, line_out, even_way, odd_way)


def copy_rows(ref, index, hbm, f, y, sem):
    return pltpu.make_async_copy(ref.at[index * SUB : (index + TILES) * SUB, :], hbm.at[f, :, y, :], sem)


BY_ROWS = (SXX, SYY)
BY_FIELD = (SZZ, SXY, SXZ, SYZ)


def middle_rest_kernel(flags, before, after, main, windows, around, speed_in, stress_in, speed_out, stress_out, wave_hbm, sem):
    grid = Grid(flags[2], before, after)
    field = fields_of(main, windows)
    stress = block_reader(stress_in, SXX)
    speeds(
        grid, [inside(stress(f)) for f in range(SXX, SYZ + 1)], speed_reader(around, speed_in), field(BUOY), CLOSED,
        lambda c, y, t, value: store(speed_out, block_index(c, y) + t, value),
    )
    sent = [copy_rows(speed_out, block_index(c, y), wave_hbm, c, y, sem.at[i]) for i, (c, y) in enumerate(CLOSED)]
    for one in sent:
        one.start()
    stresses(
        grid, INNER, TILES, block_reader(speed_out, VX), stress,
        field(LAME), field(SHEAR),
        lambda f, y, t, value: store(stress_out, block_index(f - SXX, y) + t, value),
    )
    for f in BY_ROWS:
        for y in INNER:
            sent.append(copy_rows(stress_out, block_index(f - SXX, y), wave_hbm, f, y, sem.at[len(sent)]))
            sent[-1].start()
    for one in sent:
        one.wait()


def last_kernel(
    flags, before, after, main, windows, flat, flat_windows, stress_in, ocean_in, partial, level, speed_in, inner_in,
    early_even, early_odd, even_in, odd_in, wave_in,
    wave_hbm, ocean_out,
    sums, pressure, around, turned, wave, sem,
):
    grid = Grid(flags[2], before, after)
    odd = (flags[1] & 1) == 1
    lo, hi = received(LATER, odd, even_in, odd_in)
    lo_buoy, hi_buoy = early(odd, early_even, early_odd, (lo, hi))
    field = fields_of(main, windows)
    stress = block_reader(stress_in, SXX)
    finish(
        grid, TILES, lambda c, y, t: tile(partial, edge_index(c, y) + t), stress, field(BUOY),
        lo, hi, lo_buoy, hi_buoy, around,
    )
    speed = speed_reader(around, speed_in)
    sent = []

    def copy(source, target):
        sent.append(pltpu.make_async_copy(source, target, sem.at[len(sent)]))
        sent[-1].start()

    for c, y in OPEN:
        sent.append(copy_rows(around, (c * AROUND + y + 2) * SPAN, wave_hbm, c, y, sem.at[len(sent)]))
        sent[-1].start()
    flats = (flat, flat_windows)
    fixed = lambda f, k: tile(flats[k], f)

    def line(f, k, y):
        return row(flats[k], f * ROWS + y) if f >= DEPTH else row(ocean_in, (3 * k + f) * ROWS + y)

    def new(f, k, value):
        if k == 0:
            store(ocean_out, f, value)

    levels = sea(
        grid, speed, lambda k: tile(level, k), lambda f, k: tile(ocean_in, 3 * k + f), fixed, line, lo, hi, sums, new, True
    )
    load = press(grid, levels, fixed, line, pressure)

    size = TILES * SUB * ROWS

    def put(f, y, t, value):
        if f in BY_ROWS:
            turned[f - SXX, y, t * SUB : (t + 1) * SUB, :] = value
            return
        if f == SZZ:
            value = value - load(y, t)
        wave[pl.ds(BY_FIELD.index(f) * size + t * SUB * ROWS + y, SUB, stride=ROWS), :] = value

    def done(y):
        copy(turned.at[:, y], wave_hbm.at[SXX : SYY + 1, :, y, :])

    stresses(grid, OUTER, TILES, speed, stress, field(LAME), field(SHEAR), put, done)
    for f in BY_FIELD:
        for y in INNER:
            for t in range(TILES):
                put(f, y, t, tile(inner_in, block_index(f - SXX, y) + t))
    copy(wave, wave_hbm.at[SZZ : SYZ + 1].reshape(len(BY_FIELD) * size, LANES))
    for one in sent:
        one.wait()


IN_VMEM = pl.BlockSpec(memory_space=pltpu.VMEM)
IN_SMEM = pl.BlockSpec(memory_space=pltpu.SMEM)
IN_HBM = pl.BlockSpec(memory_space=pltpu.HBM)


def call(kernel, tiles, scratch, *arguments, flags=None, place=IN_VMEM, out_places=None, work=1, aliases={}):
    specs = place if isinstance(place, list) else [place] * len(arguments)
    if flags is not None:
        arguments, specs = (flags, *arguments), [IN_SMEM] + specs
    moved = sum(x.size for x in arguments) + sum(n for n in tiles if isinstance(n, int)) * SUB * LANES
    return pl.pallas_call(
        kernel,
        out_shape=[n if hasattr(n, "dtype") else jax.ShapeDtypeStruct((n * SUB, LANES), jnp.float32) for n in tiles],
        in_specs=specs,
        out_specs=out_places or [IN_VMEM] * len(tiles),
        scratch_shapes=scratch,
        input_output_aliases=aliases,
        cost_estimate=pl.CostEstimate(flops=work * 1000000, bytes_accessed=4 * moved, transcendentals=0),
        compiler_params=pltpu.CompilerParams(vmem_limit_bytes=24 * 1024 * 1024),
    )(*arguments)


def planes(n):
    return pltpu.VMEM((n * SUB, LANES), jnp.float32)


def swap(x, axis, start):
    pairs = [(i, i + 1) for i in range(start, lax.axis_size(axis) - 1, 2)]
    return lax.ppermute(x, axis, pairs + [(j, i) for i, j in pairs])


def local(*arguments):
    ocean_state = arguments[4]
    inputs = [pltpu.with_memory_space_constraint(x, pltpu.HBM) for x in arguments]
    flags = jnp.stack([lax.axis_index("gx"), lax.axis_index("gy"), 0])
    matrix = jax.ShapeDtypeStruct((2 * LANES, SPAN * LANES), jnp.bfloat16)
    cells4 = jax.ShapeDtypeStruct((FIELDS, ROWS, TILES * SUB, LANES), jnp.float32)

    edge = FIELDS * ROWS // 4 + 2
    before, after, main, flat, own, own_flat, even_way, odd_way, early_even, early_odd = call(
        edges_kernel, [matrix, matrix, cells4, 6, FIELDS * ROWS, 6, edge, edge, 2 * TILES, 2 * TILES],
        [planes(FIELDS * ROWS), planes(6)] + [pltpu.VMEM(x.shape, x.dtype) for x in inputs[4:]]
        + [pltpu.SemaphoreType.DMA((4 + 5 * ROWS,))],
        *inputs, flags=flags, place=IN_HBM,
    )
    x_in = swap(even_way, "gx", 0), swap(odd_way, "gx", 1)
    early_in = swap(early_even, "gy", 0), swap(early_odd, "gy", 1)
    main = main.reshape(-1, LANES)
    first, later = [message_tiles(kind) for kind in (FIRST, LATER)]
    edges, block = len(OPEN) * SPAN, ROWS * SPAN
    windows, flat_windows, partial, level, even_way, odd_way = call(
        start_kernel, [FIELDS * ROWS, 6, edges, 2, first, first], [],
        before, after, main, flat, own, own_flat, *x_in, *early_in[::-1], flags=flags,
    )
    y_in = swap(even_way, "gy", 0), swap(odd_way, "gy", 1)
    speed, inner = call(start_rest_kernel, [3 * block, 6 * block], [], before, after, main, windows, flags=flags, work=4)
    around, stress, ocean, partial, level, even_way, odd_way = call(
        middle_kernel, [3 * AROUND * SPAN, 6 * block, 6, edges, 2, later, later], [planes(4), planes(2)],
        before, after, main, windows, flat, flat_windows, partial, level, speed, inner, *early_in, *y_in[::-1], flags=flags,
    )
    y_in = swap(even_way, "gy", 0), swap(odd_way, "gy", 1)
    wave = jax.ShapeDtypeStruct(arguments[0].shape, jnp.float32)
    speed, inner, wave_part = call(
        middle_rest_kernel, [3 * block, 6 * block, wave],
        [pltpu.SemaphoreType.DMA((len(CLOSED) + len(BY_ROWS) * len(INNER),))],
        before, after, main, windows, around, speed, stress, flags=flags, out_places=[IN_VMEM, IN_VMEM, IN_HBM], work=4,
    )
    operands = (
        before, after, main, windows, flat, flat_windows, stress, ocean, partial, level, speed, inner, *early_in, *y_in, wave_part
    )
    wave_out, ocean_out = call(
        last_kernel, [wave, 3],
        [
            planes(4), planes(2), planes(3 * AROUND * SPAN),
            pltpu.VMEM((len(BY_ROWS), *cells4.shape[1:]), jnp.float32), planes(len(BY_FIELD) * ROWS * TILES),
            pltpu.SemaphoreType.DMA((len(OPEN) + len(OUTER) + 1,)),
        ],
        *operands, flags=flags, place=[IN_VMEM] * (len(operands) - 1) + [IN_HBM], out_places=[IN_HBM, IN_VMEM],
        aliases={len(operands): 0},
    )
    return wave_out, ocean_out.reshape(ocean_state.shape)


def solution(mesh):
    in_specs = (
        P(None, None, "gy", "gx"),
        P(None, "gy", "gx"),
        P(None, "gy", "gx"),
        P(None, "gy", "gx"),
        P(None, "gy", "gx"),
        P("gy", "gx"),
        P("gy", "gx"),
        P("gy", "gx"),
    )
    out_specs = (P(None, None, "gy", "gx"), P(None, "gy", "gx"))
    return jax.shard_map(local, mesh=mesh, in_specs=in_specs, out_specs=out_specs, check_vma=False)
```
